32 devices in a mesh: grp: 2 (over core), dp: 16 (over z, y, x).
Axes of the slice: x: 2, y: 2, z: 4, core: 2. Of those that a mesh axis runs over, the one named last changes fastest.
Arguments:
- pixels: bfloat16 [2, 2, 16, 8, 196, 768], P(None, None, 'dp', 'grp'), may hold values from -6 to 6
- counts: int32 [2, 2, 16], P(None, None, 'dp'), may hold values from 4 to 8, as said below
- step_mask: int32 [2, 2, 16, 8], P(None, None, 'dp'), may hold values from 0 to 1, as said below
- owner: int32 [2, 16], P(None, 'dp'), may hold values from 0 to 1
- params: bfloat16 [4123136], P(('grp', 'dp'))
- cotangent: bfloat16 [2, 2, 16, 8, 16, 512], P(None, 'grp', 'dp'), may hold values from -6 to 6
Outputs:
- processed: bfloat16 [2, 2, 16, 8, 16, 512], P(None, 'grp', 'dp')
- pixel_grad: bfloat16 [2, 2, 16, 8, 196, 768], P(None, None, 'dp', 'grp')
- param_grad: float32 [4123136], P(('grp', 'dp'))
The draws below stay inside these ranges and needn't reach their ends.
Inputs may be any that keep to these rules, and one draw needn't show every extreme that they name: `counts`: some clip has 8 frames in every draw. `step_mask`: in each half of a clip's 8 slots (the first 4 and the last 4) 1 to 2 slots hold 1; the clip with 8 frames has exactly 2 in both halves.
All inputs are finite; a program needn't handle non-finite values.
Results may differ from the reference program's by a relative error of at most 0.015.
Values may be sent and summed in bfloat16 or wider, within the bound.
A program may use at most 192 MiB of HBM per device.

```python
import math
import jax
import jax.numpy as jnp
from jax import lax

D = 512
HEADS = 8
FFN = 2048
PIN = 768
P_SIZE = 196
MEM = 96
READ = 16
HID = 512
STEPS = 8
KEEP = 2
MICRO = 2
GROUPS = 2
CLIPS_H = 16
PADDED = 4123136


def chosen_clip(key):
    clip_total = MICRO * GROUPS * CLIPS_H
    return jax.random.randint(jax.random.fold_in(key, 97), (), 0, clip_total)


def draw_counts(key, part):
    chosen = chosen_clip(key)
    key = jax.random.fold_in(key, 5)
    clip_total = MICRO * GROUPS * CLIPS_H
    lengths_drawn = jax.random.randint(key, (clip_total,), STEPS // 2, STEPS + 1)
    lengths_drawn = lengths_drawn.at[chosen].set(STEPS)
    return lengths_drawn.reshape(MICRO, GROUPS, CLIPS_H).astype(jnp.int32)


def draw_step_mask(key, part):
    chosen = chosen_clip(key)
    key = jax.random.fold_in(key, 7)
    key_number, key_order = jax.random.split(key)
    clip_total = MICRO * GROUPS * CLIPS_H
    half_steps = STEPS // 2
    numbers = jax.random.randint(key_number, (clip_total, 2), 1, KEEP + 1)
    clip_ids = jnp.arange(clip_total, dtype=jnp.int32)[:, None]
    numbers = jnp.where(clip_ids == chosen, KEEP, numbers)
    order_keys = jax.random.split(key_order, clip_total * 2)
    orders = jax.vmap(lambda k: jax.random.permutation(k, half_steps))(order_keys).reshape(clip_total, 2, half_steps)
    mask_values = (orders < numbers[:, :, None]).astype(jnp.int32)
    return mask_values.reshape(MICRO, GROUPS, CLIPS_H, STEPS)


def draw_params(key, part):
    key = jax.random.fold_in(key, 11)
    layout = [(PIN * D, PIN ** (-0.5), 0.0), (D, 0.5, 0.0), (D, 0.2, 1.0), (D * HID, D ** (-0.5), 0.0), (HID * READ, 2.0 * HID ** (-0.5), 0.0), (D, 0.2, 1.0), (3 * D * D, D ** (-0.5), 0.0), (D * D, 2.0 * D ** (-0.5), 0.0), (D, 0.2, 1.0), (D * FFN, D ** (-0.5), 0.0), (FFN * D, FFN ** (-0.5), 0.0), (D, 0.2, 1.0), (D * HID, D ** (-0.5), 0.0), (HID * MEM, 2.0 * HID ** (-0.5), 0.0)]
    used_length = sum((entry[0] for entry in layout))
    spreads = jnp.concatenate([jnp.full((length,), spread, jnp.float32) for length, spread, offset in layout] + [jnp.zeros((PADDED - used_length,), jnp.float32)])
    offsets = jnp.concatenate([jnp.full((length,), offset, jnp.float32) for length, spread, offset in layout] + [jnp.zeros((PADDED - used_length,), jnp.float32)])
    noise = jnp.clip(jax.random.normal(key, (PADDED,), jnp.float32), -3.0, 3.0)
    return (offsets + spreads * noise).astype(jnp.bfloat16)


def touch_ends(entries, stream_key, smallest, largest):
    longest = entries.shape.index(max(entries.shape))
    spots = []
    for shift in (0, 1):
        where = [jax.random.randint(jax.random.fold_in(stream_key, axis), (), 0, length) for axis, length in enumerate(entries.shape)]
        where[longest] = (where[longest] + shift) % entries.shape[longest]
        spots.append(tuple(where))
    return entries.at[spots[0]].set(smallest).at[spots[1]].set(largest)


def block_levels(own_key, dims, cuts, low, high):
    loudness = 1.0
    for axis_at, shards_of in cuts:
        draws = jax.random.uniform(jax.random.fold_in(jax.random.fold_in(own_key, 6), axis_at), (shards_of,), jnp.float32, low / len(cuts), high / len(cuts))
        loudness = loudness * jnp.repeat(jnp.exp(draws), dims[axis_at] // shards_of).reshape((-1,) + (1,) * (len(dims) - 1 - axis_at))
    return loudness


def scatter_about(own_key, dims, scale, bound, cuts=(), kind=jnp.bfloat16):
    level = block_levels(own_key, dims, cuts, -0.22, 0.18) if cuts else 1.0
    values = jax.random.normal(own_key, dims, jnp.float32) * scale * level
    return jnp.minimum(jnp.maximum(values, -bound), bound).astype(kind)


def setup_inputs(seed: int = 0) -> dict:
    key_of = jax.random.split(jax.random.key(seed), 7)
    pixels = scatter_about(key_of[0], (MICRO, GROUPS, CLIPS_H, STEPS, P_SIZE, PIN), 1.0, 6.0, ((2, 16), (3, 2)))
    counts = draw_counts(jax.random.fold_in(key_of[6], 71), 0)
    step_mask = draw_step_mask(jax.random.fold_in(key_of[6], 71), 0)
    owner = touch_ends(jax.random.randint(key_of[3], (MICRO, CLIPS_H), 0, 2), jax.random.fold_in(key_of[3], 1), 0, 1).astype(jnp.int32)
    params = draw_params(jax.random.fold_in(key_of[6], 71), 0)
    cotangent = scatter_about(key_of[5], (MICRO, GROUPS, CLIPS_H, STEPS, READ, D), 1.0, 6.0, ((1, 2), (2, 16)))
    return dict(pixels=pixels, counts=counts, step_mask=step_mask, owner=owner, params=params, cotangent=cotangent)


@jax.custom_vjp
def low(v):
    return lax.optimization_barrier(v.astype(jnp.bfloat16)).astype(jnp.float32)

@jax.custom_vjp
def low_back(v):
    return v

def low_keep(v):
    return (low(v), None)

def low_pass(kept, grad):
    return (grad,)

def back_keep(v):
    return (v, None)

def back_low(kept, grad):
    return (low(grad),)
low.defvjp(low_keep, low_pass)
low_back.defvjp(back_keep, back_low)

def segments():
    return [('patch_weight', (PIN, D)), ('patch_bias', (D,)), ('read_gain', (D,)), ('read_hidden', (D, HID)), ('read_scores', (HID, READ)), ('attn_gain', (D,)), ('qkv_weight', (D, 3 * D)), ('attn_out', (D, D)), ('ffn_gain', (D,)), ('ffn_in', (D, FFN)), ('ffn_out', (FFN, D)), ('write_gain', (D,)), ('write_hidden', (D, HID)), ('write_scores', (HID, MEM))]

def unpack(flat_params):
    pieces = {}
    offset = 0
    for segment_name, extent in segments():
        length = math.prod(extent)
        pieces[segment_name] = flat_params[offset:offset + length].reshape(extent)
        offset = offset + length
    return pieces

def matmul(operand_a, operand_b):
    return low_back(jnp.matmul(operand_a, operand_b, precision=lax.Precision.HIGHEST))

def layer_norm(values, scale_vec):
    average = lax.optimization_barrier(jnp.mean(values, -1, keepdims=True))
    centered = values - average
    variance = lax.optimization_barrier(jnp.mean(centered * centered, -1, keepdims=True))
    return centered * lax.rsqrt(variance + 1e-06) * scale_vec

def summarize(tokens_in, scale_vec, hidden_weight, score_weight):
    normed = low(layer_norm(tokens_in, scale_vec))
    hidden = low(jax.nn.gelu(matmul(normed, hidden_weight), approximate=False))
    scores = matmul(hidden, score_weight)
    weights = low(jax.nn.softmax(scores, axis=1))
    return matmul(jnp.swapaxes(weights, 1, 2), tokens_in)

def process(summary, pieces):
    batch_size = summary.shape[0]
    head_size = D // HEADS
    normed = low(layer_norm(summary, pieces['attn_gain']))
    united_qkv = low(matmul(normed, pieces['qkv_weight']))
    split_heads = united_qkv.reshape(batch_size, READ, 3, HEADS, head_size).transpose(2, 0, 3, 1, 4)
    scores = matmul(split_heads[0], jnp.swapaxes(split_heads[1], 2, 3)) * (1.0 / math.sqrt(head_size))
    probabilities = low(jax.nn.softmax(scores, axis=-1))
    attended = matmul(probabilities, split_heads[2])
    joined = low(attended.transpose(0, 2, 1, 3).reshape(batch_size, READ, D))
    middle = summary + matmul(joined, pieces['attn_out'])
    normed_two = low(layer_norm(middle, pieces['ffn_gain']))
    inner_act = low(jax.nn.gelu(matmul(normed_two, pieces['ffn_in']), approximate=False))
    return middle + matmul(inner_act, pieces['ffn_out'])

def advance(pieces, memory, frame_tokens, valid_flag):
    memory_low = low(memory)
    summary = summarize(jnp.concatenate([memory_low, frame_tokens], 1), pieces['read_gain'], pieces['read_hidden'], pieces['read_scores'])
    tokens_out = low(process(summary, pieces))
    written = summarize(jnp.concatenate([memory_low, tokens_out, frame_tokens], 1), pieces['write_gain'], pieces['write_hidden'], pieces['write_scores'])
    keep_mask = valid_flag[:, None, None]
    return (jnp.where(keep_mask > 0.5, written, memory), tokens_out * keep_mask)

def run_core(pieces, frames, valid_steps):
    frames = low_back(frames)
    initial = jnp.zeros((frames.shape[0], MEM, D), jnp.float32)

    def step_fn(memory, inputs):
        return advance(pieces, memory, inputs[0], inputs[1])
    final_memory, outputs = lax.scan(jax.checkpoint(step_fn), initial, (jnp.swapaxes(frames, 0, 1), jnp.swapaxes(valid_steps, 0, 1)))
    return jnp.swapaxes(outputs, 0, 1)

def clip_forward(flat_params, pixel_block, valid_steps):
    pieces = unpack(flat_params)
    frames = low(matmul(pixel_block, pieces['patch_weight']) + pieces['patch_bias'])
    return run_core(pieces, frames, valid_steps)

def reference(pixels, counts, step_mask, owner, params, cotangent):
    flat_params = params.astype(jnp.float32)
    clip_total = MICRO * GROUPS * CLIPS_H
    blocks = clip_total // 2
    positions = jnp.arange(STEPS, dtype=jnp.int32)
    valid_all = ((positions < counts[..., None]) & (step_mask == 1)).astype(jnp.float32)
    flipped = (owner == 1)[:, None, :, None, None, None]
    cot_groups = jnp.where(flipped, cotangent[:, ::-1], cotangent)
    pixel_blocks = pixels.reshape(blocks, 2, STEPS, P_SIZE, PIN)
    valid_blocks = valid_all.reshape(blocks, 2, STEPS)
    cot_blocks = cot_groups.reshape(blocks, 2, STEPS, READ, D)

    def block_fn(running_total, inputs):
        pixel_block, valid_block, cot_block = inputs
        outputs, pullback = jax.vjp(lambda w, p: clip_forward(w, p, valid_block), flat_params, pixel_block.astype(jnp.float32))
        grad_params, grad_pixels = pullback(cot_block.astype(jnp.float32))
        return (running_total + grad_params, (outputs.astype(jnp.bfloat16), grad_pixels.astype(jnp.bfloat16)))
    total_grad, (processed, pixel_grad) = lax.scan(block_fn, jnp.zeros_like(flat_params), (pixel_blocks, valid_blocks, cot_blocks))
    processed = processed.reshape(MICRO, GROUPS, CLIPS_H, STEPS, READ, D)
    processed = jnp.where(flipped, processed[:, ::-1], processed)
    return (processed, pixel_grad.reshape(MICRO, GROUPS, CLIPS_H, STEPS, P_SIZE, PIN), total_grad)
```

```python
import functools
import math

import jax
import jax.numpy as jnp
from jax import lax
from jax.experimental import pallas as pl
from jax.experimental.pallas import tpu as pltpu
from jax.sharding import PartitionSpec as P

MESH = pl.DeviceIdType.MESH
F32 = jnp.float32
BF16 = jnp.bfloat16

D = 512
HEADS = 8
HEAD = D // HEADS
FFN = 2048
PIN = 768
P_SIZE = 196
ROWS = 208
MEM = 96
READ = 16
NCOL = MEM + READ
STEPS = 8
BLOCK = 16
EPS = 1e-6
RING = 4
HUGE = 1e30

ROW_PATCH = 0
ROW_BIAS = 768
ROW_RGAIN = 769
ROW_RHID = 770
ROW_RSCORE = 1282
ROW_AGAIN = 1298
ROW_QKV = 1299
ROW_AOUT = 2835
ROW_FGAIN = 3347
ROW_FIN = 3348
ROW_FOUT = 5396
ROW_WGAIN = 7444
ROW_WHID = 7445
ROW_WSCORE = 7957
ROW_END = 8053

VMEM_LIMIT = 60 * 2**20


def dot(a, b, ca=1, cb=0):
    return lax.dot_general(a, b, (((ca,), (cb,)), ((), ())), preferred_element_type=F32)


def window_rows(length):
    return (length + BLOCK * D - 2) // (BLOCK * D) * BLOCK + BLOCK


def plan(chips):
    bits = chips.bit_length() - 1
    low = [b for b in (0, 1) if b < bits]
    high = list(range(low[-1] + 1 if low else 0, bits))
    return high + low, high + low[::-1]


def partners(chips, core, me):
    orders = plan(chips)
    steps = []
    for one, two in zip(*orders):
        a = (1 - 2 * ((me // (1 << one)) % 2)) * (1 << one)
        b = (1 - 2 * ((me // (1 << two)) % 2)) * (1 << two)
        steps.append(a + core * (b - a))
    return steps


def shifted(me, steps, r):
    at = me
    for k, step in enumerate(steps):
        if (r >> k) & 1:
            at = at + step
    return at


def first_block(index, length):
    return (index * length) // (BLOCK * D)


def gather_order(chips):
    return sorted(range(1, chips), key=lambda r: (bin(r).count("1"), r))


def greet(core, me, steps):
    barrier = pltpu.get_barrier_semaphore()
    places = [(core, me + step) for step in steps] + [(1 - core, me)]
    for place in places:
        pl.semaphore_signal(barrier, inc=1, device_id=place, device_id_type=MESH)
    pl.semaphore_wait(barrier, len(places))


def gather_kernel(chips, win, pix, out, pixout, send, recv, sibsend, sibrecv, local, pixsem):
    core = lax.axis_index("grp")
    me = lax.axis_index("dp")
    steps = partners(chips, core, me)
    bits = len(steps)
    sibling = (1 - core, me)
    greet(core, me, steps)

    def remote(src, dst, s, r, place):
        return pltpu.make_async_remote_copy(
            src_ref=src, dst_ref=dst, send_sem=s, recv_sem=r, device_id=place, device_id_type=MESH
        )

    mine = core * chips + me
    started = []
    for k in range(bits - 1, -1, -1):
        copy = remote(win, out.at[mine], send.at[k, 0], recv.at[1 << k], (core, me + steps[k]))
        copy.start()
        started.append(copy)
    keep = pltpu.make_async_copy(win, out.at[mine], local.at[0])
    keep.start()
    keep_pix = pltpu.make_async_copy(pix.at[0], pixout.at[core], local.at[1])
    keep_pix.start()
    swap_pix = remote(pix.at[1], pixout.at[core], pixsem.at[0], pixsem.at[1], sibling)
    swap_pix.start()
    side = [remote(win, out.at[mine], sibsend.at[0], sibrecv.at[0], sibling)]
    side[0].start()
    for r in gather_order(chips):
        at = out.at[core * chips + shifted(me, steps, r)]
        top = r.bit_length() - 1
        remote(at, at, send.at[0, 0], recv.at[r], sibling).wait_recv()
        for k in range(bits - 1, top, -1):
            copy = remote(at, at, send.at[k, r], recv.at[r | (1 << k)], (core, me + steps[k]))
            copy.start()
            started.append(copy)
        copy = remote(at, at, sibsend.at[r], sibrecv.at[r], sibling)
        copy.start()
        side.append(copy)
    for copy in started:
        copy.wait_send()
    for copy in side:
        copy.wait()
    keep.wait()
    keep_pix.wait()
    swap_pix.wait()


def gather(win, pix, chips):
    rows = win.shape[0]
    bits = chips.bit_length() - 1
    return pl.pallas_call(
        functools.partial(gather_kernel, chips),
        out_shape=(
            jax.ShapeDtypeStruct((2 * chips, rows, D), BF16),
            jax.ShapeDtypeStruct((2, 4, ROWS, PIN), BF16),
        ),
        in_specs=[pl.BlockSpec(memory_space=pl.ANY)] * 2,
        out_specs=[pl.BlockSpec(memory_space=pl.ANY)] * 2,
        scratch_shapes=[
            pltpu.SemaphoreType.DMA((bits, chips)),
            pltpu.SemaphoreType.DMA((chips,)),
            pltpu.SemaphoreType.DMA((chips,)),
            pltpu.SemaphoreType.DMA((chips,)),
            pltpu.SemaphoreType.DMA((2,)),
            pltpu.SemaphoreType.DMA((2,)),
        ],
        compiler_params=pltpu.CompilerParams(collective_id=0, has_side_effects=True),
        name="gather",
    )(win, pix)


def reduce_kernel(
    chips, length, grads, pg, out, pgout, own, side, held, send, recv, sibsend, sibrecv, local, pixsem
):
    core = lax.axis_index("grp")
    me = lax.axis_index("dp")
    steps = partners(chips, core, me)
    other_steps = partners(chips, 1 - core, me)
    bits = len(steps)
    rows = own.shape[1]
    sibling = (1 - core, me)

    def remote(src, dst, s, r, place):
        return pltpu.make_async_remote_copy(
            src_ref=src, dst_ref=dst, send_sem=s, recv_sem=r, device_id=place, device_id_type=MESH
        )

    def window(index):
        start = pl.multiple_of(first_block(index, length) * BLOCK, BLOCK)
        return grads.at[pl.ds(start, rows)]

    def mine(r):
        src = window(core * chips + shifted(me, steps, r))
        return pltpu.make_async_copy(src, own.at[r], local.at[r])

    for r in range(chips - 1, -1, -1):
        mine(r).start()
    greet(core, me, steps)
    swaps = []
    for r in range(chips - 1, -1, -1):
        src = window((1 - core) * chips + shifted(me, other_steps, r))
        copy = remote(src, side.at[r], sibsend.at[r], sibrecv.at[r], sibling)
        copy.start()
        swaps.append(copy)
    swap_pix = remote(pg.at[1 - core], pgout.at[1], pixsem.at[0], pixsem.at[1], sibling)
    swap_pix.start()
    keep_pix = pltpu.make_async_copy(pg.at[core], pgout.at[0], local.at[chips])
    keep_pix.start()

    started = []
    for r in range(chips - 1, -1, -1):
        mine(r).wait()
        remote(side.at[r], side.at[r], sibsend.at[r], sibrecv.at[r], sibling).wait_recv()
        top = r.bit_length() - 1
        slots = []
        for k in range(bits - 1, top, -1):
            slot = held.at[(1 << k) - 1 + r]
            remote(slot, slot, send.at[r], recv.at[(1 << k) - 1 + r], sibling).wait_recv()
            slots.append((1 << k) - 1 + r)

        def add(i, carry, r=r, slots=tuple(slots)):
            at = pl.ds(pl.multiple_of(i * BLOCK, BLOCK), BLOCK)
            total = own[r, at, :].astype(F32) + side[r, at, :].astype(F32)
            for slot in slots:
                total = total + held[slot, at, :].astype(F32)
            if r == 0:
                out[at, :] = total
            else:
                own[r, at, :] = total.astype(BF16)
            return carry

        lax.fori_loop(0, rows // BLOCK, add, 0)
        if r > 0:
            at = r - (1 << top)
            slot = (1 << top) - 1 + at
            copy = remote(
                own.at[r], held.at[slot], send.at[r], recv.at[slot], (core, me + steps[top])
            )
            copy.start()
            started.append(copy)
    for copy in started:
        copy.wait_send()
    for copy in swaps:
        copy.wait_send()
    swap_pix.wait()
    keep_pix.wait()


def reduce(grads, pg, chips, length):
    rows = window_rows(length)
    return pl.pallas_call(
        functools.partial(reduce_kernel, chips, length),
        out_shape=(
            jax.ShapeDtypeStruct((rows, D), F32),
            jax.ShapeDtypeStruct((2, 4, ROWS, PIN), BF16),
        ),
        in_specs=[pl.BlockSpec(memory_space=pl.ANY)] * 2,
        out_specs=[pl.BlockSpec(memory_space=pltpu.VMEM), pl.BlockSpec(memory_space=pl.ANY)],
        scratch_shapes=[
            pltpu.VMEM((chips, rows, D), BF16),
            pltpu.VMEM((chips, rows, D), BF16),
            pltpu.VMEM((chips - 1, rows, D), BF16),
            pltpu.SemaphoreType.DMA((chips,)),
            pltpu.SemaphoreType.DMA((chips,)),
            pltpu.SemaphoreType.DMA((chips,)),
            pltpu.SemaphoreType.DMA((chips,)),
            pltpu.SemaphoreType.DMA((chips + 1,)),
            pltpu.SemaphoreType.DMA((2,)),
        ],
        compiler_params=pltpu.CompilerParams(
            collective_id=1, has_side_effects=True, vmem_limit_bytes=VMEM_LIMIT
        ),
        name="reduce",
    )(grads, pg)


def pick_kernel(where_ref, pix_ref, out_ref):
    out_ref[0, 0, :P_SIZE] = pix_ref[0, 0, 0, 0]
    out_ref[0, 0, P_SIZE:] = jnp.zeros((ROWS - P_SIZE, PIN), BF16)


def pick(pixels, where):
    def source(e, where_ref):
        return ((e // 2) % 2, where_ref[0, e], 0, where_ref[1, e], 0, 0)

    return pl.pallas_call(
        pick_kernel,
        out_shape=jax.ShapeDtypeStruct((2, 4, ROWS, PIN), BF16),
        grid_spec=pltpu.PrefetchScalarGridSpec(
            num_scalar_prefetch=1,
            grid=(8,),
            in_specs=[pl.BlockSpec((1, 1, 1, 1, P_SIZE, PIN), source)],
            out_specs=pl.BlockSpec((1, 1, ROWS, PIN), lambda e, w: (e // 4, e % 4, 0, 0)),
        ),
        name="pick",
    )(where, pixels)


def place_kernel(where_ref, grad_ref, out_ref):
    e = pl.program_id(0)

    @pl.when(where_ref[1, e] == 1)
    def _():
        out_ref[0, 0, 0, 0] = grad_ref[0, :P_SIZE]

    @pl.when(where_ref[1, e] == 0)
    def _():
        out_ref[0, 0, 0, 0] = jnp.zeros((P_SIZE, PIN), BF16)


def place(grads, where, shape):
    return pl.pallas_call(
        place_kernel,
        out_shape=jax.ShapeDtypeStruct(shape, BF16),
        grid_spec=pltpu.PrefetchScalarGridSpec(
            num_scalar_prefetch=1,
            grid=(16,),
            in_specs=[pl.BlockSpec((1, ROWS, PIN), lambda e, w: (w[0, e], 0, 0))],
            out_specs=pl.BlockSpec(
                (1, 1, 1, 1, P_SIZE, PIN), lambda e, w: (e // 8, (e // 4) % 2, 0, e % 4, 0, 0)
            ),
        ),
        name="place",
    )(where, grads.reshape(8, ROWS, PIN))


def frame_index(clip, step):
    return (step // 2) * 4 + clip * 2 + step % 2


def norm(x):
    mean = jnp.mean(x, -1, keepdims=True)
    centered = x - mean
    r = lax.rsqrt(jnp.mean(centered * centered, -1, keepdims=True) + EPS)
    return centered * r, r


def norm_back(g, xh, r):
    return r * (g - jnp.mean(g, -1, keepdims=True) - xh * jnp.mean(g * xh, -1, keepdims=True))


def gelu(x):
    cdf = 0.5 + 0.5 * lax.erf(x * math.sqrt(0.5))
    slope = cdf + x * (jnp.exp(-0.5 * x * x) * (1.0 / math.sqrt(2.0 * math.pi)))
    return (x * cdf).astype(BF16), slope.astype(BF16)


def col_sum(x):
    return jnp.sum(x, 0, keepdims=True)


def row_sum(x):
    return jnp.sum(x, -1, keepdims=True)


def row_max(x):
    return jnp.max(x, -1, keepdims=True)


def iota(shape, dim):
    return lax.broadcasted_iota(jnp.int32, shape, dim)


def score_masks(width, part):
    group = 512 // math.gcd(512, width)
    lane = iota((D, D), 1) + 512 * part
    hidden = iota((D, D), 0)
    where = ((hidden % group) == (lane // width)).astype(BF16)
    lane = iota((width, D), 1) + 512 * part
    pick = ((lane % width) == iota((width, D), 0)).astype(BF16)
    rows = 512 // group
    spread = ((iota((D, rows), 0) // group) == iota((D, rows), 1)).astype(BF16)
    return where, pick, spread


def main_kernel(
    chips,
    length,
    slot_ref,
    flag_ref,
    shards,
    px,
    cot,
    done,
    pg,
    flat,
    planes,
    wp,
    wr,
    ww,
    wqkv,
    wo,
    win,
    wout,
    wsr,
    wsw,
    gains,
    xs,
    a_r,
    a_w,
    h_r,
    h_w,
    d_r,
    d_w,
    ps,
    rs,
    top,
    tot,
    scale,
    cs,
    dsc,
    mem,
    dmem,
    mls,
    mxh,
    mr,
    mnew,
    al_r,
    al_m,
    al_t,
    zs,
    xh1,
    r1,
    us,
    qs,
    prob,
    att,
    xh2,
    r2,
    u2,
    gs,
    dg,
    toks,
    xhk,
    rk,
    dqs,
    dys,
    dpre,
    dos,
    acc_r,
    acc_w,
    vecs,
    ring,
    ring_sem,
):
    rows = shards.shape[1]
    frames = 8

    def fetch(i):
        return pltpu.make_async_copy(shards.at[i], ring.at[i % RING], ring_sem.at[i % RING])

    def lay(i, carry):
        fetch(i).wait()
        start = pl.multiple_of(first_block(i, length) * BLOCK, BLOCK)
        flat[pl.ds(start, BLOCK), :] = flat[pl.ds(start, BLOCK), :] + ring[i % RING, :BLOCK, :]
        start = pl.multiple_of(start + BLOCK, BLOCK)
        flat[pl.ds(start, rows - BLOCK), :] = ring[i % RING, BLOCK:, :]

        @pl.when(i + RING < 2 * chips)
        def _():
            fetch(i + RING).start()

        return carry

    flat[:BLOCK, :] = jnp.zeros((BLOCK, D), BF16)
    for i in range(RING):
        fetch(i).start()
    lax.fori_loop(0, 2 * chips, lay, 0)

    wp[...] = flat[ROW_PATCH : ROW_PATCH + PIN, :]
    wr[...] = flat[ROW_RHID : ROW_RHID + D, :]
    wo[...] = flat[ROW_AOUT : ROW_AOUT + D, :]
    wout[...] = flat[ROW_FOUT : ROW_FOUT + FFN, :]
    ww[...] = flat[ROW_WHID : ROW_WHID + D, :]
    for k, row in enumerate((ROW_BIAS, ROW_RGAIN, ROW_AGAIN, ROW_FGAIN, ROW_WGAIN)):
        base = row // BLOCK * BLOCK
        gains[k : k + 1, :] = flat[base : base + BLOCK, :].astype(F32)[row - base : row - base + 1, :]
    for row, parts, dst in ((ROW_QKV, 3, wqkv), (ROW_FIN, 4, win)):
        for c in range(4):
            at = slice(c * 128, c * 128 + 128)
            planes[c, : parts * D, :] = flat[row : row + parts * D, at].astype(F32)
            for j in range(parts):
                dst[j, :, at] = planes[c, pl.ds(j, D, stride=parts), :].astype(BF16)
    where, chosen, spread = score_masks(READ, 0)
    wide = dot(spread, flat[ROW_RSCORE : ROW_RSCORE + READ, :]).astype(BF16) * where
    wsr[...] = dot(chosen, wide, 1, 1).astype(BF16)
    total = jnp.zeros((MEM, D), F32)
    for c in range(4):
        at = slice(c * 128, c * 128 + 128)
        planes[c, :MEM, :] = flat[ROW_WSCORE : ROW_WSCORE + MEM, at].astype(F32)
    for part in range(3):
        where, chosen, spread = score_masks(MEM, part)
        these = jnp.concatenate(
            [planes[c, pl.ds(part, 32, stride=3), :] for c in range(4)], -1
        ).astype(BF16)
        wide = dot(spread, these).astype(BF16) * where
        total = total + dot(chosen, wide, 1, 1)
    wsw[...] = total.astype(BF16)

    bias = gains[0:1, :]
    g_read = gains[1:2, :]
    g_attn = gains[2:3, :]
    g_ffn = gains[3:4, :]
    g_write = gains[4:5, :]

    lanes = iota((NCOL, ROWS), 1) < P_SIZE

    def frame_forward(f, carry):
        at = pl.ds(pl.multiple_of(f * ROWS, ROWS), ROWS)
        x = (dot(px[f], wp[...]) + bias).astype(BF16)
        xs[f] = x
        xh, r = norm(x.astype(F32))
        a_r[at, :] = (xh * g_read).astype(BF16)
        a_w[at, :] = (xh * g_write).astype(BF16)
        h, d = gelu(dot(a_r[at, :], wr[...]))
        h_r[at, :] = h
        d_r[at, :] = d
        s_read = dot(wsr[...], h, 1, 1)
        h, d = gelu(dot(a_w[at, :], ww[...]))
        h_w[at, :] = h
        d_w[at, :] = d
        s_write = dot(wsw[...], h, 1, 1)
        scores = jnp.where(lanes, jnp.concatenate([s_write, s_read], 0), -HUGE)
        best = row_max(scores)
        p = jnp.exp(scores - best)
        pb = p.astype(BF16)
        ps[f] = pb
        top[f] = best
        tot[f] = row_sum(p)
        rs[f] = dot(pb, x)
        return carry

    lax.fori_loop(0, frames, frame_forward, 0)

    done[...] = jnp.zeros(done.shape, BF16)
    mem[...] = jnp.zeros(mem.shape, F32)
    head_of = [(iota((1, D), 1) // HEAD == h) for h in range(HEADS)]
    same_clip = ((iota((HEADS * 32, 32), 0) // READ) % 2) == (iota((HEADS * 32, 32), 1) // READ)
    zero = jnp.zeros((), F32)

    def by_head(x):
        return jnp.concatenate([jnp.where(m, x, jnp.zeros_like(x)) for m in head_of], 0)

    def from_heads(x):
        total = jnp.where(head_of[0], x[:32], zero)
        for h in range(1, HEADS):
            total = total + jnp.where(head_of[h], x[32 * h : 32 * h + 32], zero)
        return total

    base_r = frames * ROWS
    base_w = frames * ROWS
    base_k = base_w + 2 * 192

    def step_forward(t):
        live = t > 0
        last = t == 3
        if live:
            ml = mem[...].astype(BF16)
            mls[t] = ml
            xh, r = norm(ml.astype(F32))
            mxh[t] = xh
            mr[t] = r
            at = slice(base_r + (t - 1) * 192, base_r + t * 192)
            a = (xh * g_read).astype(BF16)
            a_r[at, :] = a
            h, d = gelu(dot(a, wr[...]))
            h_r[at, :] = h
            d_r[at, :] = d
            if not last:
                a = (xh * g_write).astype(BF16)
                a_w[at, :] = a
                hw, d = gelu(dot(a, ww[...]))
                h_w[at, :] = hw
                d_w[at, :] = d
        z_parts = []
        for b in range(2):
            f = frame_index(b, t)
            m_f = top[f, MEM:, :]
            if live:
                s = dot(wsr[...], h[96 * b : 96 * b + 96], 1, 1)
                best = jnp.maximum(row_max(s), m_f)
                e = jnp.exp(s - best)
                part = row_sum(e)
            else:
                best = jnp.maximum(m_f, 0.0)
                part = MEM * jnp.exp(-best)
            w = jnp.exp(m_f - best)
            inv = 1.0 / (part + w * tot[f, MEM:, :])
            scale[f, MEM:, :] = w * inv
            z = (w * inv) * rs[f, MEM:, :]
            if live:
                al = (e * inv).astype(BF16)
                al_r[t, b] = al
                z = z + dot(al, ml[96 * b : 96 * b + 96])
            z_parts.append(z)
        z = jnp.concatenate(z_parts, 0)
        zs[t] = z
        at = slice(32 * t, 32 * t + 32)
        xh, r = norm(z)
        xh1[t] = xh
        r1[t] = r
        u = (xh * g_attn).astype(BF16)
        us[at, :] = u
        q = dot(u, wqkv[0]).astype(BF16)
        k = dot(u, wqkv[1]).astype(BF16)
        v = dot(u, wqkv[2]).astype(BF16)
        qs[0, t] = q
        qs[1, t] = k
        qs[2, t] = v
        s = jnp.where(same_clip, dot(by_head(q), k, 1, 1) * (1.0 / math.sqrt(HEAD)), -HUGE)
        e = jnp.exp(s - row_max(s))
        p = (e / row_sum(e)).astype(BF16)
        prob[t] = p
        joined = from_heads(dot(p, v)).astype(BF16)
        att[at, :] = joined
        y = z + dot(joined, wo[...])
        xh, r = norm(y)
        xh2[t] = xh
        r2[t] = r
        n = (xh * g_ffn).astype(BF16)
        u2[at, :] = n
        o = y
        for j in range(4):
            g, d = gelu(dot(n, win[j]))
            gs[at, D * j : D * j + D] = g
            dg[t, :, D * j : D * j + D] = d
            o = o + dot(g, wout[D * j : D * j + D, :])
        tok = o.astype(BF16)
        for b in range(2):

            @pl.when(flag_ref[b, t] == 1)
            def _(b=b):
                done[b, slot_ref[b, t]] = tok[16 * b : 16 * b + 16]

        if last:
            return
        toks[t] = tok
        xh, r = norm(tok.astype(F32))
        xhk[t] = xh
        rk[t] = r
        a = (xh * g_write).astype(BF16)
        at = slice(base_k + 32 * t, base_k + 32 * t + 32)
        a_w[at, :] = a
        hk, d = gelu(dot(a, ww[...]))
        h_w[at, :] = hk
        d_w[at, :] = d
        for b in range(2):
            f = frame_index(b, t)
            m_f = top[f, :MEM, :]
            s_tok = dot(wsw[...], hk[16 * b : 16 * b + 16], 1, 1)
            best = jnp.maximum(row_max(s_tok), m_f)
            if live:
                s = dot(wsw[...], hw[96 * b : 96 * b + 96], 1, 1)
                best = jnp.maximum(best, row_max(s))
                e = jnp.exp(s - best)
                part = row_sum(e)
            else:
                best = jnp.maximum(best, 0.0)
                part = MEM * jnp.exp(-best)
            e_tok = jnp.exp(s_tok - best)
            w = jnp.exp(m_f - best)
            inv = 1.0 / (part + row_sum(e_tok) + w * tot[f, :MEM, :])
            scale[f, :MEM, :] = w * inv
            al = (e_tok * inv).astype(BF16)
            al_t[t, b] = al
            new = (w * inv) * rs[f, :MEM, :] + dot(al, tok[16 * b : 16 * b + 16])
            if live:
                al = (e * inv).astype(BF16)
                al_m[t, b] = al
                new = new + dot(al, ml[96 * b : 96 * b + 96])
            mnew[t, b] = new
            old = mem[96 * b : 96 * b + 96, :]
            mem[96 * b : 96 * b + 96, :] = jnp.where(flag_ref[b, t] == 1, new, old)

    for t in range(4):
        step_forward(t)

    vecs[...] = jnp.zeros(vecs.shape, F32)
    acc_r[...] = jnp.zeros(acc_r.shape, F32)
    acc_w[...] = jnp.zeros(acc_w.shape, F32)
    dmem[...] = jnp.zeros(dmem.shape, F32)

    def add_vec(k, x):
        vecs[k : k + 1, :] = vecs[k : k + 1, :] + x

    def step_backward(t):
        live = t > 0
        last = t == 3
        gates = [(flag_ref[b, t] == 1).astype(F32) for b in range(2)]
        d_out = [cot[b, slot_ref[b, t]].astype(F32) * gates[b] for b in range(2)]
        d_ml = []
        dh_mem = []
        keeps = []
        if last:
            for b in range(2):
                f = frame_index(b, t)
                dsc[f, :MEM, :] = jnp.zeros((MEM, D), BF16)
                scale[f, :MEM, :] = jnp.zeros((MEM, 1), F32)
                cs[f, :MEM, :] = jnp.zeros((MEM, 1), F32)
                keeps.append(jnp.zeros((96, D), F32))
                d_ml.append(keeps[b])
        else:
            dh_tok = []
            at_k = slice(base_k + 32 * t, base_k + 32 * t + 32)
            hk = h_w[at_k, :]
            tok = toks[t]
            for b in range(2):
                f = frame_index(b, t)
                down = dmem[96 * b : 96 * b + 96, :]
                ds = (down * gates[b]).astype(BF16)
                keeps.append(down * (1.0 - gates[b]))
                dsc[f, :MEM, :] = ds
                c = row_sum(ds.astype(F32) * mnew[t, b])
                cs[f, :MEM, :] = c
                al = al_t[t, b]
                rows_b = slice(16 * b, 16 * b + 16)
                d_out[b] = d_out[b] + dot(al, ds, 0, 0)
                back = (al.astype(F32) * (dot(ds, tok[rows_b], 1, 1) - c)).astype(BF16)
                dh_tok.append(dot(back, wsw[...], 0, 0))
                acc = dot(back, hk[rows_b])
                if live:
                    rows_b = slice(96 * b, 96 * b + 96)
                    ml = mls[t, rows_b, :]
                    al = al_m[t, b]
                    d_ml.append(dot(al, ds, 0, 0))
                    back = (al.astype(F32) * (dot(ds, ml, 1, 1) - c)).astype(BF16)
                    dh_mem.append(dot(back, wsw[...], 0, 0))
                    at = slice(base_w + (t - 1) * 192 + 96 * b, base_w + (t - 1) * 192 + 96 * b + 96)
                    acc = acc + dot(back, h_w[at, :])
                acc_w[...] = acc_w[...] + acc
            dgk = (jnp.concatenate(dh_tok, 0) * d_w[at_k, :].astype(F32)).astype(BF16)
            d_w[at_k, :] = dgk
            da = dot(dgk, ww[...], 1, 1)
            xh = xhk[t]
            add_vec(4, col_sum(da * xh))
            dx = norm_back(da * g_write, xh, rk[t])
            for b in range(2):
                d_out[b] = d_out[b] + dx[16 * b : 16 * b + 16]
        at = slice(32 * t, 32 * t + 32)
        do = jnp.concatenate(d_out, 0)
        dob = do.astype(BF16)
        dos[at, :] = dob
        dn = jnp.zeros((32, D), F32)
        for j in range(4):
            sl = slice(D * j, D * j + D)
            dp = (dot(dob, wout[sl, :], 1, 1) * dg[t, :, sl].astype(F32)).astype(BF16)
            dpre[at, sl] = dp
            dn = dn + dot(dp, win[j], 1, 1)
        add_vec(3, col_sum(dn * xh2[t]))
        dy = do + norm_back(dn * g_ffn, xh2[t], r2[t])
        dyb = dy.astype(BF16)
        dys[at, :] = dyb
        dbig = by_head(dot(dyb, wo[...], 1, 1).astype(BF16))
        p = prob[t]
        q, k, v = qs[0, t], qs[1, t], qs[2, t]
        dp = dot(dbig, v, 1, 1)
        pf = p.astype(F32)
        ds = (pf * (dp - row_sum(dp * pf)) * (1.0 / math.sqrt(HEAD))).astype(BF16)
        dv = dot(p, dbig, 0, 0).astype(BF16)
        dq = from_heads(dot(ds, k)).astype(BF16)
        dk = dot(ds, by_head(q), 0, 0).astype(BF16)
        dqs[0, at, :] = dq
        dqs[1, at, :] = dk
        dqs[2, at, :] = dv
        du = dot(dq, wqkv[0], 1, 1) + dot(dk, wqkv[1], 1, 1) + dot(dv, wqkv[2], 1, 1)
        add_vec(2, col_sum(du * xh1[t]))
        dz = dy + norm_back(du * g_attn, xh1[t], r1[t])
        dzb = dz.astype(BF16)
        c_all = row_sum(dzb.astype(F32) * zs[t])
        dh_r = []
        for b in range(2):
            f = frame_index(b, t)
            ds = dzb[16 * b : 16 * b + 16]
            c = c_all[16 * b : 16 * b + 16]
            dsc[f, MEM:, :] = ds
            cs[f, MEM:, :] = c
            if live:
                rows_b = slice(96 * b, 96 * b + 96)
                al = al_r[t, b]
                d_ml[b] = d_ml[b] + dot(al, ds, 0, 0)
                back = (al.astype(F32) * (dot(ds, mls[t, rows_b, :], 1, 1) - c)).astype(BF16)
                dh_r.append(dot(back, wsr[...], 0, 0))
                at_b = slice(base_r + (t - 1) * 192 + 96 * b, base_r + (t - 1) * 192 + 96 * b + 96)
                acc_r[...] = acc_r[...] + dot(back, h_r[at_b, :])
        if not live:
            return
        at_m = slice(base_r + (t - 1) * 192, base_r + t * 192)
        xh = mxh[t]
        dgr = (jnp.concatenate(dh_r, 0) * d_r[at_m, :].astype(F32)).astype(BF16)
        d_r[at_m, :] = dgr
        da = dot(dgr, wr[...], 1, 1)
        add_vec(1, col_sum(da * xh))
        g = da * g_read
        if not last:
            dgw = (jnp.concatenate(dh_mem, 0) * d_w[at_m, :].astype(F32)).astype(BF16)
            d_w[at_m, :] = dgw
            da = dot(dgw, ww[...], 1, 1)
            add_vec(4, col_sum(da * xh))
            g = g + da * g_write
        dx = norm_back(g, xh, mr[t])
        for b in range(2):
            rows_b = slice(96 * b, 96 * b + 96)
            dmem[rows_b, :] = keeps[b] + d_ml[b] + dx[rows_b]

    for t in range(3, -1, -1):
        step_backward(t)

    def frame_backward(f, carry):
        at = pl.ds(pl.multiple_of(f * ROWS, ROWS), ROWS)
        x = xs[f]
        ds = dsc[f]
        al = ps[f].astype(F32) * scale[f]
        alb = al.astype(BF16)
        back = (al * (dot(ds, x, 1, 1) - cs[f])).astype(BF16)
        acc_w[...] = acc_w[...] + dot(back[:MEM], h_w[at, :])
        acc_r[...] = acc_r[...] + dot(back[MEM:], h_r[at, :])
        xh, r = norm(x.astype(F32))
        dgr = (dot(back[MEM:], wsr[...], 0, 0) * d_r[at, :].astype(F32)).astype(BF16)
        d_r[at, :] = dgr
        da = dot(dgr, wr[...], 1, 1)
        add_vec(1, col_sum(da * xh))
        g = da * g_read
        dgw = (dot(back[:MEM], wsw[...], 0, 0) * d_w[at, :].astype(F32)).astype(BF16)
        d_w[at, :] = dgw
        da = dot(dgw, ww[...], 1, 1)
        add_vec(4, col_sum(da * xh))
        g = g + da * g_write
        dx = (dot(alb, ds, 0, 0) + norm_back(g, xh, r)).astype(BF16)
        a_dx = pl.ds(pl.multiple_of(f * ROWS, ROWS), ROWS)
        xs[f] = dx
        add_vec(0, col_sum(dx.astype(F32)))
        pg[f] = dot(dx, wp[...], 1, 1).astype(BF16)
        return carry

    lax.fori_loop(0, frames, frame_backward, 0)

    n = frames * ROWS
    flat[ROW_PATCH : ROW_PATCH + PIN, :] = dot(
        px[...].reshape(n, PIN), xs[...].reshape(n, D), 0, 0
    ).astype(BF16)
    flat[ROW_RHID : ROW_RHID + D, :] = dot(a_r[...], d_r[...], 0, 0).astype(BF16)
    flat[ROW_WHID : ROW_WHID + D, :] = dot(a_w[...], d_w[...], 0, 0).astype(BF16)
    flat[ROW_AOUT : ROW_AOUT + D, :] = dot(att[...], dys[...], 0, 0).astype(BF16)
    for j in range(4):
        sl = slice(D * j, D * j + D)
        flat[ROW_FOUT + D * j : ROW_FOUT + D * j + D, :] = dot(gs[:, sl], dos[...], 0, 0).astype(BF16)
    for j in range(3):
        part = dot(us[...], dqs[j], 0, 0)
        for c in range(4):
            planes[c, pl.ds(j, D, stride=3), :] = part[:, 128 * c : 128 * c + 128]
    for c in range(4):
        at = slice(128 * c, 128 * c + 128)
        flat[ROW_QKV : ROW_QKV + 3 * D, at] = planes[c, : 3 * D, :].astype(BF16)
    for j in range(4):
        part = dot(u2[...], dpre[:, D * j : D * j + D], 0, 0)
        for c in range(4):
            planes[c, pl.ds(j, D, stride=4), :] = part[:, 128 * c : 128 * c + 128]
    for c in range(4):
        at = slice(128 * c, 128 * c + 128)
        flat[ROW_FIN : ROW_FIN + FFN, at] = planes[c, :FFN, :].astype(BF16)
    where, chosen, spread = score_masks(READ, 0)
    wide = dot(acc_r[...].astype(BF16), chosen, 0, 0).astype(BF16) * where
    flat[ROW_RSCORE : ROW_RSCORE + READ, :] = dot(spread, wide, 0, 0).astype(BF16)
    for part in range(3):
        where, chosen, spread = score_masks(MEM, part)
        wide = dot(acc_w[...].astype(BF16), chosen, 0, 0).astype(BF16) * where
        these = dot(spread, wide, 0, 0)
        for c in range(4):
            planes[c, pl.ds(part, 32, stride=3), :] = these[:, 128 * c : 128 * c + 128]
    for c in range(4):
        at = slice(128 * c, 128 * c + 128)
        flat[ROW_WSCORE : ROW_WSCORE + MEM, at] = planes[c, :MEM, :].astype(BF16)
    for k, row in enumerate((ROW_BIAS, ROW_RGAIN, ROW_AGAIN, ROW_FGAIN, ROW_WGAIN)):
        flat[row : row + 1, :] = vecs[k : k + 1, :].astype(BF16)
    flat[ROW_END:, :] = jnp.zeros((flat.shape[0] - ROW_END, D), BF16)


def main(shards, px, cot, slots, flags, chips, length):
    rows = shards.shape[1]
    total = (2 * chips - 1) * length // (BLOCK * D) * BLOCK + rows
    n = 8 * ROWS
    vmem = pl.BlockSpec(memory_space=pltpu.VMEM)
    smem = pl.BlockSpec(memory_space=pltpu.SMEM)
    v = pltpu.VMEM
    return pl.pallas_call(
        functools.partial(main_kernel, chips, length),
        out_shape=(
            jax.ShapeDtypeStruct((2, STEPS, READ, D), BF16),
            jax.ShapeDtypeStruct((8, ROWS, PIN), BF16),
            jax.ShapeDtypeStruct((total, D), BF16),
        ),
        in_specs=[smem, smem, pl.BlockSpec(memory_space=pl.ANY), vmem, vmem],
        out_specs=[vmem, vmem, vmem],
        scratch_shapes=[
            v((4, FFN, 128), F32),
            v((PIN, D), BF16),
            v((D, D), BF16),
            v((D, D), BF16),
            v((3, D, D), BF16),
            v((D, D), BF16),
            v((4, D, D), BF16),
            v((FFN, D), BF16),
            v((READ, D), BF16),
            v((MEM, D), BF16),
            v((8, D), F32),
            v((8, ROWS, D), BF16),
            v((n + 576, D), BF16),
            v((n + 480, D), BF16),
            v((n + 576, D), BF16),
            v((n + 480, D), BF16),
            v((n + 576, D), BF16),
            v((n + 480, D), BF16),
            v((8, NCOL, ROWS), BF16),
            v((8, NCOL, D), F32),
            v((8, NCOL, 1), F32),
            v((8, NCOL, 1), F32),
            v((8, NCOL, 1), F32),
            v((8, NCOL, 1), F32),
            v((8, NCOL, D), BF16),
            v((192, D), F32),
            v((192, D), F32),
            v((4, 192, D), BF16),
            v((4, 192, D), F32),
            v((4, 192, 1), F32),
            v((3, 2, MEM, D), F32),
            v((4, 2, READ, MEM), BF16),
            v((3, 2, MEM, MEM), BF16),
            v((3, 2, MEM, READ), BF16),
            v((4, 32, D), F32),
            v((4, 32, D), F32),
            v((4, 32, 1), F32),
            v((128, D), BF16),
            v((3, 4, 32, D), BF16),
            v((4, HEADS * 32, 32), BF16),
            v((128, D), BF16),
            v((4, 32, D), F32),
            v((4, 32, 1), F32),
            v((128, D), BF16),
            v((128, FFN), BF16),
            v((4, 32, FFN), BF16),
            v((3, 32, D), BF16),
            v((3, 32, D), F32),
            v((3, 32, 1), F32),
            v((3, 128, D), BF16),
            v((128, D), BF16),
            v((128, FFN), BF16),
            v((128, D), BF16),
            v((READ, D), F32),
            v((MEM, D), F32),
            v((8, D), F32),
            v((RING, rows, D), BF16),
            pltpu.SemaphoreType.DMA((RING,)),
        ],
        compiler_params=pltpu.CompilerParams(vmem_limit_bytes=VMEM_LIMIT),
        name="model",
    )(slots, flags, shards, px, cot)


def body(pixels, counts, step_mask, owner, params, cotangent):
    chips = lax.axis_size("dp")
    length = params.shape[0]
    core = lax.axis_index("grp").astype(jnp.int32)
    dp = lax.axis_index("dp").astype(jnp.int32)
    half = STEPS // 2

    positions = jnp.arange(STEPS, dtype=jnp.int32)
    valid = ((positions < counts[..., None]) & (step_mask == 1)).astype(jnp.int32)
    valid = valid.reshape(2, 2, 2, half)
    number = jnp.sum(valid, -1)
    local = jnp.arange(half, dtype=jnp.int32)
    first = jnp.min(jnp.where(valid == 1, local, half), -1) % half
    second = jnp.maximum(jnp.max(jnp.where(valid == 1, local, -1), -1), 0)
    slot = jnp.stack([first, second], -1)
    flag = jnp.stack([(number > 0), (number > 1)], -1).astype(jnp.int32)
    mine = (core + owner[:, 0]) % 2
    is_mine = jnp.arange(2, dtype=jnp.int32)[None, :] == mine[:, None]

    def of_group(values, groups):
        pick_second = (groups == 1).reshape((2,) + (1,) * (values.ndim - 2))
        return jnp.where(pick_second, values[:, 1], values[:, 0])

    own_slot = of_group(slot, mine)
    own_flag = of_group(flag, mine)
    slots = (own_slot + half * jnp.arange(2, dtype=jnp.int32)[None, :, None]).reshape(2, 4)
    flags = own_flag.reshape(2, 4)

    def of_half(values):
        return jnp.where(core == 1, values[..., 1, :], values[..., 0, :])

    here = of_half(slot)
    here_flag = of_half(flag)
    groups = jnp.stack([mine, 1 - mine], 0)
    picked = jnp.stack([of_group(here, mine), of_group(here, 1 - mine)], 0)
    where_in = jnp.stack(
        [jnp.broadcast_to(groups[:, :, None], (2, 2, 2)).reshape(8), picked.reshape(8)], 0
    )
    hit0 = (here[..., 0:1] == local) & (here_flag[..., 0:1] == 1)
    hit1 = (here[..., 1:2] == local) & (here_flag[..., 1:2] == 1)
    source = (
        jnp.where(is_mine, 0, 4)[:, :, None]
        + 2 * jnp.arange(2, dtype=jnp.int32)[:, None, None]
        + jnp.where(hit0, 0, 1)
    )
    where_out = jnp.stack([source.reshape(16), (hit0 | hit1).astype(jnp.int32).reshape(16)], 0)

    rows = window_rows(length)
    index = core * chips + dp
    offset = (index * length) % (BLOCK * D)
    win = lax.dynamic_update_slice(jnp.zeros((rows * D,), BF16), params, (offset,))
    win = win.reshape(rows, D)

    pix = pick(pixels, where_in)
    shards, px = gather(win, pix, chips)
    cot = cotangent[:, 0, 0]
    done, pg, grads = main(shards, px.reshape(8, ROWS, PIN), cot, slots, flags, chips, length)
    total, pgs = reduce(grads, pg.reshape(2, 4, ROWS, PIN), chips, length)
    shard_grad = lax.dynamic_slice(total.reshape(rows * D), (offset,), (length,))
    pixel_grad = place(pgs, where_out, pixels.shape)
    return (done[:, None, None], pixel_grad, shard_grad)


def solution(mesh):
    return jax.shard_map(
        body,
        mesh=mesh,
        in_specs=(
            P(None, None, "dp", "grp", None, None),
            P(None, None, "dp"),
            P(None, None, "dp", None),
            P(None, "dp"),
            P(("grp", "dp")),
            P(None, "grp", "dp", None, None, None),
        ),
        out_specs=(
            P(None, "grp", "dp", None, None, None),
            P(None, None, "dp", "grp", None, None),
            P(("grp", "dp")),
        ),
        check_vma=False,
    )
```

```python
import functools
import math

import jax
import jax.numpy as jnp
from jax import lax
from jax.experimental import pallas as pl
from jax.experimental.pallas import tpu as pltpu
from jax.sharding import PartitionSpec as P

MESH = pl.DeviceIdType.MESH
F32 = jnp.float32
BF16 = jnp.bfloat16

D = 512
HEADS = 8
HEAD = D // HEADS
FFN = 2048
PIN = 768
P_SIZE = 196
ROWS = 208
MEM = 96
READ = 16
NCOL = MEM + READ
STEPS = 8
BLOCK = 16
EPS = 1e-6
RING = 4
PARTS = 3
HUGE = 1e30
HALF_INT = 1 << 30

ROW_PATCH = 0
ROW_BIAS = 768
ROW_RGAIN = 769
ROW_RHID = 770
ROW_RSCORE = 1282
ROW_AGAIN = 1298
ROW_QKV = 1299
ROW_AOUT = 2835
ROW_FGAIN = 3347
ROW_FIN = 3348
ROW_FOUT = 5396
ROW_WGAIN = 7444
ROW_WHID = 7445
ROW_WSCORE = 7957
ROW_END = 8053

VMEM_LIMIT = 62 * 2**20


def dot(a, b, ca=1, cb=0):
    return lax.dot_general(a, b, (((ca,), (cb,)), ((), ())), preferred_element_type=F32)


def window_rows(length):
    return (length + BLOCK * D - 2) // (BLOCK * D) * BLOCK + BLOCK


def first_block(index, length):
    return (index * length) // (BLOCK * D)


def parts_of(chips, rows):
    bits = chips.bit_length() - 1
    high = list(range(bits - 1, 1, -1))
    blocks = rows // BLOCK
    a, b = (blocks * 3 + 4) // 8 * BLOCK, (blocks * 6 + 4) // 8 * BLOCK
    return [
        (0, a, high + [0, 1], high + [1, 0]),
        (a, b - a, high + [0, 1], high + [1, 0]),
        (b, rows - b, [0, 1] + high, [1, 0] + high),
    ]


def partners(orders, core, me):
    steps = []
    for one, two in zip(*orders):
        a = (1 - 2 * ((me // (1 << one)) % 2)) * (1 << one)
        b = (1 - 2 * ((me // (1 << two)) % 2)) * (1 << two)
        steps.append(a + core * (b - a))
    return steps


def shifted(me, steps, r):
    at = me
    for k, step in enumerate(steps):
        if (r >> k) & 1:
            at = at + step
    return at


def greet(core, me, steps):
    barrier = pltpu.get_barrier_semaphore()
    places = [(core, me + step) for step in steps] + [(1 - core, me)]
    for place in places:
        pl.semaphore_signal(barrier, inc=1, device_id=place, device_id_type=MESH)
    pl.semaphore_wait(barrier, len(places))


def remote(src, dst, s, r, place):
    return pltpu.make_async_remote_copy(
        src_ref=src, dst_ref=dst, send_sem=s, recv_sem=r, device_id=place, device_id_type=MESH
    )


def gather_kernel(chips, win, pix, out, pixout, send, recv, sibsend, sibrecv, local, pixsem):
    core = lax.axis_index("grp")
    me = lax.axis_index("dp")
    parts = parts_of(chips, win.shape[0])
    bits = chips.bit_length() - 1
    sibling = (1 - core, me)
    all_steps = [partners(part[2:], core, me) for part in parts]
    greet(core, me, all_steps[0])

    mine = core * chips + me
    started = []
    side = []

    def pass_on(p, r, src):
        start, size = parts[p][:2]
        steps = all_steps[p]
        dst = out.at[core * chips + shifted(me, steps, r), pl.ds(start, size)]
        src = dst if src is None else src.at[pl.ds(start, size)]
        for k in range(bits - 1, r.bit_length() - 1, -1):
            copy = remote(
                src, dst, send.at[p, (1 << k) - 1 + r], recv.at[p, r | (1 << k)], (core, me + steps[k])
            )
            copy.start()
            started.append(copy)
        copy = remote(src, dst, sibsend.at[p, r], sibrecv.at[p, r], sibling)
        copy.start()
        side.append(copy)

    for p in range(len(parts)):
        pass_on(p, 0, win)
    keep = pltpu.make_async_copy(win, out.at[mine], local)
    keep.start()
    swap_pix = remote(pix, pixout, pixsem.at[0], pixsem.at[1], sibling)
    swap_pix.start()
    for r in sorted(range(1, chips), key=lambda r: (bin(r).count("1"), r)):
        for p in range(len(parts)):
            start, size = parts[p][:2]
            at = out.at[core * chips + shifted(me, all_steps[p], r), pl.ds(start, size)]
            remote(at, at, send.at[p, 0], recv.at[p, r], sibling).wait_recv()
            pass_on(p, r, None)
    for copy in started:
        copy.wait_send()
    for copy in side:
        copy.wait()
    keep.wait()
    swap_pix.wait()


def gather(win, pix, chips):
    rows = win.shape[0]
    dma = pltpu.SemaphoreType.DMA
    return pl.pallas_call(
        functools.partial(gather_kernel, chips),
        out_shape=(
            jax.ShapeDtypeStruct((2 * chips, rows, D), BF16),
            jax.ShapeDtypeStruct((4, ROWS, PIN), BF16),
        ),
        in_specs=[pl.BlockSpec(memory_space=pltpu.VMEM), pl.BlockSpec(memory_space=pl.ANY)],
        out_specs=[pl.BlockSpec(memory_space=pl.ANY)] * 2,
        scratch_shapes=[
            dma((PARTS, chips)),
            dma((PARTS, chips)),
            dma((PARTS, chips)),
            dma((PARTS, chips)),
            dma(()),
            dma((2,)),
        ],
        compiler_params=pltpu.CompilerParams(collective_id=0, has_side_effects=True),
        name="gather",
    )(win, pix)


CHUNK = 64
FULL = P_SIZE // CHUNK * CHUNK
TAIL = P_SIZE - FULL


def kept(counts, mask, m, g, half):
    base = half * (STEPS // 2)
    ok = [(mask[m, g, base + i] == 1) & (base + i < counts[m, g]) for i in range(4)]
    last = jnp.int32
    first = jnp.where(ok[0], 0, jnp.where(ok[1], 1, jnp.where(ok[2], 2, 3))).astype(last)
    second = jnp.where(ok[3], 3, jnp.where(ok[2], 2, jnp.where(ok[1], 1, 0))).astype(last)
    number = sum(o.astype(jnp.int32) for o in ok)
    return (first, second), (number > 0, number > 1)


def pick_kernel(sides, counts, mask, pix, near, far):
    e = pl.program_id(0)
    slots, _ = kept(counts, mask, e % 2, sides[e], lax.axis_index("grp"))
    x = pix[0, 0, 0].reshape(4 * P_SIZE, PIN)

    def chosen(rows, cols):
        one = [(iota((rows, cols), 1) == 4 * iota((rows, cols), 0) + s).astype(BF16) for s in slots]
        return jnp.concatenate(one, 0)

    def fill(out):
        whole = chosen(CHUNK, 4 * CHUNK)
        for c in range(FULL // CHUNK):
            got = dot(whole, x[4 * CHUNK * c : 4 * CHUNK * c + 4 * CHUNK]).astype(BF16)
            for j in range(2):
                out[0, j, CHUNK * c : CHUNK * c + CHUNK] = got[CHUNK * j : CHUNK * j + CHUNK]
        rest = ROWS - FULL
        got = dot(chosen(rest, 4 * TAIL), x[4 * FULL :]).astype(BF16)
        for j in range(2):
            out[0, j, FULL:] = got[rest * j : rest * j + rest]

    @pl.when(e < 2)
    def _():
        fill(near)

    @pl.when(e >= 2)
    def _():
        fill(far)


def pick(pixels, sides, counts, mask):
    block = (1, 2, ROWS, PIN)
    return pl.pallas_call(
        pick_kernel,
        out_shape=(jax.ShapeDtypeStruct((2, 2, ROWS, PIN), BF16),) * 2,
        grid_spec=pltpu.PrefetchScalarGridSpec(
            num_scalar_prefetch=3,
            grid=(4,),
            in_specs=[
                pl.BlockSpec(
                    (1, 1, 1, P_SIZE, 4, PIN), lambda e, s, *_: (e % 2, s[e], 0, 0, 0, 0)
                )
            ],
            out_specs=[
                pl.BlockSpec(block, lambda e, *_: (jnp.minimum(e, 1), 0, 0, 0)),
                pl.BlockSpec(block, lambda e, *_: (jnp.maximum(e, 2) - 2, 0, 0, 0)),
            ],
        ),
        compiler_params=pltpu.CompilerParams(vmem_limit_bytes=VMEM_LIMIT),
        name="pick",
    )(sides, counts, mask, jnp.swapaxes(pixels, 3, 4))


def place_kernel(sides, counts, mask, near, far, out):
    e = pl.program_id(0)
    m = e % 2
    slots, flags = kept(counts, mask, m, sides[e], lax.axis_index("grp"))
    where = [jnp.where(flag, slot, -HALF_INT) for slot, flag in zip(slots, flags)]

    def spread(rows, cols):
        one = [(iota((rows, cols), 0) == 4 * iota((rows, cols), 1) + s).astype(BF16) for s in where]
        return jnp.concatenate(one, 1)

    def to_slots(first, count, weights):
        at = slice(first, first + count)
        these = [jnp.where(e < 2, near[0, 0, j, at], far[0, j, at]) for j in range(2)]
        return dot(weights, jnp.concatenate(these, 0)).astype(BF16)

    whole = spread(4 * CHUNK, CHUNK)
    for c in range(FULL // CHUNK):
        got = to_slots(CHUNK * c, CHUNK, whole)
        out[0, 0, 0, CHUNK * c : CHUNK * c + CHUNK] = got.reshape(CHUNK, 4, PIN)
    got = to_slots(FULL, ROWS - FULL, spread(4 * TAIL, ROWS - FULL))
    out[0, 0, 0, FULL:] = got.reshape(TAIL, 4, PIN)


def place(near, far, sides, counts, mask, shape):
    m, g, c, s, rows, cols = shape
    out = pl.pallas_call(
        place_kernel,
        out_shape=jax.ShapeDtypeStruct((m, g, c, rows, s, cols), BF16),
        grid_spec=pltpu.PrefetchScalarGridSpec(
            num_scalar_prefetch=3,
            grid=(4,),
            in_specs=[
                pl.BlockSpec((1, 1, 2, ROWS, PIN), lambda e, *_: (0, jnp.minimum(e, 1), 0, 0, 0)),
                pl.BlockSpec((1, 2, ROWS, PIN), lambda e, *_: (jnp.maximum(e, 2) - 2, 0, 0, 0)),
            ],
            out_specs=pl.BlockSpec(
                (1, 1, 1, rows, s, cols), lambda e, s, *_: (e % 2, s[e], 0, 0, 0, 0)
            ),
        ),
        compiler_params=pltpu.CompilerParams(vmem_limit_bytes=VMEM_LIMIT),
        name="place",
    )(sides, counts, mask, near.reshape(2, 2, 2, ROWS, PIN), far.reshape(2, 2, ROWS, PIN))
    return jnp.swapaxes(out, 3, 4)


def frame_index(clip, step):
    return (step // 2) * 4 + clip * 2 + step % 2


def norm(x):
    mean = jnp.mean(x, -1, keepdims=True)
    centered = x - mean
    r = lax.rsqrt(jnp.mean(centered * centered, -1, keepdims=True) + EPS)
    return centered * r, r


def norm_back(g, xh, r):
    return r * (g - jnp.mean(g, -1, keepdims=True) - xh * jnp.mean(g * xh, -1, keepdims=True))


def gelu(x):
    cdf = 0.5 + 0.5 * lax.erf(x * math.sqrt(0.5))
    slope = cdf + x * (jnp.exp(-0.5 * x * x) * (1.0 / math.sqrt(2.0 * math.pi)))
    return (x * cdf).astype(BF16), slope.astype(BF16)


def col_sum(x):
    return jnp.sum(x, 0, keepdims=True)


def row_sum(x):
    return jnp.sum(x, -1, keepdims=True)


def row_max(x):
    return jnp.max(x, -1, keepdims=True)


def iota(shape, dim):
    return lax.broadcasted_iota(jnp.int32, shape, dim)


def score_masks(width, part):
    group = 512 // math.gcd(512, width)
    lane = iota((D, D), 1) + 512 * part
    hidden = iota((D, D), 0)
    where = ((hidden % group) == (lane // width)).astype(BF16)
    lane = iota((width, D), 1) + 512 * part
    pick = ((lane % width) == iota((width, D), 0)).astype(BF16)
    rows = 512 // group
    spread = ((iota((D, rows), 0) // group) == iota((D, rows), 1)).astype(BF16)
    return where, pick, spread


def main_kernel(
    chips,
    length,
    sides,
    counts,
    mask,
    shards,
    pix,
    far,
    cot,
    done,
    pg,
    total,
    pgout,
    flat,
    planes,
    wp,
    wr,
    ww,
    wbig,
    wsr,
    wsw,
    gains,
    xs,
    a_r,
    a_w,
    h_r,
    h_w,
    d_r,
    d_w,
    ps,
    rs,
    stat,
    dsc,
    mem,
    dmem,
    mls,
    mxh,
    mr,
    mnew,
    al_r,
    al_m,
    al_t,
    zs,
    xh1,
    r1,
    us,
    qs,
    prob,
    att,
    xh2,
    r2,
    u2,
    gs,
    dg,
    toks,
    xhk,
    rk,
    dqs,
    dys,
    dpre,
    dos,
    acc_r,
    acc_w,
    vecs,
    ring,
    held,
    ring_sem,
    send,
    recv,
    sibsend,
    sibrecv,
    pixsem,
    ready,
):
    rows = shards.shape[1]
    frames = 8
    core = lax.axis_index("grp")
    me = lax.axis_index("dp")
    sibling = (1 - core, me)
    parts = parts_of(chips, rows)
    bits = chips.bit_length() - 1
    all_steps = [partners(part[2:], core, me) for part in parts]
    other_steps = [partners(part[2:], 1 - core, me) for part in parts]
    greet(core, me, all_steps[0])

    slot_of = []
    flag_of = []
    for b in range(2):
        pairs = [kept(counts, mask, b, sides[b], half) for half in range(2)]
        slot_of.append([pairs[t // 2][0][t % 2] for t in range(4)])
        flag_of.append([pairs[t // 2][1][t % 2] for t in range(4)])

    wo = wbig.at[0:D]
    wqkv = [wbig.at[D + D * j : 2 * D + D * j] for j in range(3)]
    win = [wbig.at[4 * D + D * j : 5 * D + D * j] for j in range(4)]
    wout = wbig.at[8 * D : 12 * D]

    def fetch(i):
        return pltpu.make_async_copy(shards.at[i], ring.at[i % RING], ring_sem.at[i % RING])

    def lay(i, carry):
        fetch(i).wait()
        start = pl.multiple_of(first_block(i, length) * BLOCK, BLOCK)
        flat[pl.ds(start, BLOCK), :] = flat[pl.ds(start, BLOCK), :] + ring[i % RING, :BLOCK, :]
        start = pl.multiple_of(start + BLOCK, BLOCK)
        flat[pl.ds(start, rows - BLOCK), :] = ring[i % RING, BLOCK:, :]

        @pl.when(i + RING < 2 * chips)
        def _():
            fetch(i + RING).start()

        return carry

    flat[:BLOCK, :] = jnp.zeros((BLOCK, D), BF16)
    for i in range(RING):
        fetch(i).start()
    lax.fori_loop(0, 2 * chips, lay, 0)

    wp[...] = flat[ROW_PATCH : ROW_PATCH + PIN, :]
    wr[...] = flat[ROW_RHID : ROW_RHID + D, :]
    wo[...] = flat[ROW_AOUT : ROW_AOUT + D, :]
    wout[...] = flat[ROW_FOUT : ROW_FOUT + FFN, :]
    ww[...] = flat[ROW_WHID : ROW_WHID + D, :]
    for k, row in enumerate((ROW_BIAS, ROW_RGAIN, ROW_AGAIN, ROW_FGAIN, ROW_WGAIN)):
        base = row // BLOCK * BLOCK
        gains[k : k + 1, :] = flat[base : base + BLOCK, :].astype(F32)[row - base : row - base + 1, :]
    for row, count, dst in ((ROW_QKV, 3, wqkv), (ROW_FIN, 4, win)):
        for q in range(4):
            base = row + count * 128 * q
            for c in range(4):
                at = slice(c * 128, c * 128 + 128)
                planes[c, : count * 128, :] = flat[base : base + count * 128, at].astype(F32)
                for j in range(count):
                    these = planes[c, pl.ds(j, 128, stride=count), :]
                    dst[j][128 * q : 128 * q + 128, at] = these.astype(BF16)
    where, chosen, spread = score_masks(READ, 0)
    wide = dot(spread, flat[ROW_RSCORE : ROW_RSCORE + READ, :]).astype(BF16) * where
    wsr[...] = dot(chosen, wide, 1, 1).astype(BF16)
    scores = jnp.zeros((MEM, D), F32)
    for c in range(4):
        at = slice(c * 128, c * 128 + 128)
        planes[c, :MEM, :] = flat[ROW_WSCORE : ROW_WSCORE + MEM, at].astype(F32)
    for part in range(3):
        where, chosen, spread = score_masks(MEM, part)
        these = jnp.concatenate(
            [planes[c, pl.ds(part, 32, stride=3), :] for c in range(4)], -1
        ).astype(BF16)
        wide = dot(spread, these).astype(BF16) * where
        scores = scores + dot(chosen, wide, 1, 1)
    wsw[...] = scores.astype(BF16)

    bias = gains[0:1, :]
    g_read = gains[1:2, :]
    g_attn = gains[2:3, :]
    g_ffn = gains[3:4, :]
    g_write = gains[4:5, :]

    lanes = iota((NCOL, ROWS), 1) < P_SIZE

    def frame_forward(f, carry):
        at = pl.ds(pl.multiple_of(f * ROWS, ROWS), ROWS)
        seen = jnp.where(f // 4 == core, pix[f % 4], far[f % 4])
        x = (dot(seen, wp[...]) + bias).astype(BF16)
        xs[f] = x
        xh, r = norm(x.astype(F32))
        a_r[at, :] = (xh * g_read).astype(BF16)
        a_w[at, :] = (xh * g_write).astype(BF16)
        h, d = gelu(dot(a_r[at, :], wr[...]))
        h_r[at, :] = h
        d_r[at, :] = d
        s_read = dot(wsr[...], h, 1, 1)
        h, d = gelu(dot(a_w[at, :], ww[...]))
        h_w[at, :] = h
        d_w[at, :] = d
        s_write = dot(wsw[...], h, 1, 1)
        scores = jnp.where(lanes, jnp.concatenate([s_write, s_read], 0), -HUGE)
        best = row_max(scores)
        p = jnp.exp(scores - best)
        pb = p.astype(BF16)
        ps[f] = pb
        stat[f, :, 0:1] = best
        stat[f, :, 1:2] = row_sum(p)
        rs[f] = dot(pb, x)
        return carry

    lax.fori_loop(0, frames, frame_forward, 0)

    mem[...] = jnp.zeros(mem.shape, F32)
    head_of = [(iota((1, D), 1) // HEAD == h) for h in range(HEADS)]
    same_clip = ((iota((HEADS * 32, 32), 0) // READ) % 2) == (iota((HEADS * 32, 32), 1) // READ)
    zero = jnp.zeros((), F32)

    def by_head(x):
        return jnp.concatenate([jnp.where(m, x, jnp.zeros_like(x)) for m in head_of], 0)

    def from_heads(x):
        total = jnp.where(head_of[0], x[:32], zero)
        for h in range(1, HEADS):
            total = total + jnp.where(head_of[h], x[32 * h : 32 * h + 32], zero)
        return total

    base_r = frames * ROWS
    base_w = frames * ROWS
    base_k = base_w + 2 * 192

    def step_forward(t):
        live = t > 0
        last = t == 3
        if live:
            ml = mem[...].astype(BF16)
            mls[t - 1] = ml
            xh, r = norm(ml.astype(F32))
            mxh[t - 1] = xh
            mr[t - 1] = r
            at = slice(base_r + (t - 1) * 192, base_r + t * 192)
            a = (xh * g_read).astype(BF16)
            a_r[at, :] = a
            h, d = gelu(dot(a, wr[...]))
            h_r[at, :] = h
            d_r[at, :] = d
            if not last:
                a = (xh * g_write).astype(BF16)
                a_w[at, :] = a
                hw, d = gelu(dot(a, ww[...]))
                h_w[at, :] = hw
                d_w[at, :] = d
        z_parts = []
        for b in range(2):
            f = frame_index(b, t)
            m_f = stat[f, MEM:, 0:1]
            if live:
                s = dot(wsr[...], h[96 * b : 96 * b + 96], 1, 1)
                best = jnp.maximum(row_max(s), m_f)
                e = jnp.exp(s - best)
                part = row_sum(e)
            else:
                best = jnp.maximum(m_f, 0.0)
                part = MEM * jnp.exp(-best)
            w = jnp.exp(m_f - best)
            inv = 1.0 / (part + w * stat[f, MEM:, 1:2])
            stat[f, MEM:, 2:3] = w * inv
            z = (w * inv) * rs[f, MEM:, :]
            if live:
                al = (e * inv).astype(BF16)
                al_r[t - 1, b] = al
                z = z + dot(al, ml[96 * b : 96 * b + 96])
            z_parts.append(z)
        z = jnp.concatenate(z_parts, 0)
        zs[t] = z
        at = slice(32 * t, 32 * t + 32)
        xh, r = norm(z)
        xh1[t] = xh
        r1[t] = r
        u = (xh * g_attn).astype(BF16)
        us[at, :] = u
        q = dot(u, wqkv[0][...]).astype(BF16)
        k = dot(u, wqkv[1][...]).astype(BF16)
        v = dot(u, wqkv[2][...]).astype(BF16)
        qs[0, t] = q
        qs[1, t] = k
        qs[2, t] = v
        s = jnp.where(same_clip, dot(by_head(q), k, 1, 1) * (1.0 / math.sqrt(HEAD)), -HUGE)
        e = jnp.exp(s - row_max(s))
        p = (e / row_sum(e)).astype(BF16)
        prob[t] = p
        joined = from_heads(dot(p, v)).astype(BF16)
        att[at, :] = joined
        y = z + dot(joined, wo[...])
        xh, r = norm(y)
        xh2[t] = xh
        r2[t] = r
        n = (xh * g_ffn).astype(BF16)
        u2[at, :] = n
        o = y
        for j in range(4):
            g, d = gelu(dot(n, win[j][...]))
            gs[at, D * j : D * j + D] = g
            dg[t, :, D * j : D * j + D] = d
            o = o + dot(g, wout[D * j : D * j + D, :])
        tok = o.astype(BF16)
        toks[t] = tok
        if last:
            return
        xh, r = norm(tok.astype(F32))
        xhk[t] = xh
        rk[t] = r
        a = (xh * g_write).astype(BF16)
        at = slice(base_k + 32 * t, base_k + 32 * t + 32)
        a_w[at, :] = a
        hk, d = gelu(dot(a, ww[...]))
        h_w[at, :] = hk
        d_w[at, :] = d
        for b in range(2):
            f = frame_index(b, t)
            m_f = stat[f, :MEM, 0:1]
            s_tok = dot(wsw[...], hk[16 * b : 16 * b + 16], 1, 1)
            best = jnp.maximum(row_max(s_tok), m_f)
            if live:
                s = dot(wsw[...], hw[96 * b : 96 * b + 96], 1, 1)
                best = jnp.maximum(best, row_max(s))
                e = jnp.exp(s - best)
                part = row_sum(e)
            else:
                best = jnp.maximum(best, 0.0)
                part = MEM * jnp.exp(-best)
            e_tok = jnp.exp(s_tok - best)
            w = jnp.exp(m_f - best)
            inv = 1.0 / (part + row_sum(e_tok) + w * stat[f, :MEM, 1:2])
            stat[f, :MEM, 2:3] = w * inv
            al = (e_tok * inv).astype(BF16)
            al_t[t, b] = al
            new = (w * inv) * rs[f, :MEM, :] + dot(al, tok[16 * b : 16 * b + 16])
            if live:
                al = (e * inv).astype(BF16)
                al_m[t - 1, b] = al
                new = new + dot(al, ml[96 * b : 96 * b + 96])
            mnew[t, b] = new
            old = mem[96 * b : 96 * b + 96, :]
            mem[96 * b : 96 * b + 96, :] = jnp.where(flag_of[b][t], new, old)

    for t in range(4):
        step_forward(t)

    vecs[...] = jnp.zeros(vecs.shape, F32)
    acc_r[...] = jnp.zeros(acc_r.shape, F32)
    acc_w[...] = jnp.zeros(acc_w.shape, F32)
    dmem[...] = jnp.zeros(dmem.shape, F32)

    def add_vec(k, x):
        vecs[k : k + 1, :] = vecs[k : k + 1, :] + x

    def step_backward(t):
        live = t > 0
        last = t == 3
        gates = [jnp.where(flag_of[b][t], 1.0, 0.0) for b in range(2)]
        d_out = []
        for b in range(2):
            base = 4 * (t // 2)
            given = cot[b, base + 3]
            for i in range(3):
                given = jnp.where(slot_of[b][t] == i, cot[b, base + i], given)
            d_out.append(given.astype(F32) * gates[b])
        d_ml = []
        dh_mem = []
        keeps = []
        if last:
            for b in range(2):
                f = frame_index(b, t)
                dsc[f, :MEM, :] = jnp.zeros((MEM, D), BF16)
                stat[f, :MEM, 2:3] = jnp.zeros((MEM, 1), F32)
                stat[f, :MEM, 3:4] = jnp.zeros((MEM, 1), F32)
                keeps.append(jnp.zeros((96, D), F32))
                d_ml.append(keeps[b])
        else:
            dh_tok = []
            at_k = slice(base_k + 32 * t, base_k + 32 * t + 32)
            hk = h_w[at_k, :]
            tok = toks[t]
            for b in range(2):
                f = frame_index(b, t)
                down = dmem[96 * b : 96 * b + 96, :]
                ds = (down * gates[b]).astype(BF16)
                keeps.append(down * (1.0 - gates[b]))
                dsc[f, :MEM, :] = ds
                c = row_sum(ds.astype(F32) * mnew[t, b])
                stat[f, :MEM, 3:4] = c
                al = al_t[t, b]
                rows_b = slice(16 * b, 16 * b + 16)
                d_out[b] = d_out[b] + dot(al, ds, 0, 0)
                back = (al.astype(F32) * (dot(ds, tok[rows_b], 1, 1) - c)).astype(BF16)
                dh_tok.append(dot(back, wsw[...], 0, 0))
                acc = dot(back, hk[rows_b])
                if live:
                    rows_b = slice(96 * b, 96 * b + 96)
                    ml = mls[t - 1, rows_b, :]
                    al = al_m[t - 1, b]
                    d_ml.append(dot(al, ds, 0, 0))
                    back = (al.astype(F32) * (dot(ds, ml, 1, 1) - c)).astype(BF16)
                    dh_mem.append(dot(back, wsw[...], 0, 0))
                    at = slice(base_w + (t - 1) * 192 + 96 * b, base_w + (t - 1) * 192 + 96 * b + 96)
                    acc = acc + dot(back, h_w[at, :])
                acc_w[...] = acc_w[...] + acc
            dgk = (jnp.concatenate(dh_tok, 0) * d_w[at_k, :].astype(F32)).astype(BF16)
            d_w[at_k, :] = dgk
            da = dot(dgk, ww[...], 1, 1)
            xh = xhk[t]
            add_vec(4, col_sum(da * xh))
            dx = norm_back(da * g_write, xh, rk[t])
            for b in range(2):
                d_out[b] = d_out[b] + dx[16 * b : 16 * b + 16]
        at = slice(32 * t, 32 * t + 32)
        do = jnp.concatenate(d_out, 0)
        dob = do.astype(BF16)
        dos[at, :] = dob
        dn = jnp.zeros((32, D), F32)
        for j in range(4):
            sl = slice(D * j, D * j + D)
            dp = (dot(dob, wout[sl, :], 1, 1) * dg[t, :, sl].astype(F32)).astype(BF16)
            dpre[at, sl] = dp
            dn = dn + dot(dp, win[j][...], 1, 1)
        add_vec(3, col_sum(dn * xh2[t]))
        dy = do + norm_back(dn * g_ffn, xh2[t], r2[t])
        dyb = dy.astype(BF16)
        dys[at, :] = dyb
        dbig = by_head(dot(dyb, wo[...], 1, 1).astype(BF16))
        p = prob[t]
        q, k, v = qs[0, t], qs[1, t], qs[2, t]
        dp = dot(dbig, v, 1, 1)
        pf = p.astype(F32)
        ds = (pf * (dp - row_sum(dp * pf)) * (1.0 / math.sqrt(HEAD))).astype(BF16)
        dv = dot(p, dbig, 0, 0).astype(BF16)
        dq = from_heads(dot(ds, k)).astype(BF16)
        dk = dot(ds, by_head(q), 0, 0).astype(BF16)
        dqs[0, at, :] = dq
        dqs[1, at, :] = dk
        dqs[2, at, :] = dv
        du = dot(dq, wqkv[0][...], 1, 1) + dot(dk, wqkv[1][...], 1, 1) + dot(dv, wqkv[2][...], 1, 1)
        add_vec(2, col_sum(du * xh1[t]))
        dz = dy + norm_back(du * g_attn, xh1[t], r1[t])
        dzb = dz.astype(BF16)
        c_all = row_sum(dzb.astype(F32) * zs[t])
        dh_r = []
        for b in range(2):
            f = frame_index(b, t)
            ds = dzb[16 * b : 16 * b + 16]
            c = c_all[16 * b : 16 * b + 16]
            dsc[f, MEM:, :] = ds
            stat[f, MEM:, 3:4] = c
            if live:
                rows_b = slice(96 * b, 96 * b + 96)
                al = al_r[t - 1, b]
                d_ml[b] = d_ml[b] + dot(al, ds, 0, 0)
                back = (al.astype(F32) * (dot(ds, mls[t - 1, rows_b, :], 1, 1) - c)).astype(BF16)
                dh_r.append(dot(back, wsr[...], 0, 0))
                at_b = slice(base_r + (t - 1) * 192 + 96 * b, base_r + (t - 1) * 192 + 96 * b + 96)
                acc_r[...] = acc_r[...] + dot(back, h_r[at_b, :])
        if not live:
            return
        at_m = slice(base_r + (t - 1) * 192, base_r + t * 192)
        xh = mxh[t - 1]
        dgr = (jnp.concatenate(dh_r, 0) * d_r[at_m, :].astype(F32)).astype(BF16)
        d_r[at_m, :] = dgr
        da = dot(dgr, wr[...], 1, 1)
        add_vec(1, col_sum(da * xh))
        g = da * g_read
        if not last:
            dgw = (jnp.concatenate(dh_mem, 0) * d_w[at_m, :].astype(F32)).astype(BF16)
            d_w[at_m, :] = dgw
            da = dot(dgw, ww[...], 1, 1)
            add_vec(4, col_sum(da * xh))
            g = g + da * g_write
        dx = norm_back(g, xh, mr[t - 1])
        for b in range(2):
            rows_b = slice(96 * b, 96 * b + 96)
            dmem[rows_b, :] = keeps[b] + d_ml[b] + dx[rows_b]

    for t in range(3, -1, -1):
        step_backward(t)

    pl.semaphore_signal(ready, inc=1, device_id=sibling, device_id_type=MESH)
    flat[ROW_AOUT : ROW_AOUT + D, :] = dot(att[...], dys[...], 0, 0).astype(BF16)
    for j in range(4):
        sl = slice(D * j, D * j + D)
        flat[ROW_FOUT + D * j : ROW_FOUT + D * j + D, :] = dot(gs[:, sl], dos[...], 0, 0).astype(BF16)
    for row, count, left, right in (
        (ROW_QKV, 3, us, lambda j: dqs[j]),
        (ROW_FIN, 4, u2, lambda j: dpre[:, D * j : D * j + D]),
    ):
        for q in range(4):
            for j in range(count):
                part = dot(left[:, 128 * q : 128 * q + 128], right(j), 0, 0)
                for c in range(4):
                    planes[c, pl.ds(j, 128, stride=count), :] = part[:, 128 * c : 128 * c + 128]
            base = row + count * 128 * q
            for c in range(4):
                at = slice(128 * c, 128 * c + 128)
                flat[base : base + count * 128, at] = planes[c, : count * 128, :].astype(BF16)
    flat[ROW_AGAIN : ROW_AGAIN + 1, :] = vecs[2:3, :].astype(BF16)
    flat[ROW_FGAIN : ROW_FGAIN + 1, :] = vecs[3:4, :].astype(BF16)

    def block_of(index):
        return first_block(index, length) * BLOCK

    def is_late(index):
        start = block_of(index)
        return (start < ROW_QKV) | (start + rows > ROW_WGAIN)

    def place_of(p, r):
        start, size = parts[p][:2]
        return chips * start + r * size

    def side(p, r):
        return wbig.at[pl.ds(place_of(p, r), parts[p][1])]

    def slot(p, k, r):
        start, size = parts[p][:2]
        return (chips - 1) * start + ((1 << k) - 1 + r) * size

    def turns(top, end):
        return [(p, r) for r in range(top - 1, end - 1, -1) for p in range(len(parts))]


    def swap(p, r):
        index = (1 - core) * chips + shifted(me, other_steps[p], r)
        start = pl.multiple_of(block_of(index) + parts[p][0], BLOCK)
        src = flat.at[pl.ds(start, parts[p][1])]
        return remote(src, side(p, r), sibsend.at[p, r], sibrecv.at[p, r], sibling), index

    def send_on(p, r):
        top = r.bit_length() - 1
        low = r - (1 << top)
        return remote(
            side(p, r),
            held.at[pl.ds(slot(p, top, low), parts[p][1])],
            send.at[p, r],
            recv.at[p, (1 << top) - 1 + low],
            (core, me + all_steps[p][top]),
        )

    def swap_all(late):
        for p, r in turns(chips, 0):
            copy, index = swap(p, r)

            @pl.when(is_late(index) == late)
            def _(copy=copy):
                copy.start()

    def turn(p, r, late):
        index = core * chips + shifted(me, all_steps[p], r)
        start, size = parts[p][:2]

        @pl.when(is_late(index) == late)
        def _():
            swap(p, r)[0].wait_recv()
            slots = []
            for k in range(bits - 1, r.bit_length() - 1, -1):
                at = held.at[pl.ds(slot(p, k, r), size)]
                remote(at, at, send.at[p, r], recv.at[p, (1 << k) - 1 + r], sibling).wait_recv()
                slots.append(slot(p, k, r))
            base = block_of(index) + start

            def add(i, carry):
                step = i * BLOCK
                at = pl.ds(pl.multiple_of(place_of(p, r) + step, BLOCK), BLOCK)
                mine = flat[pl.ds(pl.multiple_of(base + step, BLOCK), BLOCK), :]
                value = mine.astype(F32) + wbig[at, :].astype(F32)
                for one in slots:
                    value = value + held[pl.ds(pl.multiple_of(one + step, BLOCK), BLOCK), :].astype(F32)
                if r == 0:
                    total[pl.ds(pl.multiple_of(start + step, BLOCK), BLOCK), :] = value
                else:
                    wbig[at, :] = value.astype(BF16)
                return carry

            lax.fori_loop(0, size // BLOCK, add, 0)
            if r > 0:
                send_on(p, r).start()

    def frame_backward(f):
        at = slice(f * ROWS, f * ROWS + ROWS)
        x = xs[f]
        ds = dsc[f]
        al = ps[f].astype(F32) * stat[f, :, 2:3]
        alb = al.astype(BF16)
        back = (al * (dot(ds, x, 1, 1) - stat[f, :, 3:4])).astype(BF16)
        acc_w[...] = acc_w[...] + dot(back[:MEM], h_w[at, :])
        acc_r[...] = acc_r[...] + dot(back[MEM:], h_r[at, :])
        xh, r = norm(x.astype(F32))
        dgr = (dot(back[MEM:], wsr[...], 0, 0) * d_r[at, :].astype(F32)).astype(BF16)
        d_r[at, :] = dgr
        da = dot(dgr, wr[...], 1, 1)
        add_vec(1, col_sum(da * xh))
        g = da * g_read
        dgw = (dot(back[:MEM], wsw[...], 0, 0) * d_w[at, :].astype(F32)).astype(BF16)
        d_w[at, :] = dgw
        da = dot(dgw, ww[...], 1, 1)
        add_vec(4, col_sum(da * xh))
        g = g + da * g_write
        dx = (dot(alb, ds, 0, 0) + norm_back(g, xh, r)).astype(BF16)
        xs[f] = dx
        add_vec(0, col_sum(dx.astype(F32)))
        to = jnp.where(core == f // 4, 0, 4) + f % 4
        pg[to] = dot(dx, wp[...], 1, 1).astype(BF16)

    pl.semaphore_wait(ready, 1)
    swap_all(False)
    half, quarter = chips // 2, chips // 4
    for first, todo in ((0, turns(chips, half)), (4, turns(half, quarter))):
        every = len(todo) // 4
        for i, (p, r) in enumerate(todo):
            if i % every == 0 and i // every < 4:
                frame_backward(first + i // every)
            turn(p, r, False)

    swap_pix = remote(pg.at[pl.ds(4, 4)], pgout, pixsem.at[0], pixsem.at[1], sibling)
    swap_pix.start()
    n = 4 * ROWS
    flat[ROW_PATCH : ROW_PATCH + PIN, :] = (
        dot(pix[...].reshape(n, PIN), xs[pl.ds(4 * core, 4)].reshape(n, D), 0, 0)
        + dot(far[...].reshape(n, PIN), xs[pl.ds(4 - 4 * core, 4)].reshape(n, D), 0, 0)
    ).astype(BF16)
    flat[ROW_RHID : ROW_RHID + D, :] = dot(a_r[...], d_r[...], 0, 0).astype(BF16)
    flat[ROW_WHID : ROW_WHID + D, :] = dot(a_w[...], d_w[...], 0, 0).astype(BF16)
    where, chosen, spread = score_masks(READ, 0)
    wide = dot(acc_r[...].astype(BF16), chosen, 0, 0).astype(BF16) * where
    flat[ROW_RSCORE : ROW_RSCORE + READ, :] = dot(spread, wide, 0, 0).astype(BF16)
    for part in range(3):
        where, chosen, spread = score_masks(MEM, part)
        wide = dot(acc_w[...].astype(BF16), chosen, 0, 0).astype(BF16) * where
        these = dot(spread, wide, 0, 0)
        for c in range(4):
            planes[c, pl.ds(part, 32, stride=3), :] = these[:, 128 * c : 128 * c + 128]
    for c in range(4):
        at = slice(128 * c, 128 * c + 128)
        flat[ROW_WSCORE : ROW_WSCORE + MEM, at] = planes[c, :MEM, :].astype(BF16)
    for k, row in ((0, ROW_BIAS), (1, ROW_RGAIN), (4, ROW_WGAIN)):
        flat[row : row + 1, :] = vecs[k : k + 1, :].astype(BF16)
    flat[ROW_END:, :] = jnp.zeros((flat.shape[0] - ROW_END, D), BF16)

    swap_all(True)
    for b in range(2):
        for s in range(STEPS):
            value = jnp.zeros((READ, D), BF16)
            for t in (s // 4 * 2, s // 4 * 2 + 1):
                hit = (slot_of[b][t] == s % 4) & flag_of[b][t]
                value = jnp.where(hit, toks[t, READ * b : READ * b + READ, :], value)
            done[b, s] = value
    for p, r in turns(chips, half):
        turn(p, r, True)
    early = turns(quarter, 0)
    for i, (p, r) in enumerate(turns(half, quarter)):
        if i < len(early):
            turn(*early[i], False)
        turn(p, r, True)
    for p, r in early:
        turn(p, r, True)
    for p, r in turns(chips, 0):
        swap(p, r)[0].wait_send()
        if r > 0:
            send_on(p, r).wait_send()
    swap_pix.wait()


def main(shards, pix, far, cot, sides, counts, mask, chips, length):
    rows = shards.shape[1]
    height = (2 * chips - 1) * length // (BLOCK * D) * BLOCK + rows
    n = 8 * ROWS
    vmem = pl.BlockSpec(memory_space=pltpu.VMEM)
    smem = pl.BlockSpec(memory_space=pltpu.SMEM)
    hbm = pl.BlockSpec(memory_space=pl.ANY)
    v = pltpu.VMEM
    dma = pltpu.SemaphoreType.DMA
    return pl.pallas_call(
        functools.partial(main_kernel, chips, length),
        out_shape=(
            jax.ShapeDtypeStruct((2, STEPS, READ, D), BF16),
            jax.ShapeDtypeStruct((8, ROWS, PIN), BF16),
            jax.ShapeDtypeStruct((rows, D), F32),
            jax.ShapeDtypeStruct((4, ROWS, PIN), BF16),
        ),
        in_specs=[smem, smem, smem, hbm, vmem, vmem, vmem],
        out_specs=[vmem, vmem, vmem, hbm],
        scratch_shapes=[
            v((height, D), BF16),
            v((4, D, 128), F32),
            v((PIN, D), BF16),
            v((D, D), BF16),
            v((D, D), BF16),
            v((max(12 * D, chips * rows), D), BF16),
            v((READ, D), BF16),
            v((MEM, D), BF16),
            v((8, D), F32),
            v((8, ROWS, D), BF16),
            v((n + 576, D), BF16),
            v((n + 480, D), BF16),
            v((n + 576, D), BF16),
            v((n + 480, D), BF16),
            v((n + 576, D), BF16),
            v((n + 480, D), BF16),
            v((8, NCOL, ROWS), BF16),
            v((8, NCOL, D), F32),
            v((8, NCOL, 8), F32),
            v((8, NCOL, D), BF16),
            v((192, D), F32),
            v((192, D), F32),
            v((3, 192, D), BF16),
            v((3, 192, D), F32),
            v((3, 192, 1), F32),
            v((3, 2, MEM, D), F32),
            v((3, 2, READ, MEM), BF16),
            v((2, 2, MEM, MEM), BF16),
            v((3, 2, MEM, READ), BF16),
            v((4, 32, D), F32),
            v((4, 32, D), F32),
            v((4, 32, 1), F32),
            v((128, D), BF16),
            v((3, 4, 32, D), BF16),
            v((4, HEADS * 32, 32), BF16),
            v((128, D), BF16),
            v((4, 32, D), F32),
            v((4, 32, 1), F32),
            v((128, D), BF16),
            v((128, FFN), BF16),
            v((4, 32, FFN), BF16),
            v((4, 32, D), BF16),
            v((3, 32, D), F32),
            v((3, 32, 1), F32),
            v((3, 128, D), BF16),
            v((128, D), BF16),
            v((128, FFN), BF16),
            v((128, D), BF16),
            v((READ, D), F32),
            v((MEM, D), F32),
            v((8, D), F32),
            v((RING, rows, D), BF16),
            v(((chips - 1) * rows, D), BF16),
            dma((RING,)),
            dma((PARTS, chips)),
            dma((PARTS, chips)),
            dma((PARTS, chips)),
            dma((PARTS, chips)),
            dma((2,)),
            pltpu.SemaphoreType.REGULAR,
        ],
        compiler_params=pltpu.CompilerParams(
            collective_id=1, has_side_effects=True, vmem_limit_bytes=VMEM_LIMIT
        ),
        name="model",
    )(sides, counts, mask, shards, pix, far, cot)


def body(pixels, counts, step_mask, owner, params, cotangent):
    chips = lax.axis_size("dp")
    length = params.shape[0]
    core = lax.axis_index("grp").astype(jnp.int32)
    dp = lax.axis_index("dp").astype(jnp.int32)
    counts = counts[:, :, 0]
    mask = step_mask[:, :, 0]
    mine = (core + owner[:, 0]) % 2
    sides = jnp.concatenate([mine, 1 - mine])

    rows = window_rows(length)
    offset = ((core * chips + dp) * length) % (BLOCK * D)
    wide = jnp.pad(params, (BLOCK * D, rows * D - length))
    win = lax.dynamic_slice(wide, (BLOCK * D - offset,), (rows * D,)).reshape(rows, D)

    pix, other = pick(pixels, sides, counts, mask)
    shards, far = gather(win, other.reshape(4, ROWS, PIN), chips)
    cot = cotangent[:, 0, 0]
    done, near_grad, total, far_grad = main(
        shards, pix.reshape(4, ROWS, PIN), far, cot, sides, counts, mask, chips, length
    )
    shard_grad = lax.dynamic_slice(total.reshape(rows * D), (offset,), (length,))
    pixel_grad = place(near_grad, far_grad, sides, counts, mask, pixels.shape)
    return (done[:, None, None], pixel_grad, shard_grad)


def solution(mesh):
    return jax.shard_map(
        body,
        mesh=mesh,
        in_specs=(
            P(None, None, "dp", "grp", None, None),
            P(None, None, "dp"),
            P(None, None, "dp", None),
            P(None, "dp"),
            P(("grp", "dp")),
            P(None, "grp", "dp", None, None, None),
        ),
        out_specs=(
            P(None, "grp", "dp", None, None, None),
            P(None, None, "dp", "grp", None, None),
            P(("grp", "dp")),
        ),
        check_vma=False,
    )
```

```python
import functools
import math

import jax
import jax.numpy as jnp
from jax import lax
from jax.experimental import pallas as pl
from jax.experimental.pallas import tpu as pltpu
from jax.sharding import PartitionSpec as P

MESH = pl.DeviceIdType.MESH
F32 = jnp.float32
BF16 = jnp.bfloat16

D = 512
HEADS = 8
HEAD = D // HEADS
FFN = 2048
PIN = 768
P_SIZE = 196
ROWS = 208
MEM = 96
READ = 16
NCOL = MEM + READ
STEPS = 8
BLOCK = 16
EPS = 1e-6
PARTS = 3
HUGE = 1e30
HALF_INT = 1 << 30

ROW_PATCH = 0
ROW_BIAS = 768
ROW_RGAIN = 769
ROW_RHID = 770
ROW_RSCORE = 1282
ROW_AGAIN = 1298
ROW_QKV = 1299
ROW_AOUT = 2835
ROW_FGAIN = 3347
ROW_FIN = 3348
ROW_FOUT = 5396
ROW_WGAIN = 7444
ROW_WHID = 7445
ROW_WSCORE = 7957
ROW_END = 8053

VMEM_LIMIT = 63 * 2**20


def dot(a, b, ca=1, cb=0):
    return lax.dot_general(a, b, (((ca,), (cb,)), ((), ())), preferred_element_type=F32)


def window_rows(length):
    return (length + BLOCK * D - 2) // (BLOCK * D) * BLOCK + BLOCK


def first_block(index, length):
    return (index * length) // (BLOCK * D)


def parts_of(chips, rows):
    bits = chips.bit_length() - 1
    high = list(range(bits - 1, 1, -1))
    blocks = rows // BLOCK
    a, b = (blocks * 3 + 4) // 8 * BLOCK, (blocks * 6 + 4) // 8 * BLOCK
    return [
        (0, a, high + [0, 1], high + [1, 0]),
        (a, b - a, high + [0, 1], high + [1, 0]),
        (b, rows - b, [0, 1] + high, [1, 0] + high),
    ]


def partners(orders, core, me):
    steps = []
    for one, two in zip(*orders):
        a = (1 - 2 * ((me // (1 << one)) % 2)) * (1 << one)
        b = (1 - 2 * ((me // (1 << two)) % 2)) * (1 << two)
        steps.append(a + core * (b - a))
    return steps


def shifted(me, steps, r):
    at = me
    for k, step in enumerate(steps):
        if (r >> k) & 1:
            at = at + step
    return at


def greet(core, me, steps):
    barrier = pltpu.get_barrier_semaphore()
    places = [(core, me + step) for step in steps] + [(1 - core, me)]
    for place in places:
        pl.semaphore_signal(barrier, inc=1, device_id=place, device_id_type=MESH)
    pl.semaphore_wait(barrier, len(places))


def remote(src, dst, s, r, place):
    return pltpu.make_async_remote_copy(
        src_ref=src, dst_ref=dst, send_sem=s, recv_sem=r, device_id=place, device_id_type=MESH
    )


CHUNK = 64
FULL = P_SIZE // CHUNK * CHUNK
TAIL = P_SIZE - FULL


def kept(counts, mask, m, g, half):
    base = half * (STEPS // 2)
    ok = [(mask[m, g, base + i] == 1) & (base + i < counts[m, g]) for i in range(4)]
    last = jnp.int32
    first = jnp.where(ok[0], 0, jnp.where(ok[1], 1, jnp.where(ok[2], 2, 3))).astype(last)
    second = jnp.where(ok[3], 3, jnp.where(ok[2], 2, jnp.where(ok[1], 1, 0))).astype(last)
    number = sum(o.astype(jnp.int32) for o in ok)
    return (first, second), (number > 0, number > 1)


def place_kernel(sides, counts, mask, near, far, out):
    e = pl.program_id(0)
    m = e % 2
    slots, flags = kept(counts, mask, m, sides[e], lax.axis_index("grp"))
    where = [jnp.where(flag, slot, -HALF_INT) for slot, flag in zip(slots, flags)]

    def spread(rows, cols):
        one = [(iota((rows, cols), 0) == 4 * iota((rows, cols), 1) + s).astype(BF16) for s in where]
        return jnp.concatenate(one, 1)

    def to_slots(first, count, weights):
        at = slice(first, first + count)
        these = [jnp.where(e < 2, near[0, 0, j, at], far[0, j, at]) for j in range(2)]
        return dot(weights, jnp.concatenate(these, 0)).astype(BF16)

    whole = spread(4 * CHUNK, CHUNK)
    for c in range(FULL // CHUNK):
        got = to_slots(CHUNK * c, CHUNK, whole)
        out[0, 0, 0, CHUNK * c : CHUNK * c + CHUNK] = got.reshape(CHUNK, 4, PIN)
    got = to_slots(FULL, ROWS - FULL, spread(4 * TAIL, ROWS - FULL))
    out[0, 0, 0, FULL:] = got.reshape(TAIL, 4, PIN)


def place(near, far, sides, counts, mask, shape):
    m, g, c, s, rows, cols = shape
    out = pl.pallas_call(
        place_kernel,
        out_shape=jax.ShapeDtypeStruct((m, g, c, rows, s, cols), BF16),
        grid_spec=pltpu.PrefetchScalarGridSpec(
            num_scalar_prefetch=3,
            grid=(4,),
            in_specs=[
                pl.BlockSpec((1, 1, 2, ROWS, PIN), lambda e, *_: (0, jnp.minimum(e, 1), 0, 0, 0)),
                pl.BlockSpec((1, 2, ROWS, PIN), lambda e, *_: (jnp.maximum(e, 2) - 2, 0, 0, 0)),
            ],
            out_specs=pl.BlockSpec(
                (1, 1, 1, rows, s, cols), lambda e, s, *_: (e % 2, s[e], 0, 0, 0, 0)
            ),
        ),
        compiler_params=pltpu.CompilerParams(vmem_limit_bytes=VMEM_LIMIT),
        name="place",
    )(sides, counts, mask, near.reshape(2, 2, 2, ROWS, PIN), far.reshape(2, 2, ROWS, PIN))
    return jnp.swapaxes(out, 3, 4)


def frame_index(clip, step):
    return (step // 2) * 4 + clip * 2 + step % 2


def norm(x):
    mean = jnp.mean(x, -1, keepdims=True)
    centered = x - mean
    r = lax.rsqrt(jnp.mean(centered * centered, -1, keepdims=True) + EPS)
    return centered * r, r


def norm_back(g, xh, r):
    return r * (g - jnp.mean(g, -1, keepdims=True) - xh * jnp.mean(g * xh, -1, keepdims=True))


def gelu(x):
    cdf = 0.5 + 0.5 * lax.erf(x * math.sqrt(0.5))
    slope = cdf + x * (jnp.exp(-0.5 * x * x) * (1.0 / math.sqrt(2.0 * math.pi)))
    return (x * cdf).astype(BF16), slope.astype(BF16)


def col_sum(x):
    return jnp.sum(x, 0, keepdims=True)


def row_sum(x):
    return jnp.sum(x, -1, keepdims=True)


def row_max(x):
    return jnp.max(x, -1, keepdims=True)


def iota(shape, dim):
    return lax.broadcasted_iota(jnp.int32, shape, dim)


def score_masks(width, part):
    group = 512 // math.gcd(512, width)
    lane = iota((D, D), 1) + 512 * part
    hidden = iota((D, D), 0)
    where = ((hidden % group) == (lane // width)).astype(BF16)
    lane = iota((width, D), 1) + 512 * part
    pick = ((lane % width) == iota((width, D), 0)).astype(BF16)
    rows = 512 // group
    spread = ((iota((D, rows), 0) // group) == iota((D, rows), 1)).astype(BF16)
    return where, pick, spread


def main_kernel(
    chips,
    length,
    sides,
    counts,
    mask,
    own,
    pixels,
    cot,
    done,
    pg,
    total,
    pgout,
    shards,
    flat,
    planes,
    wp,
    wr,
    ww,
    wbig,
    wsr,
    wsw,
    gains,
    xs,
    a_r,
    a_w,
    h_r,
    h_w,
    d_r,
    d_w,
    ps,
    rs,
    stat,
    dsc,
    mem,
    dmem,
    mls,
    mxh,
    mr,
    mnew,
    al_r,
    al_m,
    al_t,
    zs,
    xh1,
    r1,
    us,
    qs,
    prob,
    att,
    xh2,
    r2,
    u2,
    gs,
    dg,
    toks,
    xhk,
    rk,
    dqs,
    dys,
    dpre,
    dos,
    acc_r,
    acc_w,
    vecs,
    pix,
    far,
    stage,
    held,
    stage_sem,
    lay_sem,
    grecv,
    gsibrecv,
    send,
    recv,
    sibsend,
    sibrecv,
    pixsem,
    ready,
):
    rows = own.shape[0]
    frames = 8
    core = lax.axis_index("grp")
    me = lax.axis_index("dp")
    sibling = (1 - core, me)
    parts = parts_of(chips, rows)
    bits = chips.bit_length() - 1
    all_steps = [partners(part[2:], core, me) for part in parts]
    other_steps = [partners(part[2:], 1 - core, me) for part in parts]
    mine = core * chips + me

    def load(m, g):
        return pltpu.make_async_copy(pixels.at[m, g, 0], stage.at[g], stage_sem.at[m, g])

    for g in range(2):
        load(0, g).start()
    greet(core, me, all_steps[0])

    def block_of(index):
        return first_block(index, length) * BLOCK

    def is_outer(index):
        start = block_of(index)
        return (start < ROW_QKV) | (start + rows > ROW_WGAIN)

    def pass_on(p, r, src):
        start, size = parts[p][:2]
        steps = all_steps[p]
        dst = shards.at[core * chips + shifted(me, steps, r), pl.ds(start, size)]
        src = dst if src is None else src.at[pl.ds(start, size)]
        copies = []
        for k in range(bits - 1, r.bit_length() - 1, -1):
            to = (core, me + steps[k])
            copies.append(
                remote(src, dst, send.at[p, (1 << k) - 1 + r], grecv.at[p, r | (1 << k)], to)
            )
        copies.append(remote(src, dst, sibsend.at[p, r], gsibrecv.at[p, r], sibling))
        return copies

    def strip(index, b):
        return held.at[pl.ds(pl.multiple_of(index * 2 * BLOCK + b, BLOCK), BLOCK)]

    def lay(index, src):
        start = pl.multiple_of(block_of(index), BLOCK)
        inner = rows - 2 * BLOCK
        at = flat.at[pl.ds(pl.multiple_of(start + BLOCK, BLOCK), inner)]
        ends = [(0, 0), (rows - BLOCK, BLOCK)]
        copies = [pltpu.make_async_copy(src.at[pl.ds(BLOCK, inner)], at, lay_sem.at[0, index])]
        for k, (a, b) in enumerate(ends):
            copies.append(
                pltpu.make_async_copy(
                    src.at[pl.ds(a, BLOCK)], strip(index, b), lay_sem.at[1 + k, index]
                )
            )
        return copies

    def start_all(copies):
        for copy in copies:
            copy.start()

    def at_distance(c):
        return [r for r in range(chips) if bin(r).count("1") == c]

    def arrive(p, r, outer):
        index = core * chips + shifted(me, all_steps[p], r)

        @pl.when(is_outer(index) == outer)
        def _():
            at = shards.at[index, pl.ds(*parts[p][:2])]
            remote(at, at, send.at[p, 0], grecv.at[p, r], sibling).wait_recv()
            start_all(pass_on(p, r, None))

    def arrive_side(p, r, outer):
        index = (1 - core) * chips + shifted(me, other_steps[p], r)

        @pl.when(is_outer(index) == outer)
        def _():
            at = shards.at[index, pl.ds(*parts[p][:2])]
            remote(at, at, sibsend.at[p, 0], gsibrecv.at[p, r], sibling).wait_recv()

    def lay_down(base, steps, r, outer):
        index = base * chips + shifted(me, steps, r)

        @pl.when(is_outer(index) == outer)
        def _():
            start_all(lay(index, shards.at[index]))

    def taking(outer, c):
        todo = [functools.partial(arrive, p, r, outer) for r in at_distance(c) for p in range(len(parts))]
        return todo + [
            functools.partial(lay_down, core, all_steps[0], r, outer) for r in at_distance(c)
        ]

    def taking_side(outer, c):
        todo = [
            functools.partial(arrive_side, p, r, outer) for r in at_distance(c) for p in range(len(parts))
        ]
        return todo + [
            functools.partial(lay_down, 1 - core, other_steps[0], r, outer) for r in at_distance(c)
        ]

    def run(todo):
        for one in todo:
            one()

    def pick(m):
        chosen = []
        for g in range(2):
            load(m, g).wait()
            kept_slots, _ = kept(counts, mask, m, g, core)
            chosen.append(
                [
                    jnp.concatenate(
                        [
                            (iota((a, b), 1) == 4 * iota((a, b), 0) + one).astype(BF16)
                            for one in kept_slots
                        ],
                        0,
                    )
                    for a, b in ((CHUNK, 4 * CHUNK), (ROWS - FULL, 4 * TAIL))
                ]
            )
        for c in range(FULL // CHUNK + 1):
            first = CHUNK * c
            size = CHUNK if first < FULL else ROWS - FULL
            count = CHUNK if first < FULL else TAIL
            got = [
                dot(
                    chosen[g][0 if first < FULL else 1],
                    stage[g, first : first + count].reshape(4 * count, PIN),
                ).astype(BF16)
                for g in range(2)
            ]
            for j in range(2):
                a, b = (got[g][size * j : size * j + size] for g in range(2))
                pix[2 * m + j, first : first + size] = jnp.where(sides[m] == 0, a, b)
                pg[4 + 2 * m + j, first : first + size] = jnp.where(sides[m] == 0, b, a)

    for p in range(len(parts)):
        start_all(pass_on(p, 0, own))
    start_all(lay(mine, own))
    swap_in = remote(pg.at[pl.ds(4, 4)], far, pixsem.at[2], pixsem.at[3], sibling)
    for c in range(1, bits + 1):
        run(taking(True, c))
        if c <= 2:
            pick(c - 1)
        if c == 1:
            for g in range(2):
                load(1, g).start()
        if c == 2:
            swap_in.start()
        if 2 <= c < bits:
            run(taking(False, c - 1))
        run(taking_side(True, c - 1))
    run(taking_side(True, bits))

    slot_of = []
    flag_of = []
    for b in range(2):
        pairs = [kept(counts, mask, b, sides[b], half) for half in range(2)]
        slot_of.append([pairs[t // 2][0][t % 2] for t in range(4)])
        flag_of.append([pairs[t // 2][1][t % 2] for t in range(4)])

    wo = wbig.at[0:D]
    wqkv = [wbig.at[D + D * j : 2 * D + D * j] for j in range(3)]
    win = [wbig.at[4 * D + D * j : 5 * D + D * j] for j in range(4)]
    wout = wbig.at[8 * D : 12 * D]

    count = 2 * chips
    outer = [bool(is_outer(i)) for i in range(count)]

    def await_rows(i):
        for copy in lay(i, shards.at[i]):
            copy.wait()

    def join(i):
        a, b = block_of(i), block_of(i + 1)
        at = slice(b, b + BLOCK)
        before = strip(i, BLOCK)[...] if b - a == rows - BLOCK else flat[at, :]
        flat[at, :] = before + strip(i + 1, 0)[...]

    def gain(k, row):
        base = row // BLOCK * BLOCK
        gains[k : k + 1, :] = flat[base : base + BLOCK, :].astype(F32)[row - base : row - base + 1, :]

    for i in range(count):
        if outer[i]:
            await_rows(i)
    flat[:BLOCK, :] = strip(0, 0)[...]
    end = block_of(count - 1) + rows
    flat[end - BLOCK : end, :] = strip(count - 1, BLOCK)[...]
    for i in range(count - 1):
        if outer[i] and outer[i + 1]:
            join(i)
    wp[...] = flat[ROW_PATCH : ROW_PATCH + PIN, :]
    wr[...] = flat[ROW_RHID : ROW_RHID + D, :]
    ww[...] = flat[ROW_WHID : ROW_WHID + D, :]
    for k, row in ((0, ROW_BIAS), (1, ROW_RGAIN), (2, ROW_AGAIN), (4, ROW_WGAIN)):
        gain(k, row)
    where, chosen, spread = score_masks(READ, 0)
    wide = dot(spread, flat[ROW_RSCORE : ROW_RSCORE + READ, :]).astype(BF16) * where
    wsr[...] = dot(chosen, wide, 1, 1).astype(BF16)
    scores = jnp.zeros((MEM, D), F32)
    for c in range(4):
        at = slice(c * 128, c * 128 + 128)
        planes[c, :MEM, :] = flat[ROW_WSCORE : ROW_WSCORE + MEM, at].astype(F32)
    for part in range(3):
        where, chosen, spread = score_masks(MEM, part)
        these = jnp.concatenate(
            [planes[c, pl.ds(part, 32, stride=3), :] for c in range(4)], -1
        ).astype(BF16)
        wide = dot(spread, these).astype(BF16) * where
        scores = scores + dot(chosen, wide, 1, 1)
    wsw[...] = scores.astype(BF16)

    def assemble():
        for i in range(count):
            if not outer[i]:
                await_rows(i)
        for i in range(count - 1):
            if not (outer[i] and outer[i + 1]):
                join(i)
        gain(3, ROW_FGAIN)
        wo[...] = flat[ROW_AOUT : ROW_AOUT + D, :]
        wout[...] = flat[ROW_FOUT : ROW_FOUT + FFN, :]
        for row, count_j, dst in ((ROW_QKV, 3, wqkv), (ROW_FIN, 4, win)):
            for q in range(4):
                base = row + count_j * 128 * q
                for c in range(4):
                    at = slice(c * 128, c * 128 + 128)
                    planes[c, : count_j * 128, :] = flat[base : base + count_j * 128, at].astype(F32)
                    for j in range(count_j):
                        these = planes[c, pl.ds(j, 128, stride=count_j), :]
                        dst[j][128 * q : 128 * q + 128, at] = these.astype(BF16)

    bias = gains[0:1, :]
    g_read = gains[1:2, :]
    g_attn = gains[2:3, :]
    g_write = gains[4:5, :]

    lanes = iota((NCOL, ROWS), 1) < P_SIZE

    def frame_forward(f):
        at = slice(f * ROWS, f * ROWS + ROWS)
        seen = jnp.where(f // 4 == core, pix[f % 4], far[f % 4])
        x = (dot(seen, wp[...]) + bias).astype(BF16)
        xs[f] = x
        xh, r = norm(x.astype(F32))
        a_r[at, :] = (xh * g_read).astype(BF16)
        a_w[at, :] = (xh * g_write).astype(BF16)
        h, d = gelu(dot(a_r[at, :], wr[...]))
        h_r[at, :] = h
        d_r[at, :] = d
        s_read = dot(wsr[...], h, 1, 1)
        h, d = gelu(dot(a_w[at, :], ww[...]))
        h_w[at, :] = h
        d_w[at, :] = d
        s_write = dot(wsw[...], h, 1, 1)
        scores = jnp.where(lanes, jnp.concatenate([s_write, s_read], 0), -HUGE)
        best = row_max(scores)
        p = jnp.exp(scores - best)
        pb = p.astype(BF16)
        ps[f] = pb
        stat[f, :, 0:1] = best
        stat[f, :, 1:2] = row_sum(p)
        rs[f] = dot(pb, x)

    swap_in.wait()
    todo = taking(False, bits - 1)
    for c in range(bits - 1):
        todo += taking_side(False, c)
    todo += taking(False, bits)
    for c in range(bits - 1, bits + 1):
        todo += taking_side(False, c)
    every = len(todo) // frames
    for i, one in enumerate(todo):
        if i % every == 0 and i // every < frames:
            frame_forward(i // every)
        one()
    assemble()
    g_ffn = gains[3:4, :]

    mem[...] = jnp.zeros(mem.shape, F32)
    head_of = [(iota((1, D), 1) // HEAD == h) for h in range(HEADS)]
    same_clip = ((iota((HEADS * 32, 32), 0) // READ) % 2) == (iota((HEADS * 32, 32), 1) // READ)
    zero = jnp.zeros((), F32)

    def by_head(x):
        return jnp.concatenate([jnp.where(m, x, jnp.zeros_like(x)) for m in head_of], 0)

    def from_heads(x):
        total = jnp.where(head_of[0], x[:32], zero)
        for h in range(1, HEADS):
            total = total + jnp.where(head_of[h], x[32 * h : 32 * h + 32], zero)
        return total

    base_r = frames * ROWS
    base_w = frames * ROWS
    base_k = base_w + 2 * 192

    def step_forward(t):
        live = t > 0
        last = t == 3
        if live:
            ml = mem[...].astype(BF16)
            mls[t - 1] = ml
            xh, r = norm(ml.astype(F32))
            mxh[t - 1] = xh
            mr[t - 1] = r
            at = slice(base_r + (t - 1) * 192, base_r + t * 192)
            a = (xh * g_read).astype(BF16)
            a_r[at, :] = a
            h, d = gelu(dot(a, wr[...]))
            h_r[at, :] = h
            d_r[at, :] = d
            if not last:
                a = (xh * g_write).astype(BF16)
                a_w[at, :] = a
                hw, d = gelu(dot(a, ww[...]))
                h_w[at, :] = hw
                d_w[at, :] = d
        z_parts = []
        for b in range(2):
            f = frame_index(b, t)
            m_f = stat[f, MEM:, 0:1]
            if live:
                s = dot(wsr[...], h[96 * b : 96 * b + 96], 1, 1)
                best = jnp.maximum(row_max(s), m_f)
                e = jnp.exp(s - best)
                part = row_sum(e)
            else:
                best = jnp.maximum(m_f, 0.0)
                part = MEM * jnp.exp(-best)
            w = jnp.exp(m_f - best)
            inv = 1.0 / (part + w * stat[f, MEM:, 1:2])
            stat[f, MEM:, 2:3] = w * inv
            z = (w * inv) * rs[f, MEM:, :]
            if live:
                al = (e * inv).astype(BF16)
                al_r[t - 1, b] = al
                z = z + dot(al, ml[96 * b : 96 * b + 96])
            z_parts.append(z)
        z = jnp.concatenate(z_parts, 0)
        zs[t] = z
        at = slice(32 * t, 32 * t + 32)
        xh, r = norm(z)
        xh1[t] = xh
        r1[t] = r
        u = (xh * g_attn).astype(BF16)
        us[at, :] = u
        q = dot(u, wqkv[0][...]).astype(BF16)
        k = dot(u, wqkv[1][...]).astype(BF16)
        v = dot(u, wqkv[2][...]).astype(BF16)
        qs[0, t] = q
        qs[1, t] = k
        qs[2, t] = v
        s = jnp.where(same_clip, dot(by_head(q), k, 1, 1) * (1.0 / math.sqrt(HEAD)), -HUGE)
        e = jnp.exp(s - row_max(s))
        p = (e / row_sum(e)).astype(BF16)
        prob[t] = p
        joined = from_heads(dot(p, v)).astype(BF16)
        att[at, :] = joined
        y = z + dot(joined, wo[...])
        xh, r = norm(y)
        xh2[t] = xh
        r2[t] = r
        n = (xh * g_ffn).astype(BF16)
        u2[at, :] = n
        o = y
        for j in range(4):
            g, d = gelu(dot(n, win[j][...]))
            gs[at, D * j : D * j + D] = g
            dg[t, :, D * j : D * j + D] = d
            o = o + dot(g, wout[D * j : D * j + D, :])
        tok = o.astype(BF16)
        toks[t] = tok
        if last:
            return
        xh, r = norm(tok.astype(F32))
        xhk[t] = xh
        rk[t] = r
        a = (xh * g_write).astype(BF16)
        at = slice(base_k + 32 * t, base_k + 32 * t + 32)
        a_w[at, :] = a
        hk, d = gelu(dot(a, ww[...]))
        h_w[at, :] = hk
        d_w[at, :] = d
        for b in range(2):
            f = frame_index(b, t)
            m_f = stat[f, :MEM, 0:1]
            s_tok = dot(wsw[...], hk[16 * b : 16 * b + 16], 1, 1)
            best = jnp.maximum(row_max(s_tok), m_f)
            if live:
                s = dot(wsw[...], hw[96 * b : 96 * b + 96], 1, 1)
                best = jnp.maximum(best, row_max(s))
                e = jnp.exp(s - best)
                part = row_sum(e)
            else:
                best = jnp.maximum(best, 0.0)
                part = MEM * jnp.exp(-best)
            e_tok = jnp.exp(s_tok - best)
            w = jnp.exp(m_f - best)
            inv = 1.0 / (part + row_sum(e_tok) + w * stat[f, :MEM, 1:2])
            stat[f, :MEM, 2:3] = w * inv
            al = (e_tok * inv).astype(BF16)
            al_t[t, b] = al
            new = (w * inv) * rs[f, :MEM, :] + dot(al, tok[16 * b : 16 * b + 16])
            if live:
                al = (e * inv).astype(BF16)
                al_m[t - 1, b] = al
                new = new + dot(al, ml[96 * b : 96 * b + 96])
            mnew[t, b] = new
            old = mem[96 * b : 96 * b + 96, :]
            mem[96 * b : 96 * b + 96, :] = jnp.where(flag_of[b][t], new, old)

    for t in range(4):
        step_forward(t)

    vecs[...] = jnp.zeros(vecs.shape, F32)
    acc_r[...] = jnp.zeros(acc_r.shape, F32)
    acc_w[...] = jnp.zeros(acc_w.shape, F32)
    dmem[...] = jnp.zeros(dmem.shape, F32)

    def add_vec(k, x):
        vecs[k : k + 1, :] = vecs[k : k + 1, :] + x

    def step_backward(t):
        live = t > 0
        last = t == 3
        gates = [jnp.where(flag_of[b][t], 1.0, 0.0) for b in range(2)]
        d_out = []
        for b in range(2):
            base = 4 * (t // 2)
            given = cot[b, base + 3]
            for i in range(3):
                given = jnp.where(slot_of[b][t] == i, cot[b, base + i], given)
            d_out.append(given.astype(F32) * gates[b])
        d_ml = []
        dh_mem = []
        keeps = []
        if last:
            for b in range(2):
                f = frame_index(b, t)
                dsc[f, :MEM, :] = jnp.zeros((MEM, D), BF16)
                stat[f, :MEM, 2:3] = jnp.zeros((MEM, 1), F32)
                stat[f, :MEM, 3:4] = jnp.zeros((MEM, 1), F32)
                keeps.append(jnp.zeros((96, D), F32))
                d_ml.append(keeps[b])
        else:
            dh_tok = []
            at_k = slice(base_k + 32 * t, base_k + 32 * t + 32)
            hk = h_w[at_k, :]
            tok = toks[t]
            for b in range(2):
                f = frame_index(b, t)
                down = dmem[96 * b : 96 * b + 96, :]
                ds = (down * gates[b]).astype(BF16)
                keeps.append(down * (1.0 - gates[b]))
                dsc[f, :MEM, :] = ds
                c = row_sum(ds.astype(F32) * mnew[t, b])
                stat[f, :MEM, 3:4] = c
                al = al_t[t, b]
                rows_b = slice(16 * b, 16 * b + 16)
                d_out[b] = d_out[b] + dot(al, ds, 0, 0)
                back = (al.astype(F32) * (dot(ds, tok[rows_b], 1, 1) - c)).astype(BF16)
                dh_tok.append(dot(back, wsw[...], 0, 0))
                acc = dot(back, hk[rows_b])
                if live:
                    rows_b = slice(96 * b, 96 * b + 96)
                    ml = mls[t - 1, rows_b, :]
                    al = al_m[t - 1, b]
                    d_ml.append(dot(al, ds, 0, 0))
                    back = (al.astype(F32) * (dot(ds, ml, 1, 1) - c)).astype(BF16)
                    dh_mem.append(dot(back, wsw[...], 0, 0))
                    at = slice(base_w + (t - 1) * 192 + 96 * b, base_w + (t - 1) * 192 + 96 * b + 96)
                    acc = acc + dot(back, h_w[at, :])
                acc_w[...] = acc_w[...] + acc
            dgk = (jnp.concatenate(dh_tok, 0) * d_w[at_k, :].astype(F32)).astype(BF16)
            d_w[at_k, :] = dgk
            da = dot(dgk, ww[...], 1, 1)
            xh = xhk[t]
            add_vec(4, col_sum(da * xh))
            dx = norm_back(da * g_write, xh, rk[t])
            for b in range(2):
                d_out[b] = d_out[b] + dx[16 * b : 16 * b + 16]
        at = slice(32 * t, 32 * t + 32)
        do = jnp.concatenate(d_out, 0)
        dob = do.astype(BF16)
        dos[at, :] = dob
        dn = jnp.zeros((32, D), F32)
        for j in range(4):
            sl = slice(D * j, D * j + D)
            dp = (dot(dob, wout[sl, :], 1, 1) * dg[t, :, sl].astype(F32)).astype(BF16)
            dpre[at, sl] = dp
            dn = dn + dot(dp, win[j][...], 1, 1)
        add_vec(3, col_sum(dn * xh2[t]))
        dy = do + norm_back(dn * g_ffn, xh2[t], r2[t])
        dyb = dy.astype(BF16)
        dys[at, :] = dyb
        dbig = by_head(dot(dyb, wo[...], 1, 1).astype(BF16))
        p = prob[t]
        q, k, v = qs[0, t], qs[1, t], qs[2, t]
        dp = dot(dbig, v, 1, 1)
        pf = p.astype(F32)
        ds = (pf * (dp - row_sum(dp * pf)) * (1.0 / math.sqrt(HEAD))).astype(BF16)
        dv = dot(p, dbig, 0, 0).astype(BF16)
        dq = from_heads(dot(ds, k)).astype(BF16)
        dk = dot(ds, by_head(q), 0, 0).astype(BF16)
        dqs[0, at, :] = dq
        dqs[1, at, :] = dk
        dqs[2, at, :] = dv
        du = dot(dq, wqkv[0][...], 1, 1) + dot(dk, wqkv[1][...], 1, 1) + dot(dv, wqkv[2][...], 1, 1)
        add_vec(2, col_sum(du * xh1[t]))
        dz = dy + norm_back(du * g_attn, xh1[t], r1[t])
        dzb = dz.astype(BF16)
        c_all = row_sum(dzb.astype(F32) * zs[t])
        dh_r = []
        for b in range(2):
            f = frame_index(b, t)
            ds = dzb[16 * b : 16 * b + 16]
            c = c_all[16 * b : 16 * b + 16]
            dsc[f, MEM:, :] = ds
            stat[f, MEM:, 3:4] = c
            if live:
                rows_b = slice(96 * b, 96 * b + 96)
                al = al_r[t - 1, b]
                d_ml[b] = d_ml[b] + dot(al, ds, 0, 0)
                back = (al.astype(F32) * (dot(ds, mls[t - 1, rows_b, :], 1, 1) - c)).astype(BF16)
                dh_r.append(dot(back, wsr[...], 0, 0))
                at_b = slice(base_r + (t - 1) * 192 + 96 * b, base_r + (t - 1) * 192 + 96 * b + 96)
                acc_r[...] = acc_r[...] + dot(back, h_r[at_b, :])
        if not live:
            return
        at_m = slice(base_r + (t - 1) * 192, base_r + t * 192)
        xh = mxh[t - 1]
        dgr = (jnp.concatenate(dh_r, 0) * d_r[at_m, :].astype(F32)).astype(BF16)
        d_r[at_m, :] = dgr
        da = dot(dgr, wr[...], 1, 1)
        add_vec(1, col_sum(da * xh))
        g = da * g_read
        if not last:
            dgw = (jnp.concatenate(dh_mem, 0) * d_w[at_m, :].astype(F32)).astype(BF16)
            d_w[at_m, :] = dgw
            da = dot(dgw, ww[...], 1, 1)
            add_vec(4, col_sum(da * xh))
            g = g + da * g_write
        dx = norm_back(g, xh, mr[t - 1])
        for b in range(2):
            rows_b = slice(96 * b, 96 * b + 96)
            dmem[rows_b, :] = keeps[b] + d_ml[b] + dx[rows_b]

    for t in range(3, -1, -1):
        step_backward(t)

    for other in [sibling] + [(core, me + step) for step in all_steps[0]]:
        pl.semaphore_signal(ready, inc=1, device_id=other, device_id_type=MESH)
    flat[ROW_AOUT : ROW_AOUT + D, :] = dot(att[...], dys[...], 0, 0).astype(BF16)
    for j in range(4):
        sl = slice(D * j, D * j + D)
        flat[ROW_FOUT + D * j : ROW_FOUT + D * j + D, :] = dot(gs[:, sl], dos[...], 0, 0).astype(BF16)
    for row, count, left, right in (
        (ROW_QKV, 3, us, lambda j: dqs[j]),
        (ROW_FIN, 4, u2, lambda j: dpre[:, D * j : D * j + D]),
    ):
        for q in range(4):
            for j in range(count):
                part = dot(left[:, 128 * q : 128 * q + 128], right(j), 0, 0)
                for c in range(4):
                    planes[c, pl.ds(j, 128, stride=count), :] = part[:, 128 * c : 128 * c + 128]
            base = row + count * 128 * q
            for c in range(4):
                at = slice(128 * c, 128 * c + 128)
                flat[base : base + count * 128, at] = planes[c, : count * 128, :].astype(BF16)
    flat[ROW_AGAIN : ROW_AGAIN + 1, :] = vecs[2:3, :].astype(BF16)
    flat[ROW_FGAIN : ROW_FGAIN + 1, :] = vecs[3:4, :].astype(BF16)

    def place_of(p, r):
        start, size = parts[p][:2]
        return chips * start + r * size

    def side(p, r):
        return wbig.at[pl.ds(place_of(p, r), parts[p][1])]

    def slot(p, k, r):
        start, size = parts[p][:2]
        return (chips - 1) * start + ((1 << k) - 1 + r) * size

    def turns(top, end):
        return [(p, r) for r in range(top - 1, end - 1, -1) for p in range(len(parts))]


    def swap(p, r):
        index = (1 - core) * chips + shifted(me, other_steps[p], r)
        start = pl.multiple_of(block_of(index) + parts[p][0], BLOCK)
        src = flat.at[pl.ds(start, parts[p][1])]
        return remote(src, side(p, r), sibsend.at[p, r], sibrecv.at[p, r], sibling), index

    def send_on(p, r):
        top = r.bit_length() - 1
        low = r - (1 << top)
        return remote(
            side(p, r),
            held.at[pl.ds(slot(p, top, low), parts[p][1])],
            send.at[p, r],
            recv.at[p, (1 << top) - 1 + low],
            (core, me + all_steps[p][top]),
        )

    def swap_all(late):
        for p, r in turns(chips, 0):
            copy, index = swap(p, r)

            @pl.when(is_outer(index) == late)
            def _(copy=copy):
                copy.start()

    def turn(p, r, late):
        index = core * chips + shifted(me, all_steps[p], r)
        start, size = parts[p][:2]

        @pl.when(is_outer(index) == late)
        def _():
            swap(p, r)[0].wait_recv()
            slots = []
            for k in range(bits - 1, r.bit_length() - 1, -1):
                at = held.at[pl.ds(slot(p, k, r), size)]
                remote(at, at, send.at[p, r], recv.at[p, (1 << k) - 1 + r], sibling).wait_recv()
                slots.append(slot(p, k, r))
            base = block_of(index) + start

            def add(i, carry):
                step = i * BLOCK
                at = pl.ds(pl.multiple_of(place_of(p, r) + step, BLOCK), BLOCK)
                mine = flat[pl.ds(pl.multiple_of(base + step, BLOCK), BLOCK), :]
                value = mine.astype(F32) + wbig[at, :].astype(F32)
                for one in slots:
                    value = value + held[pl.ds(pl.multiple_of(one + step, BLOCK), BLOCK), :].astype(F32)
                if r == 0:
                    total[pl.ds(pl.multiple_of(start + step, BLOCK), BLOCK), :] = value
                else:
                    wbig[at, :] = value.astype(BF16)
                return carry

            lax.fori_loop(0, size // BLOCK, add, 0)
            if r > 0:
                send_on(p, r).start()

    def frame_backward(f):
        at = slice(f * ROWS, f * ROWS + ROWS)
        x = xs[f]
        ds = dsc[f]
        al = ps[f].astype(F32) * stat[f, :, 2:3]
        alb = al.astype(BF16)
        back = (al * (dot(ds, x, 1, 1) - stat[f, :, 3:4])).astype(BF16)
        acc_w[...] = acc_w[...] + dot(back[:MEM], h_w[at, :])
        acc_r[...] = acc_r[...] + dot(back[MEM:], h_r[at, :])
        xh, r = norm(x.astype(F32))
        dgr = (dot(back[MEM:], wsr[...], 0, 0) * d_r[at, :].astype(F32)).astype(BF16)
        d_r[at, :] = dgr
        da = dot(dgr, wr[...], 1, 1)
        add_vec(1, col_sum(da * xh))
        g = da * g_read
        dgw = (dot(back[:MEM], wsw[...], 0, 0) * d_w[at, :].astype(F32)).astype(BF16)
        d_w[at, :] = dgw
        da = dot(dgw, ww[...], 1, 1)
        add_vec(4, col_sum(da * xh))
        g = g + da * g_write
        dx = (dot(alb, ds, 0, 0) + norm_back(g, xh, r)).astype(BF16)
        xs[f] = dx
        add_vec(0, col_sum(dx.astype(F32)))
        to = jnp.where(core == f // 4, 0, 4) + f % 4
        pg[to] = dot(dx, wp[...], 1, 1).astype(BF16)

    for p, r in turns(chips, 0):
        for copy in pass_on(p, r, None):
            copy.wait_send()
    pl.semaphore_wait(ready, bits + 1)
    swap_all(False)
    half, quarter = chips // 2, chips // 4
    for first, todo in ((0, turns(chips, half)), (4, turns(half, quarter))):
        every = len(todo) // 4
        for i, (p, r) in enumerate(todo):
            if i % every == 0 and i // every < 4:
                frame_backward(first + i // every)
            turn(p, r, False)

    swap_pix = remote(pg.at[pl.ds(4, 4)], pgout, pixsem.at[0], pixsem.at[1], sibling)
    swap_pix.start()
    n = 4 * ROWS
    flat[ROW_PATCH : ROW_PATCH + PIN, :] = (
        dot(pix[...].reshape(n, PIN), xs[pl.ds(4 * core, 4)].reshape(n, D), 0, 0)
        + dot(far[...].reshape(n, PIN), xs[pl.ds(4 - 4 * core, 4)].reshape(n, D), 0, 0)
    ).astype(BF16)
    flat[ROW_RHID : ROW_RHID + D, :] = dot(a_r[...], d_r[...], 0, 0).astype(BF16)
    flat[ROW_WHID : ROW_WHID + D, :] = dot(a_w[...], d_w[...], 0, 0).astype(BF16)
    where, chosen, spread = score_masks(READ, 0)
    wide = dot(acc_r[...].astype(BF16), chosen, 0, 0).astype(BF16) * where
    flat[ROW_RSCORE : ROW_RSCORE + READ, :] = dot(spread, wide, 0, 0).astype(BF16)
    for part in range(3):
        where, chosen, spread = score_masks(MEM, part)
        wide = dot(acc_w[...].astype(BF16), chosen, 0, 0).astype(BF16) * where
        these = dot(spread, wide, 0, 0)
        for c in range(4):
            planes[c, pl.ds(part, 32, stride=3), :] = these[:, 128 * c : 128 * c + 128]
    for c in range(4):
        at = slice(128 * c, 128 * c + 128)
        flat[ROW_WSCORE : ROW_WSCORE + MEM, at] = planes[c, :MEM, :].astype(BF16)
    for k, row in ((0, ROW_BIAS), (1, ROW_RGAIN), (4, ROW_WGAIN)):
        flat[row : row + 1, :] = vecs[k : k + 1, :].astype(BF16)
    flat[ROW_END:, :] = jnp.zeros((flat.shape[0] - ROW_END, D), BF16)

    swap_all(True)
    for b in range(2):
        for s in range(STEPS):
            value = jnp.zeros((READ, D), BF16)
            for t in (s // 4 * 2, s // 4 * 2 + 1):
                hit = (slot_of[b][t] == s % 4) & flag_of[b][t]
                value = jnp.where(hit, toks[t, READ * b : READ * b + READ, :], value)
            done[b, s] = value
    for p, r in turns(chips, half):
        turn(p, r, True)
    early = turns(quarter, 0)
    for i, (p, r) in enumerate(turns(half, quarter)):
        if i < len(early):
            turn(*early[i], False)
        turn(p, r, True)
    for p, r in early:
        turn(p, r, True)
    for p, r in turns(chips, 0):
        swap(p, r)[0].wait_send()
        if r > 0:
            send_on(p, r).wait_send()
    swap_pix.wait()


def main(own, pixels, cot, sides, counts, mask, chips, length):
    rows = own.shape[0]
    height = (2 * chips - 1) * length // (BLOCK * D) * BLOCK + rows
    n = 8 * ROWS
    vmem = pl.BlockSpec(memory_space=pltpu.VMEM)
    smem = pl.BlockSpec(memory_space=pltpu.SMEM)
    hbm = pl.BlockSpec(memory_space=pl.ANY)
    v = pltpu.VMEM
    dma = pltpu.SemaphoreType.DMA
    return pl.pallas_call(
        functools.partial(main_kernel, chips, length),
        out_shape=(
            jax.ShapeDtypeStruct((2, STEPS, READ, D), BF16),
            jax.ShapeDtypeStruct((8, ROWS, PIN), BF16),
            jax.ShapeDtypeStruct((rows, D), F32),
            jax.ShapeDtypeStruct((4, ROWS, PIN), BF16),
            jax.ShapeDtypeStruct((2 * chips, rows, D), BF16),
        ),
        in_specs=[smem, smem, smem, vmem, hbm, vmem],
        out_specs=[vmem, vmem, vmem, hbm, hbm],
        scratch_shapes=[
            v((height, D), BF16),
            v((4, D, 128), F32),
            v((PIN, D), BF16),
            v((D, D), BF16),
            v((D, D), BF16),
            v((max(12 * D, chips * rows), D), BF16),
            v((READ, D), BF16),
            v((MEM, D), BF16),
            v((8, D), F32),
            v((8, ROWS, D), BF16),
            v((n + 576, D), BF16),
            v((n + 480, D), BF16),
            v((n + 576, D), BF16),
            v((n + 480, D), BF16),
            v((n + 576, D), BF16),
            v((n + 480, D), BF16),
            v((8, NCOL, ROWS), BF16),
            v((8, NCOL, D), F32),
            v((8, NCOL, 8), F32),
            v((8, NCOL, D), BF16),
            v((192, D), F32),
            v((192, D), F32),
            v((3, 192, D), BF16),
            v((3, 192, D), F32),
            v((3, 192, 1), F32),
            v((3, 2, MEM, D), F32),
            v((3, 2, READ, MEM), BF16),
            v((2, 2, MEM, MEM), BF16),
            v((3, 2, MEM, READ), BF16),
            v((4, 32, D), F32),
            v((4, 32, D), F32),
            v((4, 32, 1), F32),
            v((128, D), BF16),
            v((3, 4, 32, D), BF16),
            v((4, HEADS * 32, 32), BF16),
            v((128, D), BF16),
            v((4, 32, D), F32),
            v((4, 32, 1), F32),
            v((128, D), BF16),
            v((128, FFN), BF16),
            v((4, 32, FFN), BF16),
            v((4, 32, D), BF16),
            v((3, 32, D), F32),
            v((3, 32, 1), F32),
            v((3, 128, D), BF16),
            v((128, D), BF16),
            v((128, FFN), BF16),
            v((128, D), BF16),
            v((READ, D), F32),
            v((MEM, D), F32),
            v((8, D), F32),
            v((4, ROWS, PIN), BF16),
            v((4, ROWS, PIN), BF16),
            v((2, P_SIZE, 4, PIN), BF16),
            v((max((chips - 1) * rows, 4 * chips * BLOCK), D), BF16),
            dma((2, 2)),
            dma((3, 2 * chips)),
            dma((PARTS, chips)),
            dma((PARTS, chips)),
            dma((PARTS, chips)),
            dma((PARTS, chips)),
            dma((PARTS, chips)),
            dma((PARTS, chips)),
            dma((4,)),
            pltpu.SemaphoreType.REGULAR,
        ],
        compiler_params=pltpu.CompilerParams(
            collective_id=0, has_side_effects=True, vmem_limit_bytes=VMEM_LIMIT
        ),
        name="model",
    )(sides, counts, mask, own, pixels, cot)


def body(pixels, counts, step_mask, owner, params, cotangent):
    chips = lax.axis_size("dp")
    length = params.shape[0]
    core = lax.axis_index("grp").astype(jnp.int32)
    dp = lax.axis_index("dp").astype(jnp.int32)
    counts = counts[:, :, 0]
    mask = step_mask[:, :, 0]
    mine = (core + owner[:, 0]) % 2
    sides = jnp.concatenate([mine, 1 - mine])

    rows = window_rows(length)
    offset = ((core * chips + dp) * length) % (BLOCK * D)
    wide = jnp.pad(params, (BLOCK * D, rows * D - length))
    win = lax.dynamic_slice(wide, (BLOCK * D - offset,), (rows * D,)).reshape(rows, D)

    cot = cotangent[:, 0, 0]
    done, near_grad, total, far_grad, _ = main(
        win, jnp.swapaxes(pixels, 3, 4), cot, sides, counts, mask, chips, length
    )
    shard_grad = lax.dynamic_slice(total.reshape(rows * D), (offset,), (length,))
    pixel_grad = place(near_grad, far_grad, sides, counts, mask, pixels.shape)
    return (done[:, None, None], pixel_grad, shard_grad)


def solution(mesh):
    return jax.shard_map(
        body,
        mesh=mesh,
        in_specs=(
            P(None, None, "dp", "grp", None, None),
            P(None, None, "dp"),
            P(None, None, "dp", None),
            P(None, "dp"),
            P(("grp", "dp")),
            P(None, "grp", "dp", None, None, None),
        ),
        out_specs=(
            P(None, "grp", "dp", None, None, None),
            P(None, None, "dp", "grp", None, None),
            P(("grp", "dp")),
        ),
        check_vma=False,
    )
```

```python
import functools
import math

import jax
import jax.numpy as jnp
from jax import lax
from jax.experimental import pallas as pl
from jax.experimental.pallas import tpu as pltpu
from jax.sharding import PartitionSpec as P

MESH = pl.DeviceIdType.MESH
F32 = jnp.float32
BF16 = jnp.bfloat16

D = 512
HEADS = 8
HEAD = D // HEADS
FFN = 2048
PIN = 768
P_SIZE = 196
ROWS = 208
MEM = 96
READ = 16
NCOL = MEM + READ
STEPS = 8
BLOCK = 16
EPS = 1e-6
PARTS = 3
HUGE = 1e30
HALF_INT = 1 << 30

ROW_PATCH = 0
ROW_BIAS = 768
ROW_RGAIN = 769
ROW_RHID = 770
ROW_RSCORE = 1282
ROW_AGAIN = 1298
ROW_QKV = 1299
ROW_AOUT = 2835
ROW_FGAIN = 3347
ROW_FIN = 3348
ROW_FOUT = 5396
ROW_WGAIN = 7444
ROW_WHID = 7445
ROW_WSCORE = 7957
ROW_END = 8053

VMEM_LIMIT = 63 * 2**20


def dot(a, b, ca=1, cb=0):
    return lax.dot_general(a, b, (((ca,), (cb,)), ((), ())), preferred_element_type=F32)


def window_rows(length):
    return (length + BLOCK * D - 2) // (BLOCK * D) * BLOCK + BLOCK


def first_block(index, length):
    return (index * length) // (BLOCK * D)


def parts_of(chips, rows):
    bits = chips.bit_length() - 1
    high = list(range(bits - 1, 1, -1))
    blocks = rows // BLOCK
    b = (blocks * 6 + 4) // 8 * BLOCK
    return [
        (0, b, high + [0, 1], high + [1, 0]),
        (b, rows - b, [0, 1] + high, [1, 0] + high),
    ]


def partners(orders, core, me):
    steps = []
    for one, two in zip(*orders):
        a = (1 - 2 * ((me // (1 << one)) % 2)) * (1 << one)
        b = (1 - 2 * ((me // (1 << two)) % 2)) * (1 << two)
        steps.append(a + core * (b - a))
    return steps


def shifted(me, steps, r):
    at = me
    for k, step in enumerate(steps):
        if (r >> k) & 1:
            at = at + step
    return at


def greet(core, me, steps):
    barrier = pltpu.get_barrier_semaphore()
    places = [(core, me + step) for step in steps] + [(1 - core, me)]
    for place in places:
        pl.semaphore_signal(barrier, inc=1, device_id=place, device_id_type=MESH)
    pl.semaphore_wait(barrier, len(places))


def remote(src, dst, s, r, place):
    return pltpu.make_async_remote_copy(
        src_ref=src, dst_ref=dst, send_sem=s, recv_sem=r, device_id=place, device_id_type=MESH
    )


CHUNK = 64
FULL = P_SIZE // CHUNK * CHUNK
TAIL = P_SIZE - FULL


def kept(counts, mask, m, g, half):
    base = half * (STEPS // 2)
    ok = [(mask[m, g, base + i] == 1) & (base + i < counts[m, g]) for i in range(4)]
    last = jnp.int32
    first = jnp.where(ok[0], 0, jnp.where(ok[1], 1, jnp.where(ok[2], 2, 3))).astype(last)
    second = jnp.where(ok[3], 3, jnp.where(ok[2], 2, jnp.where(ok[1], 1, 0))).astype(last)
    number = sum(o.astype(jnp.int32) for o in ok)
    return (first, second), (number > 0, number > 1)


def place_kernel(owner, counts, mask, near, far, out):
    m, g = pl.program_id(0), pl.program_id(1)
    core = lax.axis_index("grp")
    is_near = (core + owner[m]) % 2 == g
    slots, flags = kept(counts, mask, m, g, core)
    where = [jnp.where(flag, slot, -HALF_INT) for slot, flag in zip(slots, flags)]

    def spread(rows, cols):
        one = [(iota((rows, cols), 0) == 4 * iota((rows, cols), 1) + s).astype(BF16) for s in where]
        return jnp.concatenate(one, 1)

    def to_slots(first, count, weights):
        at = slice(first, first + count)
        these = [jnp.where(is_near, near[0, j, at], far[0, j, at]) for j in range(2)]
        return dot(weights, jnp.concatenate(these, 0)).astype(BF16)

    whole = spread(4 * CHUNK, CHUNK)
    for c in range(FULL // CHUNK):
        got = to_slots(CHUNK * c, CHUNK, whole)
        out[0, 0, 0, CHUNK * c : CHUNK * c + CHUNK] = got.reshape(CHUNK, 4, PIN)
    got = to_slots(FULL, ROWS - FULL, spread(4 * TAIL, ROWS - FULL))
    out[0, 0, 0, FULL:] = got.reshape(TAIL, 4, PIN)


def place(near, far, owner, counts, mask, shape):
    m, g, c, s, rows, cols = shape
    out = pl.pallas_call(
        place_kernel,
        out_shape=jax.ShapeDtypeStruct((m, g, c, rows, s, cols), BF16),
        grid_spec=pltpu.PrefetchScalarGridSpec(
            num_scalar_prefetch=3,
            grid=(2, 2),
            in_specs=[pl.BlockSpec((1, 2, ROWS, PIN), lambda m, g, *_: (m, 0, 0, 0))] * 2,
            out_specs=pl.BlockSpec(
                (1, 1, 1, rows, s, cols), lambda m, g, *_: (m, g, 0, 0, 0, 0)
            ),
        ),
        compiler_params=pltpu.CompilerParams(vmem_limit_bytes=VMEM_LIMIT),
        name="place",
    )(owner, counts, mask, near.reshape(4, 2, ROWS, PIN), far.reshape(2, 2, ROWS, PIN))
    return jnp.swapaxes(out, 3, 4)


def frame_index(clip, step):
    return (step // 2) * 4 + clip * 2 + step % 2


WRITES = sorted(frame_index(clip, step) for clip in range(2) for step in range(3))


def norm(x):
    mean = jnp.mean(x, -1, keepdims=True)
    centered = x - mean
    r = lax.rsqrt(jnp.mean(centered * centered, -1, keepdims=True) + EPS)
    return centered * r, r


def norm_back(g, xh, r):
    return r * (g - jnp.mean(g, -1, keepdims=True) - xh * jnp.mean(g * xh, -1, keepdims=True))


def gelu(x):
    cdf = 0.5 + 0.5 * lax.erf(x * math.sqrt(0.5))
    slope = cdf + x * (jnp.exp(-0.5 * x * x) * (1.0 / math.sqrt(2.0 * math.pi)))
    return (x * cdf).astype(BF16), slope.astype(BF16)


def col_sum(x):
    return jnp.sum(x, 0, keepdims=True)


def row_sum(x):
    return jnp.sum(x, -1, keepdims=True)


def row_max(x):
    return jnp.max(x, -1, keepdims=True)


def iota(shape, dim):
    return lax.broadcasted_iota(jnp.int32, shape, dim)


def score_masks(width, part):
    group = 512 // math.gcd(512, width)
    lane = iota((D, D), 1) + 512 * part
    hidden = iota((D, D), 0)
    where = ((hidden % group) == (lane // width)).astype(BF16)
    lane = iota((width, D), 1) + 512 * part
    pick = ((lane % width) == iota((width, D), 0)).astype(BF16)
    rows = 512 // group
    spread = ((iota((D, rows), 0) // group) == iota((D, rows), 1)).astype(BF16)
    return where, pick, spread


def main_kernel(
    chips,
    length,
    owner,
    counts,
    mask,
    own,
    pixels,
    cot,
    done,
    pg,
    total,
    pgout,
    flat,
    planes,
    wp,
    wr,
    ww,
    wbig,
    wsr,
    wsw,
    gains,
    xs,
    a_r,
    a_w,
    h_r,
    h_w,
    d_r,
    d_w,
    ps,
    rs,
    stat,
    dsc,
    mem,
    dmem,
    mls,
    mxh,
    mr,
    mnew,
    al_r,
    al_m,
    al_t,
    zs,
    xh1,
    r1,
    us,
    qs,
    prob,
    att,
    xh2,
    r2,
    u2,
    gs,
    dg,
    toks,
    xhk,
    rk,
    dqs,
    dys,
    dpre,
    dos,
    acc_r,
    acc_w,
    vecs,
    pix,
    far,
    stage,
    held,
    stage_sem,
    grecv,
    gsibrecv,
    send,
    recv,
    sibsend,
    sibrecv,
    pixsem,
    ready,
):
    rows = own.shape[0]
    frames = 8
    core = lax.axis_index("grp")
    me = lax.axis_index("dp")
    sibling = (1 - core, me)
    parts = parts_of(chips, rows)
    bits = chips.bit_length() - 1
    all_steps = [partners(part[2:], core, me) for part in parts]
    other_steps = [partners(part[2:], 1 - core, me) for part in parts]
    mine = core * chips + me

    def load(m, g):
        return pltpu.make_async_copy(pixels.at[m, g, 0], stage.at[g], stage_sem.at[m, g])

    for g in range(2):
        load(0, g).start()
    greet(core, me, all_steps[0])

    def block_of(index):
        return first_block(index, length) * BLOCK

    def is_outer(index):
        start = block_of(index)
        return (start < ROW_QKV) | (start + rows > ROW_WGAIN)

    inner = rows - 2 * BLOCK
    cut = (inner // BLOCK * 3 + 2) // 4 * BLOCK
    pieces = [parts[0][2:], parts[-1][2:], parts[0][2:]]
    own_steps = [partners(orders, core, me) for orders in pieces]
    side_steps = [partners(orders, 1 - core, me) for orders in pieces]

    def piece(p, index):
        start = block_of(index) + BLOCK
        if p == 0:
            return flat.at[pl.ds(pl.multiple_of(start, BLOCK), cut)]
        if p == 1:
            return flat.at[pl.ds(pl.multiple_of(start + cut, BLOCK), inner - cut)]
        return held.at[pl.ds(pl.multiple_of(index * 2 * BLOCK, BLOCK), 2 * BLOCK)]

    def pass_on(p, r):
        steps = own_steps[p]
        at = piece(p, core * chips + shifted(me, steps, r))
        copies = []
        for k in range(bits - 1, r.bit_length() - 1, -1):
            to = (core, me + steps[k])
            copies.append(
                remote(at, at, send.at[p, (1 << k) - 1 + r], grecv.at[p, r | (1 << k)], to)
            )
        copies.append(remote(at, at, sibsend.at[p, r], gsibrecv.at[p, r], sibling))
        return copies

    def start_all(copies):
        for copy in copies:
            copy.start()

    def at_distance(c):
        return [(p, r) for r in range(chips) if bin(r).count("1") == c for p in range(3)]

    def arrive(p, r):
        at = piece(p, core * chips + shifted(me, own_steps[p], r))
        remote(at, at, send.at[p, 0], grecv.at[p, r], sibling).wait_recv()
        start_all(pass_on(p, r))

    def arrive_side(p, r):
        at = piece(p, (1 - core) * chips + shifted(me, side_steps[p], r))
        remote(at, at, sibsend.at[p, 0], gsibrecv.at[p, r], sibling).wait_recv()

    def pick(m):
        chosen = []
        for g in range(2):
            load(m, g).wait()
            kept_slots, _ = kept(counts, mask, m, g, core)
            chosen.append(
                [
                    jnp.concatenate(
                        [
                            (iota((a, b), 1) == 4 * iota((a, b), 0) + one).astype(BF16)
                            for one in kept_slots
                        ],
                        0,
                    )
                    for a, b in ((CHUNK, 4 * CHUNK), (ROWS - FULL, 4 * TAIL))
                ]
            )
        for c in range(FULL // CHUNK + 1):
            first = CHUNK * c
            size = CHUNK if first < FULL else ROWS - FULL
            count = CHUNK if first < FULL else TAIL
            got = [
                dot(
                    chosen[g][0 if first < FULL else 1],
                    stage[g, first : first + count].reshape(4 * count, PIN),
                ).astype(BF16)
                for g in range(2)
            ]
            for j in range(2):
                a, b = (got[g][size * j : size * j + size] for g in range(2))
                pix[2 * m + j, first : first + size] = jnp.where((core + owner[m]) % 2 == 0, a, b)
                pg[4 + 2 * m + j, first : first + size] = jnp.where((core + owner[m]) % 2 == 0, b, a)

    start = pl.multiple_of(block_of(mine), BLOCK)
    flat[pl.ds(pl.multiple_of(start + BLOCK, BLOCK), inner), :] = own[BLOCK : BLOCK + inner, :]
    at = pl.multiple_of(mine * 2 * BLOCK, BLOCK)
    held[pl.ds(at, BLOCK), :] = own[:BLOCK, :]
    held[pl.ds(pl.multiple_of(at + BLOCK, BLOCK), BLOCK), :] = own[rows - BLOCK :, :]
    for p in range(3):
        start_all(pass_on(p, 0))
    swap_in = remote(pg.at[pl.ds(4, 4)], far, pixsem.at[2], pixsem.at[3], sibling)
    pick(0)
    for g in range(2):
        load(1, g).start()
    for c in range(1, bits + 1):
        for p, r in at_distance(c):
            arrive(p, r)
        if c == 1:
            pick(1)
            swap_in.start()
        for p, r in at_distance(c - 1):
            arrive_side(p, r)
    for p, r in at_distance(bits):
        arrive_side(p, r)
    for r in range(chips):
        for p in range(3):
            for copy in pass_on(p, r):
                copy.wait_send()

    slot_of = []
    flag_of = []
    for b in range(2):
        pairs = [kept(counts, mask, b, (core + owner[b]) % 2, half) for half in range(2)]
        slot_of.append([pairs[t // 2][0][t % 2] for t in range(4)])
        flag_of.append([pairs[t // 2][1][t % 2] for t in range(4)])

    wo = wbig.at[0:D]
    wqkv = [wbig.at[D + D * j : 2 * D + D * j] for j in range(3)]
    win = [wbig.at[4 * D + D * j : 5 * D + D * j] for j in range(4)]
    wout = wbig.at[8 * D : 12 * D]

    count = 2 * chips

    def strip(index, b):
        return held[index * 2 * BLOCK + b : index * 2 * BLOCK + b + BLOCK, :]

    def join(i):
        a, b = block_of(i), block_of(i + 1)
        at = slice(b, b + BLOCK)
        before = strip(i, BLOCK) if b - a == rows - BLOCK else flat[at, :]
        flat[at, :] = before + strip(i + 1, 0)

    def gain(k, row):
        base = row // BLOCK * BLOCK
        gains[k : k + 1, :] = flat[base : base + BLOCK, :].astype(F32)[row - base : row - base + 1, :]

    flat[:BLOCK, :] = strip(0, 0)
    end = block_of(count - 1) + rows
    flat[end - BLOCK : end, :] = strip(count - 1, BLOCK)
    for i in range(count - 1):
        join(i)
    wp[...] = flat[ROW_PATCH : ROW_PATCH + PIN, :]
    wr[...] = flat[ROW_RHID : ROW_RHID + D, :]
    ww[...] = flat[ROW_WHID : ROW_WHID + D, :]
    for k, row in enumerate((ROW_BIAS, ROW_RGAIN, ROW_AGAIN, ROW_FGAIN, ROW_WGAIN)):
        gain(k, row)
    where, chosen, spread = score_masks(READ, 0)
    wide = dot(spread, flat[ROW_RSCORE : ROW_RSCORE + READ, :]).astype(BF16) * where
    wsr[...] = dot(chosen, wide, 1, 1).astype(BF16)
    scores = jnp.zeros((MEM, D), F32)
    for c in range(4):
        at = slice(c * 128, c * 128 + 128)
        planes[c, :MEM, :] = flat[ROW_WSCORE : ROW_WSCORE + MEM, at].astype(F32)
    for part in range(3):
        where, chosen, spread = score_masks(MEM, part)
        these = jnp.concatenate(
            [planes[c, pl.ds(part, 32, stride=3), :] for c in range(4)], -1
        ).astype(BF16)
        wide = dot(spread, these).astype(BF16) * where
        scores = scores + dot(chosen, wide, 1, 1)
    wsw[...] = scores.astype(BF16)

    wo[...] = flat[ROW_AOUT : ROW_AOUT + D, :]
    wout[...] = flat[ROW_FOUT : ROW_FOUT + FFN, :]
    for row, parts_j, dst in ((ROW_QKV, 3, wqkv), (ROW_FIN, 4, win)):
        for q in range(4):
            base = row + parts_j * 128 * q
            for c in range(4):
                at = slice(c * 128, c * 128 + 128)
                planes[c, : parts_j * 128, :] = flat[base : base + parts_j * 128, at].astype(F32)
                for j in range(parts_j):
                    these = planes[c, pl.ds(j, 128, stride=parts_j), :]
                    dst[j][128 * q : 128 * q + 128, at] = these.astype(BF16)

    bias = gains[0:1, :]
    g_read = gains[1:2, :]
    g_attn = gains[2:3, :]
    g_write = gains[4:5, :]

    lanes = iota((NCOL, ROWS), 1) < P_SIZE

    def write_rows(f):
        first = WRITES.index(f) * ROWS
        return slice(first, first + ROWS)

    def frame_forward(f):
        at = slice(f * ROWS, f * ROWS + ROWS)
        seen = jnp.where(f // 4 == core, pix[f % 4], far[f % 4])
        x = (dot(seen, wp[...]) + bias).astype(BF16)
        xs[f] = x
        xh, r = norm(x.astype(F32))
        a = (xh * g_read).astype(BF16)
        a_r[at, :] = a
        h, d = gelu(dot(a, wr[...]))
        h_r[at, :] = h
        d_r[at, :] = d
        scores = dot(wsr[...], h, 1, 1)
        cols = slice(MEM, NCOL)
        if f in WRITES:
            at = write_rows(f)
            a = (xh * g_write).astype(BF16)
            a_w[at, :] = a
            h, d = gelu(dot(a, ww[...]))
            h_w[at, :] = h
            d_w[at, :] = d
            scores = jnp.concatenate([dot(wsw[...], h, 1, 1), scores], 0)
            cols = slice(0, NCOL)
        scores = jnp.where(lanes[cols], scores, -HUGE)
        best = row_max(scores)
        p = jnp.exp(scores - best)
        pb = p.astype(BF16)
        ps[f, cols] = pb
        stat[f, cols, 0:1] = best
        stat[f, cols, 1:2] = row_sum(p)
        rs[f, cols] = dot(pb, x)

    swap_in.wait()
    for f in range(frames):
        frame_forward(f)
    g_ffn = gains[3:4, :]

    mem[...] = jnp.zeros(mem.shape, F32)
    head_of = [(iota((1, D), 1) // HEAD == h) for h in range(HEADS)]
    same_clip = ((iota((HEADS * 32, 32), 0) // READ) % 2) == (iota((HEADS * 32, 32), 1) // READ)
    zero = jnp.zeros((), F32)

    def by_head(x):
        return jnp.concatenate([jnp.where(m, x, jnp.zeros_like(x)) for m in head_of], 0)

    def from_heads(x):
        total = jnp.where(head_of[0], x[:32], zero)
        for h in range(1, HEADS):
            total = total + jnp.where(head_of[h], x[32 * h : 32 * h + 32], zero)
        return total

    base_r = frames * ROWS
    base_w = len(WRITES) * ROWS
    base_k = base_w + 2 * 192

    def step_forward(t):
        live = t > 0
        last = t == 3
        if live:
            ml = mem[...].astype(BF16)
            mls[t - 1] = ml
            xh, r = norm(ml.astype(F32))
            mxh[t - 1] = xh
            mr[t - 1] = r
            at = slice(base_r + (t - 1) * 192, base_r + t * 192)
            a = (xh * g_read).astype(BF16)
            a_r[at, :] = a
            h, d = gelu(dot(a, wr[...]))
            h_r[at, :] = h
            d_r[at, :] = d
            if not last:
                at = slice(base_w + (t - 1) * 192, base_w + t * 192)
                a = (xh * g_write).astype(BF16)
                a_w[at, :] = a
                hw, d = gelu(dot(a, ww[...]))
                h_w[at, :] = hw
                d_w[at, :] = d
        z_parts = []
        for b in range(2):
            f = frame_index(b, t)
            m_f = stat[f, MEM:, 0:1]
            if live:
                s = dot(wsr[...], h[96 * b : 96 * b + 96], 1, 1)
                best = jnp.maximum(row_max(s), m_f)
                e = jnp.exp(s - best)
                part = row_sum(e)
            else:
                best = jnp.maximum(m_f, 0.0)
                part = MEM * jnp.exp(-best)
            w = jnp.exp(m_f - best)
            inv = 1.0 / (part + w * stat[f, MEM:, 1:2])
            stat[f, MEM:, 2:3] = w * inv
            z = (w * inv) * rs[f, MEM:, :]
            if live:
                al = (e * inv).astype(BF16)
                al_r[t - 1, b] = al
                z = z + dot(al, ml[96 * b : 96 * b + 96])
            z_parts.append(z)
        z = jnp.concatenate(z_parts, 0)
        zs[t] = z
        at = slice(32 * t, 32 * t + 32)
        xh, r = norm(z)
        xh1[t] = xh
        r1[t] = r
        u = (xh * g_attn).astype(BF16)
        us[at, :] = u
        q = dot(u, wqkv[0][...]).astype(BF16)
        k = dot(u, wqkv[1][...]).astype(BF16)
        v = dot(u, wqkv[2][...]).astype(BF16)
        qs[0, t] = q
        qs[1, t] = k
        qs[2, t] = v
        s = jnp.where(same_clip, dot(by_head(q), k, 1, 1) * (1.0 / math.sqrt(HEAD)), -HUGE)
        e = jnp.exp(s - row_max(s))
        p = (e / row_sum(e)).astype(BF16)
        prob[t] = p
        joined = from_heads(dot(p, v)).astype(BF16)
        att[at, :] = joined
        y = z + dot(joined, wo[...])
        xh, r = norm(y)
        xh2[t] = xh
        r2[t] = r
        n = (xh * g_ffn).astype(BF16)
        u2[at, :] = n
        o = y
        for j in range(4):
            g, d = gelu(dot(n, win[j][...]))
            gs[at, D * j : D * j + D] = g
            dg[t, :, D * j : D * j + D] = d
            o = o + dot(g, wout[D * j : D * j + D, :])
        tok = o.astype(BF16)
        toks[t] = tok
        if last:
            return
        xh, r = norm(tok.astype(F32))
        xhk[t] = xh
        rk[t] = r
        a = (xh * g_write).astype(BF16)
        at = slice(base_k + 32 * t, base_k + 32 * t + 32)
        a_w[at, :] = a
        hk, d = gelu(dot(a, ww[...]))
        h_w[at, :] = hk
        d_w[at, :] = d
        for b in range(2):
            f = frame_index(b, t)
            m_f = stat[f, :MEM, 0:1]
            s_tok = dot(wsw[...], hk[16 * b : 16 * b + 16], 1, 1)
            best = jnp.maximum(row_max(s_tok), m_f)
            if live:
                s = dot(wsw[...], hw[96 * b : 96 * b + 96], 1, 1)
                best = jnp.maximum(best, row_max(s))
                e = jnp.exp(s - best)
                part = row_sum(e)
            else:
                best = jnp.maximum(best, 0.0)
                part = MEM * jnp.exp(-best)
            e_tok = jnp.exp(s_tok - best)
            w = jnp.exp(m_f - best)
            inv = 1.0 / (part + row_sum(e_tok) + w * stat[f, :MEM, 1:2])
            stat[f, :MEM, 2:3] = w * inv
            al = (e_tok * inv).astype(BF16)
            al_t[t, b] = al
            new = (w * inv) * rs[f, :MEM, :] + dot(al, tok[16 * b : 16 * b + 16])
            if live:
                al = (e * inv).astype(BF16)
                al_m[t - 1, b] = al
                new = new + dot(al, ml[96 * b : 96 * b + 96])
            mnew[t, b] = new
            old = mem[96 * b : 96 * b + 96, :]
            mem[96 * b : 96 * b + 96, :] = jnp.where(flag_of[b][t], new, old)

    for t in range(4):
        step_forward(t)

    vecs[...] = jnp.zeros(vecs.shape, F32)
    acc_r[...] = jnp.zeros(acc_r.shape, F32)
    acc_w[...] = jnp.zeros(acc_w.shape, F32)
    dmem[...] = jnp.zeros(dmem.shape, F32)

    def add_vec(k, x):
        vecs[k : k + 1, :] = vecs[k : k + 1, :] + x

    def step_backward(t):
        live = t > 0
        last = t == 3
        gates = [jnp.where(flag_of[b][t], 1.0, 0.0) for b in range(2)]
        d_out = []
        for b in range(2):
            base = 4 * (t // 2)
            given = cot[b, base + 3]
            for i in range(3):
                given = jnp.where(slot_of[b][t] == i, cot[b, base + i], given)
            d_out.append(given.astype(F32) * gates[b])
        d_ml = []
        dh_mem = []
        keeps = []
        if last:
            for b in range(2):
                keeps.append(jnp.zeros((96, D), F32))
                d_ml.append(keeps[b])
        else:
            dh_tok = []
            at_k = slice(base_k + 32 * t, base_k + 32 * t + 32)
            hk = h_w[at_k, :]
            tok = toks[t]
            for b in range(2):
                f = frame_index(b, t)
                down = dmem[96 * b : 96 * b + 96, :]
                ds = (down * gates[b]).astype(BF16)
                keeps.append(down * (1.0 - gates[b]))
                dsc[f, :MEM, :] = ds
                c = row_sum(ds.astype(F32) * mnew[t, b])
                stat[f, :MEM, 3:4] = c
                al = al_t[t, b]
                rows_b = slice(16 * b, 16 * b + 16)
                d_out[b] = d_out[b] + dot(al, ds, 0, 0)
                back = (al.astype(F32) * (dot(ds, tok[rows_b], 1, 1) - c)).astype(BF16)
                dh_tok.append(dot(back, wsw[...], 0, 0))
                acc = dot(back, hk[rows_b])
                if live:
                    rows_b = slice(96 * b, 96 * b + 96)
                    ml = mls[t - 1, rows_b, :]
                    al = al_m[t - 1, b]
                    d_ml.append(dot(al, ds, 0, 0))
                    back = (al.astype(F32) * (dot(ds, ml, 1, 1) - c)).astype(BF16)
                    dh_mem.append(dot(back, wsw[...], 0, 0))
                    at = slice(base_w + (t - 1) * 192 + 96 * b, base_w + (t - 1) * 192 + 96 * b + 96)
                    acc = acc + dot(back, h_w[at, :])
                acc_w[...] = acc_w[...] + acc
            dgk = (jnp.concatenate(dh_tok, 0) * d_w[at_k, :].astype(F32)).astype(BF16)
            d_w[at_k, :] = dgk
            da = dot(dgk, ww[...], 1, 1)
            xh = xhk[t]
            add_vec(4, col_sum(da * xh))
            dx = norm_back(da * g_write, xh, rk[t])
            for b in range(2):
                d_out[b] = d_out[b] + dx[16 * b : 16 * b + 16]
        at = slice(32 * t, 32 * t + 32)
        do = jnp.concatenate(d_out, 0)
        dob = do.astype(BF16)
        dos[at, :] = dob
        dn = jnp.zeros((32, D), F32)
        for j in range(4):
            sl = slice(D * j, D * j + D)
            dp = (dot(dob, wout[sl, :], 1, 1) * dg[t, :, sl].astype(F32)).astype(BF16)
            dpre[at, sl] = dp
            dn = dn + dot(dp, win[j][...], 1, 1)
        add_vec(3, col_sum(dn * xh2[t]))
        dy = do + norm_back(dn * g_ffn, xh2[t], r2[t])
        dyb = dy.astype(BF16)
        dys[at, :] = dyb
        dbig = by_head(dot(dyb, wo[...], 1, 1).astype(BF16))
        p = prob[t]
        q, k, v = qs[0, t], qs[1, t], qs[2, t]
        dp = dot(dbig, v, 1, 1)
        pf = p.astype(F32)
        ds = (pf * (dp - row_sum(dp * pf)) * (1.0 / math.sqrt(HEAD))).astype(BF16)
        dv = dot(p, dbig, 0, 0).astype(BF16)
        dq = from_heads(dot(ds, k)).astype(BF16)
        dk = dot(ds, by_head(q), 0, 0).astype(BF16)
        dqs[0, at, :] = dq
        dqs[1, at, :] = dk
        dqs[2, at, :] = dv
        du = dot(dq, wqkv[0][...], 1, 1) + dot(dk, wqkv[1][...], 1, 1) + dot(dv, wqkv[2][...], 1, 1)
        add_vec(2, col_sum(du * xh1[t]))
        dz = dy + norm_back(du * g_attn, xh1[t], r1[t])
        dzb = dz.astype(BF16)
        c_all = row_sum(dzb.astype(F32) * zs[t])
        dh_r = []
        for b in range(2):
            f = frame_index(b, t)
            ds = dzb[16 * b : 16 * b + 16]
            c = c_all[16 * b : 16 * b + 16]
            dsc[f, MEM:, :] = ds
            stat[f, MEM:, 3:4] = c
            if live:
                rows_b = slice(96 * b, 96 * b + 96)
                al = al_r[t - 1, b]
                d_ml[b] = d_ml[b] + dot(al, ds, 0, 0)
                back = (al.astype(F32) * (dot(ds, mls[t - 1, rows_b, :], 1, 1) - c)).astype(BF16)
                dh_r.append(dot(back, wsr[...], 0, 0))
                at_b = slice(base_r + (t - 1) * 192 + 96 * b, base_r + (t - 1) * 192 + 96 * b + 96)
                acc_r[...] = acc_r[...] + dot(back, h_r[at_b, :])
        if not live:
            return
        at_m = slice(base_r + (t - 1) * 192, base_r + t * 192)
        xh = mxh[t - 1]
        dgr = (jnp.concatenate(dh_r, 0) * d_r[at_m, :].astype(F32)).astype(BF16)
        d_r[at_m, :] = dgr
        da = dot(dgr, wr[...], 1, 1)
        add_vec(1, col_sum(da * xh))
        g = da * g_read
        if not last:
            at_m = slice(base_w + (t - 1) * 192, base_w + t * 192)
            dgw = (jnp.concatenate(dh_mem, 0) * d_w[at_m, :].astype(F32)).astype(BF16)
            d_w[at_m, :] = dgw
            da = dot(dgw, ww[...], 1, 1)
            add_vec(4, col_sum(da * xh))
            g = g + da * g_write
        dx = norm_back(g, xh, mr[t - 1])
        for b in range(2):
            rows_b = slice(96 * b, 96 * b + 96)
            dmem[rows_b, :] = keeps[b] + d_ml[b] + dx[rows_b]

    for t in range(3, -1, -1):
        step_backward(t)

    for other in [sibling] + [(core, me + step) for step in all_steps[0]]:
        pl.semaphore_signal(ready, inc=1, device_id=other, device_id_type=MESH)
    flat[ROW_AOUT : ROW_AOUT + D, :] = dot(att[...], dys[...], 0, 0).astype(BF16)
    for j in range(4):
        sl = slice(D * j, D * j + D)
        flat[ROW_FOUT + D * j : ROW_FOUT + D * j + D, :] = dot(gs[:, sl], dos[...], 0, 0).astype(BF16)
    for row, count, left, right in (
        (ROW_QKV, 3, us, lambda j: dqs[j]),
        (ROW_FIN, 4, u2, lambda j: dpre[:, D * j : D * j + D]),
    ):
        for q in range(4):
            for j in range(count):
                part = dot(left[:, 128 * q : 128 * q + 128], right(j), 0, 0)
                for c in range(4):
                    planes[c, pl.ds(j, 128, stride=count), :] = part[:, 128 * c : 128 * c + 128]
            base = row + count * 128 * q
            for c in range(4):
                at = slice(128 * c, 128 * c + 128)
                flat[base : base + count * 128, at] = planes[c, : count * 128, :].astype(BF16)
    flat[ROW_AGAIN : ROW_AGAIN + 1, :] = vecs[2:3, :].astype(BF16)
    flat[ROW_FGAIN : ROW_FGAIN + 1, :] = vecs[3:4, :].astype(BF16)

    def place_of(p, r):
        start, size = parts[p][:2]
        return chips * start + r * size

    def side(p, r):
        return wbig.at[pl.ds(place_of(p, r), parts[p][1])]

    def slot(p, k, r):
        start, size = parts[p][:2]
        return (chips - 1) * start + ((1 << k) - 1 + r) * size

    def turns(top, end):
        return [(p, r) for r in range(top - 1, end - 1, -1) for p in range(len(parts))]


    def swap(p, r):
        index = (1 - core) * chips + shifted(me, other_steps[p], r)
        start = pl.multiple_of(block_of(index) + parts[p][0], BLOCK)
        src = flat.at[pl.ds(start, parts[p][1])]
        return remote(src, side(p, r), sibsend.at[p, r], sibrecv.at[p, r], sibling), index

    def send_on(p, r):
        top = r.bit_length() - 1
        low = r - (1 << top)
        return remote(
            side(p, r),
            held.at[pl.ds(slot(p, top, low), parts[p][1])],
            send.at[p, r],
            recv.at[p, (1 << top) - 1 + low],
            (core, me + all_steps[p][top]),
        )

    def swap_all(late):
        for p, r in turns(chips, 0):
            copy, index = swap(p, r)

            @pl.when(is_outer(index) == late)
            def _(copy=copy):
                copy.start()

    def turn(p, r, late):
        index = core * chips + shifted(me, all_steps[p], r)
        start, size = parts[p][:2]

        @pl.when(is_outer(index) == late)
        def _():
            swap(p, r)[0].wait_recv()
            slots = []
            for k in range(bits - 1, r.bit_length() - 1, -1):
                at = held.at[pl.ds(slot(p, k, r), size)]
                remote(at, at, send.at[p, r], recv.at[p, (1 << k) - 1 + r], sibling).wait_recv()
                slots.append(slot(p, k, r))
            base = block_of(index) + start

            def add(i, carry):
                step = i * BLOCK
                at = pl.ds(pl.multiple_of(place_of(p, r) + step, BLOCK), BLOCK)
                mine = flat[pl.ds(pl.multiple_of(base + step, BLOCK), BLOCK), :]
                value = mine.astype(F32) + wbig[at, :].astype(F32)
                for one in slots:
                    value = value + held[pl.ds(pl.multiple_of(one + step, BLOCK), BLOCK), :].astype(F32)
                if r == 0:
                    for c in range(4):
                        spots = pl.ds(4 * (start + step) + c, BLOCK, stride=4)
                        total[spots, :] = value[:, 128 * c : 128 * c + 128]
                else:
                    wbig[at, :] = value.astype(BF16)
                return carry

            lax.fori_loop(0, size // BLOCK, add, 0)
            if r > 0:
                send_on(p, r).start()

    def frame_backward(f):
        at = slice(f * ROWS, f * ROWS + ROWS)
        x = xs[f]
        cols = slice(0 if f in WRITES else MEM, NCOL)
        ds = dsc[f, cols]
        al = ps[f, cols].astype(F32) * stat[f, cols, 2:3]
        alb = al.astype(BF16)
        back = (al * (dot(ds, x, 1, 1) - stat[f, cols, 3:4])).astype(BF16)
        back_r = back[-READ:]
        acc_r[...] = acc_r[...] + dot(back_r, h_r[at, :])
        xh, r = norm(x.astype(F32))
        dgr = (dot(back_r, wsr[...], 0, 0) * d_r[at, :].astype(F32)).astype(BF16)
        d_r[at, :] = dgr
        da = dot(dgr, wr[...], 1, 1)
        add_vec(1, col_sum(da * xh))
        g = da * g_read
        if f in WRITES:
            at = write_rows(f)
            acc_w[...] = acc_w[...] + dot(back[:MEM], h_w[at, :])
            dgw = (dot(back[:MEM], wsw[...], 0, 0) * d_w[at, :].astype(F32)).astype(BF16)
            d_w[at, :] = dgw
            da = dot(dgw, ww[...], 1, 1)
            add_vec(4, col_sum(da * xh))
            g = g + da * g_write
        dx = (dot(alb, ds, 0, 0) + norm_back(g, xh, r)).astype(BF16)
        xs[f] = dx
        add_vec(0, col_sum(dx.astype(F32)))
        to = jnp.where(core == f // 4, 0, 4) + f % 4
        pg[to] = dot(dx, wp[...], 1, 1).astype(BF16)

    pl.semaphore_wait(ready, bits + 1)
    swap_all(False)
    half = chips // 2
    todo = turns(chips, half)
    every = len(todo) // frames
    for i, (p, r) in enumerate(todo):
        if i % every == 0 and i // every < frames:
            frame_backward(i // every)
        turn(p, r, False)
    quarter = chips // 4
    for p, r in turns(half, quarter):
        turn(p, r, False)

    swap_pix = remote(pg.at[pl.ds(4, 4)], pgout, pixsem.at[0], pixsem.at[1], sibling)
    swap_pix.start()
    n = 4 * ROWS
    flat[ROW_PATCH : ROW_PATCH + PIN, :] = (
        dot(pix[...].reshape(n, PIN), xs[pl.ds(4 * core, 4)].reshape(n, D), 0, 0)
        + dot(far[...].reshape(n, PIN), xs[pl.ds(4 - 4 * core, 4)].reshape(n, D), 0, 0)
    ).astype(BF16)
    flat[ROW_RHID : ROW_RHID + D, :] = dot(a_r[...], d_r[...], 0, 0).astype(BF16)
    flat[ROW_WHID : ROW_WHID + D, :] = dot(a_w[...], d_w[...], 0, 0).astype(BF16)
    where, chosen, spread = score_masks(READ, 0)
    wide = dot(acc_r[...].astype(BF16), chosen, 0, 0).astype(BF16) * where
    flat[ROW_RSCORE : ROW_RSCORE + READ, :] = dot(spread, wide, 0, 0).astype(BF16)
    for part in range(3):
        where, chosen, spread = score_masks(MEM, part)
        wide = dot(acc_w[...].astype(BF16), chosen, 0, 0).astype(BF16) * where
        these = dot(spread, wide, 0, 0)
        for c in range(4):
            planes[c, pl.ds(part, 32, stride=3), :] = these[:, 128 * c : 128 * c + 128]
    for c in range(4):
        at = slice(128 * c, 128 * c + 128)
        flat[ROW_WSCORE : ROW_WSCORE + MEM, at] = planes[c, :MEM, :].astype(BF16)
    for k, row in ((0, ROW_BIAS), (1, ROW_RGAIN), (4, ROW_WGAIN)):
        flat[row : row + 1, :] = vecs[k : k + 1, :].astype(BF16)
    flat[ROW_END:, :] = jnp.zeros((flat.shape[0] - ROW_END, D), BF16)

    swap_all(True)
    for b in range(2):
        for s in range(STEPS):
            value = jnp.zeros((READ, D), BF16)
            for t in (s // 4 * 2, s // 4 * 2 + 1):
                hit = (slot_of[b][t] == s % 4) & flag_of[b][t]
                value = jnp.where(hit, toks[t, READ * b : READ * b + READ, :], value)
            done[b, s] = value
    for p, r in turns(chips, half):
        turn(p, r, True)
    for p, r in turns(half, quarter):
        turn(p, r, True)
    for p, r in turns(quarter, 0):
        turn(p, r, False)
        turn(p, r, True)
    for p, r in turns(chips, 0):
        swap(p, r)[0].wait_send()
        if r > 0:
            send_on(p, r).wait_send()
    swap_pix.wait()


def main(own, pixels, cot, owner, counts, mask, chips, length):
    rows = own.shape[0]
    height = (2 * chips - 1) * length // (BLOCK * D) * BLOCK + rows
    n = 8 * ROWS
    vmem = pl.BlockSpec(memory_space=pltpu.VMEM)
    smem = pl.BlockSpec(memory_space=pltpu.SMEM)
    hbm = pl.BlockSpec(memory_space=pl.ANY)
    v = pltpu.VMEM
    dma = pltpu.SemaphoreType.DMA
    return pl.pallas_call(
        functools.partial(main_kernel, chips, length),
        out_shape=(
            jax.ShapeDtypeStruct((2, STEPS, READ, D), BF16),
            jax.ShapeDtypeStruct((8, ROWS, PIN), BF16),
            jax.ShapeDtypeStruct((4 * rows, 128), F32),
            jax.ShapeDtypeStruct((4, ROWS, PIN), BF16),
        ),
        in_specs=[smem, smem, smem, vmem, hbm, vmem],
        out_specs=[vmem, vmem, vmem, hbm],
        scratch_shapes=[
            v((height, D), BF16),
            v((4, D, 128), F32),
            v((PIN, D), BF16),
            v((D, D), BF16),
            v((D, D), BF16),
            v((max(12 * D, chips * rows), D), BF16),
            v((READ, D), BF16),
            v((MEM, D), BF16),
            v((8, D), F32),
            v((8, ROWS, D), BF16),
            v((n + 576, D), BF16),
            v((n - 2 * ROWS + 480, D), BF16),
            v((n + 576, D), BF16),
            v((n - 2 * ROWS + 480, D), BF16),
            v((n + 576, D), BF16),
            v((n - 2 * ROWS + 480, D), BF16),
            v((8, NCOL, ROWS), BF16),
            v((8, NCOL, D), F32),
            v((8, NCOL, 8), F32),
            v((8, NCOL, D), BF16),
            v((192, D), F32),
            v((192, D), F32),
            v((3, 192, D), BF16),
            v((3, 192, D), F32),
            v((3, 192, 1), F32),
            v((3, 2, MEM, D), F32),
            v((3, 2, READ, MEM), BF16),
            v((2, 2, MEM, MEM), BF16),
            v((3, 2, MEM, READ), BF16),
            v((4, 32, D), F32),
            v((4, 32, D), F32),
            v((4, 32, 1), F32),
            v((128, D), BF16),
            v((3, 4, 32, D), BF16),
            v((4, HEADS * 32, 32), BF16),
            v((128, D), BF16),
            v((4, 32, D), F32),
            v((4, 32, 1), F32),
            v((128, D), BF16),
            v((128, FFN), BF16),
            v((4, 32, FFN), BF16),
            v((4, 32, D), BF16),
            v((3, 32, D), F32),
            v((3, 32, 1), F32),
            v((3, 128, D), BF16),
            v((128, D), BF16),
            v((128, FFN), BF16),
            v((128, D), BF16),
            v((READ, D), F32),
            v((MEM, D), F32),
            v((8, D), F32),
            v((4, ROWS, PIN), BF16),
            v((4, ROWS, PIN), BF16),
            v((2, P_SIZE, 4, PIN), BF16),
            v((max((chips - 1) * rows, 4 * chips * BLOCK), D), BF16),
            dma((2, 2)),
            dma((PARTS, chips)),
            dma((PARTS, chips)),
            dma((PARTS, chips)),
            dma((PARTS, chips)),
            dma((PARTS, chips)),
            dma((PARTS, chips)),
            dma((4,)),
            pltpu.SemaphoreType.REGULAR,
        ],
        compiler_params=pltpu.CompilerParams(
            collective_id=0, has_side_effects=True, vmem_limit_bytes=VMEM_LIMIT
        ),
        name="model",
    )(owner, counts, mask, own, pixels, cot)


def body(pixels, counts, step_mask, owner, params, cotangent):
    chips = lax.axis_size("dp")
    length = params.shape[0]
    core = lax.axis_index("grp").astype(jnp.int32)
    dp = lax.axis_index("dp").astype(jnp.int32)
    counts = counts[:, :, 0]
    mask = step_mask[:, :, 0]
    owner = owner[:, 0]

    rows = window_rows(length)
    offset = ((core * chips + dp) * length) % (BLOCK * D)
    wide = jnp.pad(params, (BLOCK * D, rows * D - length))
    win = lax.dynamic_slice(wide, (BLOCK * D - offset,), (rows * D,)).reshape(rows, D)

    cot = cotangent[:, 0, 0]
    done, near_grad, total, far_grad = main(
        win, jnp.swapaxes(pixels, 3, 4), cot, owner, counts, mask, chips, length
    )
    shard_grad = lax.dynamic_slice(total.reshape(rows * D), (offset,), (length,))
    pixel_grad = place(near_grad, far_grad, owner, counts, mask, pixels.shape)
    return (done[:, None, None], pixel_grad, shard_grad)


def solution(mesh):
    return jax.shard_map(
        body,
        mesh=mesh,
        in_specs=(
            P(None, None, "dp", "grp", None, None),
            P(None, None, "dp"),
            P(None, None, "dp", None),
            P(None, "dp"),
            P(("grp", "dp")),
            P(None, "grp", "dp", None, None, None),
        ),
        out_specs=(
            P(None, "grp", "dp", None, None, None),
            P(None, None, "dp", "grp", None, None),
            P(("grp", "dp")),
        ),
        check_vma=False,
    )
```

```python
import functools
import math

import jax
import jax.numpy as jnp
from jax import lax
from jax.experimental import pallas as pl
from jax.experimental.pallas import tpu as pltpu
from jax.sharding import PartitionSpec as P

MESH = pl.DeviceIdType.MESH
F32 = jnp.float32
BF16 = jnp.bfloat16

D = 512
HEADS = 8
HEAD = D // HEADS
FFN = 2048
PIN = 768
P_SIZE = 196
ROWS = 208
MEM = 96
READ = 16
NCOL = MEM + READ
STEPS = 8
BLOCK = 16
EPS = 1e-6
PARTS = 3
HUGE = 1e30
HALF_INT = 1 << 30

ROW_PATCH = 0
ROW_BIAS = 768
ROW_RGAIN = 769
ROW_RHID = 770
ROW_RSCORE = 1282
ROW_AGAIN = 1298
ROW_QKV = 1299
ROW_AOUT = 2835
ROW_FGAIN = 3347
ROW_FIN = 3348
ROW_FOUT = 5396
ROW_WGAIN = 7444
ROW_WHID = 7445
ROW_WSCORE = 7957
ROW_END = 8053

VMEM_LIMIT = 63 * 2**20


def dot(a, b, ca=1, cb=0):
    return lax.dot_general(a, b, (((ca,), (cb,)), ((), ())), preferred_element_type=F32)


def window_rows(length):
    return (length + BLOCK * D - 2) // (BLOCK * D) * BLOCK + BLOCK


def first_block(index, length):
    return (index * length) // (BLOCK * D)


def parts_of(chips, rows):
    bits = chips.bit_length() - 1
    high = list(range(bits - 1, 1, -1))
    blocks = rows // BLOCK
    b = blocks * 2 // 3 * BLOCK
    return [
        (0, b, high + [0, 1], high + [1, 0]),
        (b, rows - b, [0, 1] + high, [1, 0] + high),
    ]


def partners(orders, core, me):
    steps = []
    for one, two in zip(*orders):
        a = (1 - 2 * ((me // (1 << one)) % 2)) * (1 << one)
        b = (1 - 2 * ((me // (1 << two)) % 2)) * (1 << two)
        steps.append(a + core * (b - a))
    return steps


def shifted(me, steps, r):
    at = me
    for k, step in enumerate(steps):
        if (r >> k) & 1:
            at = at + step
    return at


def greet(core, me, steps):
    barrier = pltpu.get_barrier_semaphore()
    places = [(core, me + step) for step in steps] + [(1 - core, me)]
    for place in places:
        pl.semaphore_signal(barrier, inc=1, device_id=place, device_id_type=MESH)
    pl.semaphore_wait(barrier, len(places))


def remote(src, dst, s, r, place):
    return pltpu.make_async_remote_copy(
        src_ref=src, dst_ref=dst, send_sem=s, recv_sem=r, device_id=place, device_id_type=MESH
    )


CHUNK = 64
FULL = P_SIZE // CHUNK * CHUNK
TAIL = P_SIZE - FULL


def kept(counts, mask, m, g, half):
    base = half * (STEPS // 2)
    ok = [(mask[m, g, base + i] == 1) & (base + i < counts[m, g]) for i in range(4)]
    last = jnp.int32
    first = jnp.where(ok[0], 0, jnp.where(ok[1], 1, jnp.where(ok[2], 2, 3))).astype(last)
    second = jnp.where(ok[3], 3, jnp.where(ok[2], 2, jnp.where(ok[1], 1, 0))).astype(last)
    number = sum(o.astype(jnp.int32) for o in ok)
    return (first, second), (number > 0, number > 1)


def place_kernel(owner, counts, mask, near, far, out):
    m, g = pl.program_id(0), pl.program_id(1)
    core = lax.axis_index("grp")
    is_near = (core + owner[m]) % 2 == g
    slots, flags = kept(counts, mask, m, g, core)
    where = [jnp.where(flag, slot, -HALF_INT) for slot, flag in zip(slots, flags)]

    def spread(rows, cols):
        one = [(iota((rows, cols), 0) == 4 * iota((rows, cols), 1) + s).astype(BF16) for s in where]
        return jnp.concatenate(one, 1)

    def to_slots(first, count, weights):
        at = slice(first, first + count)
        these = [jnp.where(is_near, near[0, j, at], far[0, j, at]) for j in range(2)]
        return dot(weights, jnp.concatenate(these, 0)).astype(BF16)

    whole = spread(4 * CHUNK, CHUNK)
    for c in range(FULL // CHUNK):
        got = to_slots(CHUNK * c, CHUNK, whole)
        out[0, 0, 0, CHUNK * c : CHUNK * c + CHUNK] = got.reshape(CHUNK, 4, PIN)
    got = to_slots(FULL, ROWS - FULL, spread(4 * TAIL, ROWS - FULL))
    out[0, 0, 0, FULL:] = got.reshape(TAIL, 4, PIN)


def place(near, far, owner, counts, mask, shape):
    m, g, c, s, rows, cols = shape
    out = pl.pallas_call(
        place_kernel,
        out_shape=jax.ShapeDtypeStruct((m, g, c, rows, s, cols), BF16),
        grid_spec=pltpu.PrefetchScalarGridSpec(
            num_scalar_prefetch=3,
            grid=(2, 2),
            in_specs=[pl.BlockSpec((1, 2, ROWS, PIN), lambda m, g, *_: (m, 0, 0, 0))] * 2,
            out_specs=pl.BlockSpec(
                (1, 1, 1, rows, s, cols), lambda m, g, *_: (m, g, 0, 0, 0, 0)
            ),
        ),
        compiler_params=pltpu.CompilerParams(vmem_limit_bytes=VMEM_LIMIT),
        name="place",
    )(owner, counts, mask, near.reshape(4, 2, ROWS, PIN), far.reshape(2, 2, ROWS, PIN))
    return jnp.swapaxes(out, 3, 4)


def frame_index(clip, step):
    return (step // 2) * 4 + clip * 2 + step % 2


WRITES = sorted(frame_index(clip, step) for clip in range(2) for step in range(3))


def norm(x):
    mean = jnp.mean(x, -1, keepdims=True)
    centered = x - mean
    r = lax.rsqrt(jnp.mean(centered * centered, -1, keepdims=True) + EPS)
    return centered * r, r


def norm_back(g, xh, r):
    return r * (g - jnp.mean(g, -1, keepdims=True) - xh * jnp.mean(g * xh, -1, keepdims=True))


def gelu(x):
    cdf = 0.5 + 0.5 * lax.erf(x * math.sqrt(0.5))
    slope = cdf + x * (jnp.exp(-0.5 * x * x) * (1.0 / math.sqrt(2.0 * math.pi)))
    return (x * cdf).astype(BF16), slope.astype(BF16)


def col_sum(x):
    return jnp.sum(x, 0, keepdims=True)


def row_sum(x):
    return jnp.sum(x, -1, keepdims=True)


def row_max(x):
    return jnp.max(x, -1, keepdims=True)


def iota(shape, dim):
    return lax.broadcasted_iota(jnp.int32, shape, dim)


def score_masks(width, part):
    group = 512 // math.gcd(512, width)
    lane = iota((D, D), 1) + 512 * part
    hidden = iota((D, D), 0)
    where = ((hidden % group) == (lane // width)).astype(BF16)
    lane = iota((width, D), 1) + 512 * part
    pick = ((lane % width) == iota((width, D), 0)).astype(BF16)
    rows = 512 // group
    spread = ((iota((D, rows), 0) // group) == iota((D, rows), 1)).astype(BF16)
    return where, pick, spread


def main_kernel(
    chips,
    length,
    owner,
    counts,
    mask,
    own,
    pixels,
    cot,
    done,
    pg,
    total,
    pgout,
    flat,
    planes,
    wp,
    wr,
    ww,
    wbig,
    wsr,
    wsw,
    gains,
    xs,
    a_r,
    a_w,
    h_r,
    h_w,
    d_r,
    d_w,
    ps,
    rs,
    stat,
    dsc,
    mem,
    dmem,
    mls,
    mxh,
    mr,
    mnew,
    al_r,
    al_m,
    al_t,
    zs,
    xh1,
    r1,
    us,
    qs,
    prob,
    att,
    xh2,
    r2,
    u2,
    gs,
    dg,
    toks,
    xhk,
    rk,
    dqs,
    dys,
    dpre,
    dos,
    acc_r,
    acc_w,
    vecs,
    pix,
    far,
    stage,
    held,
    stage_sem,
    grecv,
    gsibrecv,
    send,
    recv,
    sibsend,
    sibrecv,
    pixsem,
    ready,
):
    rows = own.shape[0]
    frames = 8
    core = lax.axis_index("grp")
    me = lax.axis_index("dp")
    sibling = (1 - core, me)
    parts = parts_of(chips, rows)
    bits = chips.bit_length() - 1
    all_steps = [partners(part[2:], core, me) for part in parts]
    other_steps = [partners(part[2:], 1 - core, me) for part in parts]
    mine = core * chips + me

    def load(m, g):
        return pltpu.make_async_copy(pixels.at[m, g, 0], stage.at[g], stage_sem.at[m, g])

    for g in range(2):
        load(0, g).start()
    greet(core, me, all_steps[0])

    def block_of(index):
        return first_block(index, length) * BLOCK

    def is_outer(index):
        start = block_of(index)
        return (start < ROW_QKV) | (start + rows > ROW_WGAIN)

    inner = rows - 2 * BLOCK
    cut = (inner // BLOCK * 3 + 2) // 4 * BLOCK
    pieces = [parts[0][2:], parts[-1][2:], parts[0][2:]]
    own_steps = [partners(orders, core, me) for orders in pieces]
    side_steps = [partners(orders, 1 - core, me) for orders in pieces]

    def piece(p, index):
        start = block_of(index) + BLOCK
        if p == 0:
            return flat.at[pl.ds(pl.multiple_of(start, BLOCK), cut)]
        if p == 1:
            return flat.at[pl.ds(pl.multiple_of(start + cut, BLOCK), inner - cut)]
        return held.at[pl.ds(pl.multiple_of(index * 2 * BLOCK, BLOCK), 2 * BLOCK)]

    def pass_on(p, r):
        steps = own_steps[p]
        at = piece(p, core * chips + shifted(me, steps, r))
        copies = []
        for k in range(bits - 1, r.bit_length() - 1, -1):
            to = (core, me + steps[k])
            copies.append(
                remote(at, at, send.at[p, (1 << k) - 1 + r], grecv.at[p, r | (1 << k)], to)
            )
        copies.append(remote(at, at, sibsend.at[p, r], gsibrecv.at[p, r], sibling))
        return copies

    def start_all(copies):
        for copy in copies:
            copy.start()

    def at_distance(c):
        return [(p, r) for r in range(chips) if bin(r).count("1") == c for p in range(3)]

    def arrive(p, r):
        at = piece(p, core * chips + shifted(me, own_steps[p], r))
        remote(at, at, send.at[p, 0], grecv.at[p, r], sibling).wait_recv()
        start_all(pass_on(p, r))

    def arrive_side(p, r):
        at = piece(p, (1 - core) * chips + shifted(me, side_steps[p], r))
        remote(at, at, sibsend.at[p, 0], gsibrecv.at[p, r], sibling).wait_recv()

    def pick(m):
        chosen = []
        for g in range(2):
            load(m, g).wait()
            kept_slots, _ = kept(counts, mask, m, g, core)
            chosen.append(
                [
                    jnp.concatenate(
                        [
                            (iota((a, b), 1) == 4 * iota((a, b), 0) + one).astype(BF16)
                            for one in kept_slots
                        ],
                        0,
                    )
                    for a, b in ((CHUNK, 4 * CHUNK), (ROWS - FULL, 4 * TAIL))
                ]
            )
        for c in range(FULL // CHUNK + 1):
            first = CHUNK * c
            size = CHUNK if first < FULL else ROWS - FULL
            count = CHUNK if first < FULL else TAIL
            got = [
                dot(
                    chosen[g][0 if first < FULL else 1],
                    stage[g, first : first + count].reshape(4 * count, PIN),
                ).astype(BF16)
                for g in range(2)
            ]
            for j in range(2):
                a, b = (got[g][size * j : size * j + size] for g in range(2))
                pix[2 * m + j, first : first + size] = jnp.where((core + owner[m]) % 2 == 0, a, b)
                pg[4 + 2 * m + j, first : first + size] = jnp.where((core + owner[m]) % 2 == 0, b, a)

    start = pl.multiple_of(block_of(mine), BLOCK)
    flat[pl.ds(pl.multiple_of(start + BLOCK, BLOCK), inner), :] = own[BLOCK : BLOCK + inner, :]
    at = pl.multiple_of(mine * 2 * BLOCK, BLOCK)
    held[pl.ds(at, BLOCK), :] = own[:BLOCK, :]
    held[pl.ds(pl.multiple_of(at + BLOCK, BLOCK), BLOCK), :] = own[rows - BLOCK :, :]
    for p in range(3):
        start_all(pass_on(p, 0))
    swap_in = remote(pg.at[pl.ds(4, 4)], far, pixsem.at[2], pixsem.at[3], sibling)
    pick(0)
    for g in range(2):
        load(1, g).start()
    for c in range(1, bits + 1):
        for p, r in at_distance(c):
            arrive(p, r)
        if c == 1:
            pick(1)
            swap_in.start()
        for p, r in at_distance(c - 1):
            arrive_side(p, r)
    for p, r in at_distance(bits):
        arrive_side(p, r)
    for r in range(chips):
        for p in range(3):
            for copy in pass_on(p, r):
                copy.wait_send()

    slot_of = []
    flag_of = []
    for b in range(2):
        pairs = [kept(counts, mask, b, (core + owner[b]) % 2, half) for half in range(2)]
        slot_of.append([pairs[t // 2][0][t % 2] for t in range(4)])
        flag_of.append([pairs[t // 2][1][t % 2] for t in range(4)])

    wo = wbig.at[0:D]
    wqkv = [wbig.at[D + D * j : 2 * D + D * j] for j in range(3)]
    win = [wbig.at[4 * D + D * j : 5 * D + D * j] for j in range(4)]
    wout = wbig.at[8 * D : 12 * D]

    count = 2 * chips

    def strip(index, b):
        return held[index * 2 * BLOCK + b : index * 2 * BLOCK + b + BLOCK, :]

    def join(i):
        a, b = block_of(i), block_of(i + 1)
        at = slice(b, b + BLOCK)
        before = strip(i, BLOCK) if b - a == rows - BLOCK else flat[at, :]
        flat[at, :] = before + strip(i + 1, 0)

    def gain(k, row):
        base = row // BLOCK * BLOCK
        gains[k : k + 1, :] = flat[base : base + BLOCK, :].astype(F32)[row - base : row - base + 1, :]

    flat[:BLOCK, :] = strip(0, 0)
    end = block_of(count - 1) + rows
    flat[end - BLOCK : end, :] = strip(count - 1, BLOCK)
    for i in range(count - 1):
        join(i)
    wp[...] = flat[ROW_PATCH : ROW_PATCH + PIN, :]
    wr[...] = flat[ROW_RHID : ROW_RHID + D, :]
    ww[...] = flat[ROW_WHID : ROW_WHID + D, :]
    for k, row in enumerate((ROW_BIAS, ROW_RGAIN, ROW_AGAIN, ROW_FGAIN, ROW_WGAIN)):
        gain(k, row)
    where, chosen, spread = score_masks(READ, 0)
    wide = dot(spread, flat[ROW_RSCORE : ROW_RSCORE + READ, :]).astype(BF16) * where
    wsr[...] = dot(chosen, wide, 1, 1).astype(BF16)
    scores = jnp.zeros((MEM, D), F32)
    for c in range(4):
        at = slice(c * 128, c * 128 + 128)
        planes[c, :MEM, :] = flat[ROW_WSCORE : ROW_WSCORE + MEM, at].astype(F32)
    for part in range(3):
        where, chosen, spread = score_masks(MEM, part)
        these = jnp.concatenate(
            [planes[c, pl.ds(part, 32, stride=3), :] for c in range(4)], -1
        ).astype(BF16)
        wide = dot(spread, these).astype(BF16) * where
        scores = scores + dot(chosen, wide, 1, 1)
    wsw[...] = scores.astype(BF16)

    wo[...] = flat[ROW_AOUT : ROW_AOUT + D, :]
    wout[...] = flat[ROW_FOUT : ROW_FOUT + FFN, :]
    for row, parts_j, dst in ((ROW_QKV, 3, wqkv), (ROW_FIN, 4, win)):
        for q in range(4):
            base = row + parts_j * 128 * q
            for c in range(4):
                at = slice(c * 128, c * 128 + 128)
                planes[c, : parts_j * 128, :] = flat[base : base + parts_j * 128, at].astype(F32)
                for j in range(parts_j):
                    these = planes[c, pl.ds(j, 128, stride=parts_j), :]
                    dst[j][128 * q : 128 * q + 128, at] = these.astype(BF16)

    bias = gains[0:1, :]
    g_read = gains[1:2, :]
    g_attn = gains[2:3, :]
    g_write = gains[4:5, :]

    lanes = iota((NCOL, ROWS), 1) < P_SIZE

    def write_rows(f):
        first = WRITES.index(f) * ROWS
        return slice(first, first + ROWS)

    def frame_forward(f):
        at = slice(f * ROWS, f * ROWS + ROWS)
        seen = jnp.where(f // 4 == core, pix[f % 4], far[f % 4])
        x = (dot(seen, wp[...]) + bias).astype(BF16)
        xs[f] = x
        xh, r = norm(x.astype(F32))
        a = (xh * g_read).astype(BF16)
        a_r[at, :] = a
        h, d = gelu(dot(a, wr[...]))
        h_r[at, :] = h
        d_r[at, :] = d
        scores = dot(wsr[...], h, 1, 1)
        cols = slice(MEM, NCOL)
        if f in WRITES:
            at = write_rows(f)
            a = (xh * g_write).astype(BF16)
            a_w[at, :] = a
            h, d = gelu(dot(a, ww[...]))
            h_w[at, :] = h
            d_w[at, :] = d
            scores = jnp.concatenate([dot(wsw[...], h, 1, 1), scores], 0)
            cols = slice(0, NCOL)
        scores = jnp.where(lanes[cols], scores, -HUGE)
        best = row_max(scores)
        p = jnp.exp(scores - best)
        pb = p.astype(BF16)
        ps[f, cols] = pb
        stat[f, cols, 0:1] = best
        stat[f, cols, 1:2] = row_sum(p)
        rs[f, cols] = dot(pb, x)

    swap_in.wait()
    for f in range(frames):
        frame_forward(f)
    g_ffn = gains[3:4, :]

    mem[...] = jnp.zeros(mem.shape, F32)
    head_of = [(iota((1, D), 1) // HEAD == h) for h in range(HEADS)]
    same_clip = ((iota((HEADS * 32, 32), 0) // READ) % 2) == (iota((HEADS * 32, 32), 1) // READ)
    zero = jnp.zeros((), F32)

    def by_head(x):
        return jnp.concatenate([jnp.where(m, x, jnp.zeros_like(x)) for m in head_of], 0)

    def from_heads(x):
        total = jnp.where(head_of[0], x[:32], zero)
        for h in range(1, HEADS):
            total = total + jnp.where(head_of[h], x[32 * h : 32 * h + 32], zero)
        return total

    base_r = frames * ROWS
    base_w = len(WRITES) * ROWS
    base_k = base_w + 2 * 192

    def step_forward(t):
        live = t > 0
        last = t == 3
        if live:
            ml = mem[...].astype(BF16)
            mls[t - 1] = ml
            xh, r = norm(ml.astype(F32))
            mxh[t - 1] = xh
            mr[t - 1] = r
            at = slice(base_r + (t - 1) * 192, base_r + t * 192)
            a = (xh * g_read).astype(BF16)
            a_r[at, :] = a
            h, d = gelu(dot(a, wr[...]))
            h_r[at, :] = h
            d_r[at, :] = d
            if not last:
                at = slice(base_w + (t - 1) * 192, base_w + t * 192)
                a = (xh * g_write).astype(BF16)
                a_w[at, :] = a
                hw, d = gelu(dot(a, ww[...]))
                h_w[at, :] = hw
                d_w[at, :] = d
        z_parts = []
        for b in range(2):
            f = frame_index(b, t)
            m_f = stat[f, MEM:, 0:1]
            if live:
                s = dot(wsr[...], h[96 * b : 96 * b + 96], 1, 1)
                best = jnp.maximum(row_max(s), m_f)
                e = jnp.exp(s - best)
                part = row_sum(e)
            else:
                best = jnp.maximum(m_f, 0.0)
                part = MEM * jnp.exp(-best)
            w = jnp.exp(m_f - best)
            inv = 1.0 / (part + w * stat[f, MEM:, 1:2])
            stat[f, MEM:, 2:3] = w * inv
            z = (w * inv) * rs[f, MEM:, :]
            if live:
                al = (e * inv).astype(BF16)
                al_r[t - 1, b] = al
                z = z + dot(al, ml[96 * b : 96 * b + 96])
            z_parts.append(z)
        z = jnp.concatenate(z_parts, 0)
        zs[t] = z
        at = slice(32 * t, 32 * t + 32)
        xh, r = norm(z)
        xh1[t] = xh
        r1[t] = r
        u = (xh * g_attn).astype(BF16)
        us[at, :] = u
        q = dot(u, wqkv[0][...]).astype(BF16)
        k = dot(u, wqkv[1][...]).astype(BF16)
        v = dot(u, wqkv[2][...]).astype(BF16)
        qs[0, t] = q
        qs[1, t] = k
        qs[2, t] = v
        s = jnp.where(same_clip, dot(by_head(q), k, 1, 1) * (1.0 / math.sqrt(HEAD)), -HUGE)
        e = jnp.exp(s - row_max(s))
        p = (e / row_sum(e)).astype(BF16)
        prob[t] = p
        joined = from_heads(dot(p, v)).astype(BF16)
        att[at, :] = joined
        y = z + dot(joined, wo[...])
        xh, r = norm(y)
        xh2[t] = xh
        r2[t] = r
        n = (xh * g_ffn).astype(BF16)
        u2[at, :] = n
        o = y
        for j in range(4):
            g, d = gelu(dot(n, win[j][...]))
            gs[at, D * j : D * j + D] = g
            dg[t, :, D * j : D * j + D] = d
            o = o + dot(g, wout[D * j : D * j + D, :])
        tok = o.astype(BF16)
        toks[t] = tok
        if last:
            return
        xh, r = norm(tok.astype(F32))
        xhk[t] = xh
        rk[t] = r
        a = (xh * g_write).astype(BF16)
        at = slice(base_k + 32 * t, base_k + 32 * t + 32)
        a_w[at, :] = a
        hk, d = gelu(dot(a, ww[...]))
        h_w[at, :] = hk
        d_w[at, :] = d
        for b in range(2):
            f = frame_index(b, t)
            m_f = stat[f, :MEM, 0:1]
            s_tok = dot(wsw[...], hk[16 * b : 16 * b + 16], 1, 1)
            best = jnp.maximum(row_max(s_tok), m_f)
            if live:
                s = dot(wsw[...], hw[96 * b : 96 * b + 96], 1, 1)
                best = jnp.maximum(best, row_max(s))
                e = jnp.exp(s - best)
                part = row_sum(e)
            else:
                best = jnp.maximum(best, 0.0)
                part = MEM * jnp.exp(-best)
            e_tok = jnp.exp(s_tok - best)
            w = jnp.exp(m_f - best)
            inv = 1.0 / (part + row_sum(e_tok) + w * stat[f, :MEM, 1:2])
            stat[f, :MEM, 2:3] = w * inv
            al = (e_tok * inv).astype(BF16)
            al_t[t, b] = al
            new = (w * inv) * rs[f, :MEM, :] + dot(al, tok[16 * b : 16 * b + 16])
            if live:
                al = (e * inv).astype(BF16)
                al_m[t - 1, b] = al
                new = new + dot(al, ml[96 * b : 96 * b + 96])
            mnew[t, b] = new
            old = mem[96 * b : 96 * b + 96, :]
            mem[96 * b : 96 * b + 96, :] = jnp.where(flag_of[b][t], new, old)

    for t in range(4):
        step_forward(t)

    vecs[...] = jnp.zeros(vecs.shape, F32)
    acc_r[...] = jnp.zeros(acc_r.shape, F32)
    acc_w[...] = jnp.zeros(acc_w.shape, F32)
    dmem[...] = jnp.zeros(dmem.shape, F32)

    def add_vec(k, x):
        vecs[k : k + 1, :] = vecs[k : k + 1, :] + x

    def step_backward(t):
        live = t > 0
        last = t == 3
        gates = [jnp.where(flag_of[b][t], 1.0, 0.0) for b in range(2)]
        d_out = []
        for b in range(2):
            base = 4 * (t // 2)
            given = cot[b, base + 3]
            for i in range(3):
                given = jnp.where(slot_of[b][t] == i, cot[b, base + i], given)
            d_out.append(given.astype(F32) * gates[b])
        d_ml = []
        dh_mem = []
        keeps = []
        if last:
            for b in range(2):
                keeps.append(jnp.zeros((96, D), F32))
                d_ml.append(keeps[b])
        else:
            dh_tok = []
            at_k = slice(base_k + 32 * t, base_k + 32 * t + 32)
            hk = h_w[at_k, :]
            tok = toks[t]
            for b in range(2):
                f = frame_index(b, t)
                down = dmem[96 * b : 96 * b + 96, :]
                ds = (down * gates[b]).astype(BF16)
                keeps.append(down * (1.0 - gates[b]))
                dsc[f, :MEM, :] = ds
                c = row_sum(ds.astype(F32) * mnew[t, b])
                stat[f, :MEM, 3:4] = c
                al = al_t[t, b]
                rows_b = slice(16 * b, 16 * b + 16)
                d_out[b] = d_out[b] + dot(al, ds, 0, 0)
                back = (al.astype(F32) * (dot(ds, tok[rows_b], 1, 1) - c)).astype(BF16)
                dh_tok.append(dot(back, wsw[...], 0, 0))
                acc = dot(back, hk[rows_b])
                if live:
                    rows_b = slice(96 * b, 96 * b + 96)
                    ml = mls[t - 1, rows_b, :]
                    al = al_m[t - 1, b]
                    d_ml.append(dot(al, ds, 0, 0))
                    back = (al.astype(F32) * (dot(ds, ml, 1, 1) - c)).astype(BF16)
                    dh_mem.append(dot(back, wsw[...], 0, 0))
                    at = slice(base_w + (t - 1) * 192 + 96 * b, base_w + (t - 1) * 192 + 96 * b + 96)
                    acc = acc + dot(back, h_w[at, :])
                acc_w[...] = acc_w[...] + acc
            dgk = (jnp.concatenate(dh_tok, 0) * d_w[at_k, :].astype(F32)).astype(BF16)
            d_w[at_k, :] = dgk
            da = dot(dgk, ww[...], 1, 1)
            xh = xhk[t]
            add_vec(4, col_sum(da * xh))
            dx = norm_back(da * g_write, xh, rk[t])
            for b in range(2):
                d_out[b] = d_out[b] + dx[16 * b : 16 * b + 16]
        at = slice(32 * t, 32 * t + 32)
        do = jnp.concatenate(d_out, 0)
        dob = do.astype(BF16)
        dos[at, :] = dob
        dn = jnp.zeros((32, D), F32)
        for j in range(4):
            sl = slice(D * j, D * j + D)
            dp = (dot(dob, wout[sl, :], 1, 1) * dg[t, :, sl].astype(F32)).astype(BF16)
            dpre[at, sl] = dp
            dn = dn + dot(dp, win[j][...], 1, 1)
        add_vec(3, col_sum(dn * xh2[t]))
        dy = do + norm_back(dn * g_ffn, xh2[t], r2[t])
        dyb = dy.astype(BF16)
        dys[at, :] = dyb
        dbig = by_head(dot(dyb, wo[...], 1, 1).astype(BF16))
        p = prob[t]
        q, k, v = qs[0, t], qs[1, t], qs[2, t]
        dp = dot(dbig, v, 1, 1)
        pf = p.astype(F32)
        ds = (pf * (dp - row_sum(dp * pf)) * (1.0 / math.sqrt(HEAD))).astype(BF16)
        dv = dot(p, dbig, 0, 0).astype(BF16)
        dq = from_heads(dot(ds, k)).astype(BF16)
        dk = dot(ds, by_head(q), 0, 0).astype(BF16)
        dqs[0, at, :] = dq
        dqs[1, at, :] = dk
        dqs[2, at, :] = dv
        du = dot(dq, wqkv[0][...], 1, 1) + dot(dk, wqkv[1][...], 1, 1) + dot(dv, wqkv[2][...], 1, 1)
        add_vec(2, col_sum(du * xh1[t]))
        dz = dy + norm_back(du * g_attn, xh1[t], r1[t])
        dzb = dz.astype(BF16)
        c_all = row_sum(dzb.astype(F32) * zs[t])
        dh_r = []
        for b in range(2):
            f = frame_index(b, t)
            ds = dzb[16 * b : 16 * b + 16]
            c = c_all[16 * b : 16 * b + 16]
            dsc[f, MEM:, :] = ds
            stat[f, MEM:, 3:4] = c
            if live:
                rows_b = slice(96 * b, 96 * b + 96)
                al = al_r[t - 1, b]
                d_ml[b] = d_ml[b] + dot(al, ds, 0, 0)
                back = (al.astype(F32) * (dot(ds, mls[t - 1, rows_b, :], 1, 1) - c)).astype(BF16)
                dh_r.append(dot(back, wsr[...], 0, 0))
                at_b = slice(base_r + (t - 1) * 192 + 96 * b, base_r + (t - 1) * 192 + 96 * b + 96)
                acc_r[...] = acc_r[...] + dot(back, h_r[at_b, :])
        if not live:
            return
        at_m = slice(base_r + (t - 1) * 192, base_r + t * 192)
        xh = mxh[t - 1]
        dgr = (jnp.concatenate(dh_r, 0) * d_r[at_m, :].astype(F32)).astype(BF16)
        d_r[at_m, :] = dgr
        da = dot(dgr, wr[...], 1, 1)
        add_vec(1, col_sum(da * xh))
        g = da * g_read
        if not last:
            at_m = slice(base_w + (t - 1) * 192, base_w + t * 192)
            dgw = (jnp.concatenate(dh_mem, 0) * d_w[at_m, :].astype(F32)).astype(BF16)
            d_w[at_m, :] = dgw
            da = dot(dgw, ww[...], 1, 1)
            add_vec(4, col_sum(da * xh))
            g = g + da * g_write
        dx = norm_back(g, xh, mr[t - 1])
        for b in range(2):
            rows_b = slice(96 * b, 96 * b + 96)
            dmem[rows_b, :] = keeps[b] + d_ml[b] + dx[rows_b]

    for t in range(3, -1, -1):
        step_backward(t)

    for other in [sibling] + [(core, me + step) for step in all_steps[0]]:
        pl.semaphore_signal(ready, inc=1, device_id=other, device_id_type=MESH)
    flat[ROW_AOUT : ROW_AOUT + D, :] = dot(att[...], dys[...], 0, 0).astype(BF16)
    for j in range(4):
        sl = slice(D * j, D * j + D)
        flat[ROW_FOUT + D * j : ROW_FOUT + D * j + D, :] = dot(gs[:, sl], dos[...], 0, 0).astype(BF16)
    for row, count, left, right in (
        (ROW_QKV, 3, us, lambda j: dqs[j]),
        (ROW_FIN, 4, u2, lambda j: dpre[:, D * j : D * j + D]),
    ):
        for q in range(4):
            for j in range(count):
                part = dot(left[:, 128 * q : 128 * q + 128], right(j), 0, 0)
                for c in range(4):
                    planes[c, pl.ds(j, 128, stride=count), :] = part[:, 128 * c : 128 * c + 128]
            base = row + count * 128 * q
            for c in range(4):
                at = slice(128 * c, 128 * c + 128)
                flat[base : base + count * 128, at] = planes[c, : count * 128, :].astype(BF16)
    flat[ROW_AGAIN : ROW_AGAIN + 1, :] = vecs[2:3, :].astype(BF16)
    flat[ROW_FGAIN : ROW_FGAIN + 1, :] = vecs[3:4, :].astype(BF16)

    def place_of(p, r):
        start, size = parts[p][:2]
        return chips * start + r * size

    def side(p, r):
        return wbig.at[pl.ds(place_of(p, r), parts[p][1])]

    def slot(p, k, r):
        start, size = parts[p][:2]
        return (chips - 1) * start + ((1 << k) - 1 + r) * size

    def turns(top, end):
        return [(p, r) for r in range(top - 1, end - 1, -1) for p in range(len(parts))]


    def swap(p, r):
        index = (1 - core) * chips + shifted(me, other_steps[p], r)
        start = pl.multiple_of(block_of(index) + parts[p][0], BLOCK)
        src = flat.at[pl.ds(start, parts[p][1])]
        return remote(src, side(p, r), sibsend.at[p, r], sibrecv.at[p, r], sibling), index

    def send_on(p, r):
        top = r.bit_length() - 1
        low = r - (1 << top)
        return remote(
            side(p, r),
            held.at[pl.ds(slot(p, top, low), parts[p][1])],
            send.at[p, r],
            recv.at[p, (1 << top) - 1 + low],
            (core, me + all_steps[p][top]),
        )

    def swap_all(late):
        for p, r in turns(chips, 0):
            copy, index = swap(p, r)

            @pl.when(is_outer(index) == late)
            def _(copy=copy):
                copy.start()

    def turn(p, r, late):
        index = core * chips + shifted(me, all_steps[p], r)
        start, size = parts[p][:2]

        @pl.when(is_outer(index) == late)
        def _():
            swap(p, r)[0].wait_recv()
            slots = []
            for k in range(bits - 1, r.bit_length() - 1, -1):
                at = held.at[pl.ds(slot(p, k, r), size)]
                remote(at, at, send.at[p, r], recv.at[p, (1 << k) - 1 + r], sibling).wait_recv()
                slots.append(slot(p, k, r))
            base = block_of(index) + start

            def add(i, carry):
                step = i * BLOCK
                at = pl.ds(pl.multiple_of(place_of(p, r) + step, BLOCK), BLOCK)
                mine = flat[pl.ds(pl.multiple_of(base + step, BLOCK), BLOCK), :]
                value = mine.astype(F32) + wbig[at, :].astype(F32)
                for one in slots:
                    value = value + held[pl.ds(pl.multiple_of(one + step, BLOCK), BLOCK), :].astype(F32)
                if r == 0:
                    for c in range(4):
                        spots = pl.ds(4 * (start + step) + c, BLOCK, stride=4)
                        total[spots, :] = value[:, 128 * c : 128 * c + 128]
                else:
                    wbig[at, :] = value.astype(BF16)
                return carry

            lax.fori_loop(0, size // BLOCK, add, 0)
            if r > 0:
                send_on(p, r).start()

    def frame_backward(f):
        at = slice(f * ROWS, f * ROWS + ROWS)
        x = xs[f]
        cols = slice(0 if f in WRITES else MEM, NCOL)
        ds = dsc[f, cols]
        al = ps[f, cols].astype(F32) * stat[f, cols, 2:3]
        alb = al.astype(BF16)
        back = (al * (dot(ds, x, 1, 1) - stat[f, cols, 3:4])).astype(BF16)
        back_r = back[-READ:]
        acc_r[...] = acc_r[...] + dot(back_r, h_r[at, :])
        xh, r = norm(x.astype(F32))
        dgr = (dot(back_r, wsr[...], 0, 0) * d_r[at, :].astype(F32)).astype(BF16)
        d_r[at, :] = dgr
        da = dot(dgr, wr[...], 1, 1)
        add_vec(1, col_sum(da * xh))
        g = da * g_read
        if f in WRITES:
            at = write_rows(f)
            acc_w[...] = acc_w[...] + dot(back[:MEM], h_w[at, :])
            dgw = (dot(back[:MEM], wsw[...], 0, 0) * d_w[at, :].astype(F32)).astype(BF16)
            d_w[at, :] = dgw
            da = dot(dgw, ww[...], 1, 1)
            add_vec(4, col_sum(da * xh))
            g = g + da * g_write
        dx = (dot(alb, ds, 0, 0) + norm_back(g, xh, r)).astype(BF16)
        xs[f] = dx
        add_vec(0, col_sum(dx.astype(F32)))
        to = jnp.where(core == f // 4, 0, 4) + f % 4
        pg[to] = dot(dx, wp[...], 1, 1).astype(BF16)

    pl.semaphore_wait(ready, bits + 1)
    swap_all(False)
    half = chips // 2
    todo = turns(chips, half)
    every = len(todo) // frames
    for i, (p, r) in enumerate(todo):
        if i % every == 0 and i // every < frames:
            frame_backward(i // every)
        turn(p, r, False)
    quarter = chips // 4
    for p, r in turns(half, quarter):
        turn(p, r, False)

    swap_pix = remote(pg.at[pl.ds(4, 4)], pgout, pixsem.at[0], pixsem.at[1], sibling)
    swap_pix.start()
    n = 4 * ROWS
    flat[ROW_PATCH : ROW_PATCH + PIN, :] = (
        dot(pix[...].reshape(n, PIN), xs[pl.ds(4 * core, 4)].reshape(n, D), 0, 0)
        + dot(far[...].reshape(n, PIN), xs[pl.ds(4 - 4 * core, 4)].reshape(n, D), 0, 0)
    ).astype(BF16)
    flat[ROW_RHID : ROW_RHID + D, :] = dot(a_r[...], d_r[...], 0, 0).astype(BF16)
    flat[ROW_WHID : ROW_WHID + D, :] = dot(a_w[...], d_w[...], 0, 0).astype(BF16)
    where, chosen, spread = score_masks(READ, 0)
    wide = dot(acc_r[...].astype(BF16), chosen, 0, 0).astype(BF16) * where
    flat[ROW_RSCORE : ROW_RSCORE + READ, :] = dot(spread, wide, 0, 0).astype(BF16)
    for part in range(3):
        where, chosen, spread = score_masks(MEM, part)
        wide = dot(acc_w[...].astype(BF16), chosen, 0, 0).astype(BF16) * where
        these = dot(spread, wide, 0, 0)
        for c in range(4):
            planes[c, pl.ds(part, 32, stride=3), :] = these[:, 128 * c : 128 * c + 128]
    for c in range(4):
        at = slice(128 * c, 128 * c + 128)
        flat[ROW_WSCORE : ROW_WSCORE + MEM, at] = planes[c, :MEM, :].astype(BF16)
    for k, row in ((0, ROW_BIAS), (1, ROW_RGAIN), (4, ROW_WGAIN)):
        flat[row : row + 1, :] = vecs[k : k + 1, :].astype(BF16)
    flat[ROW_END:, :] = jnp.zeros((flat.shape[0] - ROW_END, D), BF16)

    swap_all(True)
    for b in range(2):
        for s in range(STEPS):
            value = jnp.zeros((READ, D), BF16)
            for t in (s // 4 * 2, s // 4 * 2 + 1):
                hit = (slot_of[b][t] == s % 4) & flag_of[b][t]
                value = jnp.where(hit, toks[t, READ * b : READ * b + READ, :], value)
            done[b, s] = value
    for p, r in turns(chips, half):
        turn(p, r, True)
    for p, r in turns(half, quarter):
        turn(p, r, True)
    for p, r in turns(quarter, 0):
        turn(p, r, False)
        turn(p, r, True)
    for p, r in turns(chips, 0):
        swap(p, r)[0].wait_send()
        if r > 0:
            send_on(p, r).wait_send()
    swap_pix.wait()


def main(own, pixels, cot, owner, counts, mask, chips, length):
    rows = own.shape[0]
    height = (2 * chips - 1) * length // (BLOCK * D) * BLOCK + rows
    n = 8 * ROWS
    vmem = pl.BlockSpec(memory_space=pltpu.VMEM)
    smem = pl.BlockSpec(memory_space=pltpu.SMEM)
    hbm = pl.BlockSpec(memory_space=pl.ANY)
    v = pltpu.VMEM
    dma = pltpu.SemaphoreType.DMA
    return pl.pallas_call(
        functools.partial(main_kernel, chips, length),
        out_shape=(
            jax.ShapeDtypeStruct((2, STEPS, READ, D), BF16),
            jax.ShapeDtypeStruct((8, ROWS, PIN), BF16),
            jax.ShapeDtypeStruct((4 * rows, 128), F32),
            jax.ShapeDtypeStruct((4, ROWS, PIN), BF16),
        ),
        in_specs=[smem, smem, smem, vmem, hbm, vmem],
        out_specs=[vmem, vmem, vmem, hbm],
        scratch_shapes=[
            v((height, D), BF16),
            v((4, D, 128), F32),
            v((PIN, D), BF16),
            v((D, D), BF16),
            v((D, D), BF16),
            v((max(12 * D, chips * rows), D), BF16),
            v((READ, D), BF16),
            v((MEM, D), BF16),
            v((8, D), F32),
            v((8, ROWS, D), BF16),
            v((n + 576, D), BF16),
            v((n - 2 * ROWS + 480, D), BF16),
            v((n + 576, D), BF16),
            v((n - 2 * ROWS + 480, D), BF16),
            v((n + 576, D), BF16),
            v((n - 2 * ROWS + 480, D), BF16),
            v((8, NCOL, ROWS), BF16),
            v((8, NCOL, D), F32),
            v((8, NCOL, 8), F32),
            v((8, NCOL, D), BF16),
            v((192, D), F32),
            v((192, D), F32),
            v((3, 192, D), BF16),
            v((3, 192, D), F32),
            v((3, 192, 1), F32),
            v((3, 2, MEM, D), F32),
            v((3, 2, READ, MEM), BF16),
            v((2, 2, MEM, MEM), BF16),
            v((3, 2, MEM, READ), BF16),
            v((4, 32, D), F32),
            v((4, 32, D), F32),
            v((4, 32, 1), F32),
            v((128, D), BF16),
            v((3, 4, 32, D), BF16),
            v((4, HEADS * 32, 32), BF16),
            v((128, D), BF16),
            v((4, 32, D), F32),
            v((4, 32, 1), F32),
            v((128, D), BF16),
            v((128, FFN), BF16),
            v((4, 32, FFN), BF16),
            v((4, 32, D), BF16),
            v((3, 32, D), F32),
            v((3, 32, 1), F32),
            v((3, 128, D), BF16),
            v((128, D), BF16),
            v((128, FFN), BF16),
            v((128, D), BF16),
            v((READ, D), F32),
            v((MEM, D), F32),
            v((8, D), F32),
            v((4, ROWS, PIN), BF16),
            v((4, ROWS, PIN), BF16),
            v((2, P_SIZE, 4, PIN), BF16),
            v((max((chips - 1) * rows, 4 * chips * BLOCK), D), BF16),
            dma((2, 2)),
            dma((PARTS, chips)),
            dma((PARTS, chips)),
            dma((PARTS, chips)),
            dma((PARTS, chips)),
            dma((PARTS, chips)),
            dma((PARTS, chips)),
            dma((4,)),
            pltpu.SemaphoreType.REGULAR,
        ],
        compiler_params=pltpu.CompilerParams(
            collective_id=0, has_side_effects=True, vmem_limit_bytes=VMEM_LIMIT
        ),
        name="model",
    )(owner, counts, mask, own, pixels, cot)


def body(pixels, counts, step_mask, owner, params, cotangent):
    chips = lax.axis_size("dp")
    length = params.shape[0]
    core = lax.axis_index("grp").astype(jnp.int32)
    dp = lax.axis_index("dp").astype(jnp.int32)
    counts = counts[:, :, 0]
    mask = step_mask[:, :, 0]
    owner = owner[:, 0]

    rows = window_rows(length)
    offset = ((core * chips + dp) * length) % (BLOCK * D)
    wide = jnp.pad(params, (BLOCK * D, rows * D - length))
    win = lax.dynamic_slice(wide, (BLOCK * D - offset,), (rows * D,)).reshape(rows, D)

    cot = cotangent[:, 0, 0]
    done, near_grad, total, far_grad = main(
        win, jnp.swapaxes(pixels, 3, 4), cot, owner, counts, mask, chips, length
    )
    shard_grad = lax.dynamic_slice(total.reshape(rows * D), (offset,), (length,))
    pixel_grad = place(near_grad, far_grad, owner, counts, mask, pixels.shape)
    return (done[:, None, None], pixel_grad, shard_grad)


def solution(mesh):
    return jax.shard_map(
        body,
        mesh=mesh,
        in_specs=(
            P(None, None, "dp", "grp", None, None),
            P(None, None, "dp"),
            P(None, None, "dp", None),
            P(None, "dp"),
            P(("grp", "dp")),
            P(None, "grp", "dp", None, None, None),
        ),
        out_specs=(
            P(None, "grp", "dp", None, None, None),
            P(None, None, "dp", "grp", None, None),
            P(("grp", "dp")),
        ),
        check_vma=False,
    )
```

```python
import functools
import math

import jax
import jax.numpy as jnp
from jax import lax
from jax.experimental import pallas as pl
from jax.experimental.pallas import tpu as pltpu
from jax.sharding import PartitionSpec as P

MESH = pl.DeviceIdType.MESH
F32 = jnp.float32
BF16 = jnp.bfloat16

D = 512
HEADS = 8
HEAD = D // HEADS
FFN = 2048
PIN = 768
P_SIZE = 196
ROWS = 208
MEM = 96
READ = 16
NCOL = MEM + READ
STEPS = 8
BLOCK = 16
EPS = 1e-6
PARTS = 3
HUGE = 1e30
HALF_INT = 1 << 30

ROW_PATCH = 0
ROW_BIAS = 768
ROW_RGAIN = 769
ROW_RHID = 770
ROW_RSCORE = 1282
ROW_AGAIN = 1298
ROW_QKV = 1299
ROW_AOUT = 2835
ROW_FGAIN = 3347
ROW_FIN = 3348
ROW_FOUT = 5396
ROW_WGAIN = 7444
ROW_WHID = 7445
ROW_WSCORE = 7957
ROW_END = 8053

VMEM_LIMIT = 63 * 2**20


def dot(a, b, ca=1, cb=0):
    return lax.dot_general(a, b, (((ca,), (cb,)), ((), ())), preferred_element_type=F32)


def window_rows(length):
    return (length + BLOCK * D - 2) // (BLOCK * D) * BLOCK + BLOCK


def first_block(index, length):
    return (index * length) // (BLOCK * D)


def parts_of(chips, rows):
    bits = chips.bit_length() - 1
    high = list(range(bits - 1, 1, -1))
    blocks = rows // BLOCK
    b = blocks * 2 // 3 * BLOCK
    return [
        (0, b, high + [0, 1], high + [1, 0]),
        (b, rows - b, [0, 1] + high, [1, 0] + high),
    ]


def partners(orders, core, me):
    steps = []
    for one, two in zip(*orders):
        a = (1 - 2 * ((me // (1 << one)) % 2)) * (1 << one)
        b = (1 - 2 * ((me // (1 << two)) % 2)) * (1 << two)
        steps.append(a + core * (b - a))
    return steps


def shifted(me, steps, r):
    at = me
    for k, step in enumerate(steps):
        if (r >> k) & 1:
            at = at + step
    return at


def greet(core, me, steps):
    barrier = pltpu.get_barrier_semaphore()
    places = [(core, me + step) for step in steps] + [(1 - core, me)]
    for place in places:
        pl.semaphore_signal(barrier, inc=1, device_id=place, device_id_type=MESH)
    pl.semaphore_wait(barrier, len(places))


def remote(src, dst, s, r, place):
    return pltpu.make_async_remote_copy(
        src_ref=src, dst_ref=dst, send_sem=s, recv_sem=r, device_id=place, device_id_type=MESH
    )


CHUNK = 64
FULL = P_SIZE // CHUNK * CHUNK
TAIL = P_SIZE - FULL


def kept(counts, mask, m, g, half):
    base = half * (STEPS // 2)
    ok = [(mask[m, g, base + i] == 1) & (base + i < counts[m, g]) for i in range(4)]
    last = jnp.int32
    first = jnp.where(ok[0], 0, jnp.where(ok[1], 1, jnp.where(ok[2], 2, 3))).astype(last)
    second = jnp.where(ok[3], 3, jnp.where(ok[2], 2, jnp.where(ok[1], 1, 0))).astype(last)
    number = sum(o.astype(jnp.int32) for o in ok)
    return (first, second), (number > 0, number > 1)


def place_kernel(owner, counts, mask, near, far, out):
    m, g = pl.program_id(0), pl.program_id(1)
    core = lax.axis_index("grp")
    is_near = (core + owner[m]) % 2 == g
    slots, flags = kept(counts, mask, m, g, core)
    where = [jnp.where(flag, slot, -HALF_INT) for slot, flag in zip(slots, flags)]

    def spread(rows, cols):
        one = [(iota((rows, cols), 0) == 4 * iota((rows, cols), 1) + s).astype(BF16) for s in where]
        return jnp.concatenate(one, 1)

    def to_slots(first, count, weights):
        at = slice(first, first + count)
        these = [jnp.where(is_near, near[0, j, at], far[0, j, at]) for j in range(2)]
        return dot(weights, jnp.concatenate(these, 0)).astype(BF16)

    whole = spread(4 * CHUNK, CHUNK)
    for c in range(FULL // CHUNK):
        got = to_slots(CHUNK * c, CHUNK, whole)
        out[0, 0, 0, CHUNK * c : CHUNK * c + CHUNK] = got.reshape(CHUNK, 4, PIN)
    got = to_slots(FULL, ROWS - FULL, spread(4 * TAIL, ROWS - FULL))
    out[0, 0, 0, FULL:] = got.reshape(TAIL, 4, PIN)


def place(near, far, owner, counts, mask, shape):
    m, g, c, s, rows, cols = shape
    out = pl.pallas_call(
        place_kernel,
        out_shape=jax.ShapeDtypeStruct((m, g, c, rows, s, cols), BF16),
        grid_spec=pltpu.PrefetchScalarGridSpec(
            num_scalar_prefetch=3,
            grid=(2, 2),
            in_specs=[pl.BlockSpec((1, 2, ROWS, PIN), lambda m, g, *_: (m, 0, 0, 0))] * 2,
            out_specs=pl.BlockSpec(
                (1, 1, 1, rows, s, cols), lambda m, g, *_: (m, g, 0, 0, 0, 0)
            ),
        ),
        compiler_params=pltpu.CompilerParams(vmem_limit_bytes=VMEM_LIMIT),
        name="place",
    )(owner, counts, mask, near.reshape(2, 2, ROWS, PIN), far.reshape(2, 2, ROWS, PIN))
    return jnp.swapaxes(out, 3, 4)


def frame_index(clip, step):
    return (step // 2) * 4 + clip * 2 + step % 2


WRITES = sorted(frame_index(clip, step) for clip in range(2) for step in range(3))


def norm(x):
    mean = jnp.mean(x, -1, keepdims=True)
    centered = x - mean
    r = lax.rsqrt(jnp.mean(centered * centered, -1, keepdims=True) + EPS)
    return centered * r, r


def norm_back(g, xh, r):
    return r * (g - jnp.mean(g, -1, keepdims=True) - xh * jnp.mean(g * xh, -1, keepdims=True))


def gelu(x):
    cdf = 0.5 + 0.5 * lax.erf(x * math.sqrt(0.5))
    slope = cdf + x * (jnp.exp(-0.5 * x * x) * (1.0 / math.sqrt(2.0 * math.pi)))
    return (x * cdf).astype(BF16), slope.astype(BF16)


def col_sum(x):
    return jnp.sum(x, 0, keepdims=True)


def row_sum(x):
    return jnp.sum(x, -1, keepdims=True)


def row_max(x):
    return jnp.max(x, -1, keepdims=True)


def iota(shape, dim):
    return lax.broadcasted_iota(jnp.int32, shape, dim)


def score_masks(width, part):
    group = 512 // math.gcd(512, width)
    lane = iota((D, D), 1) + 512 * part
    hidden = iota((D, D), 0)
    where = ((hidden % group) == (lane // width)).astype(BF16)
    lane = iota((width, D), 1) + 512 * part
    pick = ((lane % width) == iota((width, D), 0)).astype(BF16)
    rows = 512 // group
    spread = ((iota((D, rows), 0) // group) == iota((D, rows), 1)).astype(BF16)
    return where, pick, spread


def main_kernel(
    chips,
    length,
    owner,
    counts,
    mask,
    own,
    pixels,
    cot,
    done,
    near,
    total,
    pgout,
    flat,
    planes,
    wp,
    wr,
    ww,
    wbig,
    wsr,
    wsw,
    gains,
    xs,
    a_r,
    a_w,
    h_r,
    h_w,
    d_r,
    d_w,
    ps,
    rs,
    stat,
    dsc,
    mem,
    dmem,
    mls,
    mxh,
    mr,
    mnew,
    al_r,
    al_m,
    al_t,
    zs,
    xh1,
    r1,
    us,
    qs,
    prob,
    att,
    xh2,
    r2,
    u2,
    gs,
    dg,
    toks,
    xhk,
    rk,
    dqs,
    dys,
    dpre,
    dos,
    acc_r,
    acc_w,
    vecs,
    pix,
    far,
    stage,
    pg,
    held,
    stage_sem,
    grecv,
    gsibrecv,
    send,
    recv,
    sibsend,
    sibrecv,
    pixsem,
    ready,
):
    rows = own.shape[0]
    frames = 8
    core = lax.axis_index("grp")
    me = lax.axis_index("dp")
    sibling = (1 - core, me)
    parts = parts_of(chips, rows)
    bits = chips.bit_length() - 1
    all_steps = [partners(part[2:], core, me) for part in parts]
    other_steps = [partners(part[2:], 1 - core, me) for part in parts]
    mine = core * chips + me

    def load(m, g):
        return pltpu.make_async_copy(pixels.at[m, g, 0], stage.at[g], stage_sem.at[m, g])

    for g in range(2):
        load(0, g).start()
    greet(core, me, all_steps[0])

    def block_of(index):
        return first_block(index, length) * BLOCK

    def is_outer(index):
        start = block_of(index)
        return (start < ROW_QKV) | (start + rows > ROW_WGAIN)

    inner = rows - 2 * BLOCK
    cut = (inner // BLOCK * 3 + 2) // 4 * BLOCK
    pieces = [parts[0][2:], parts[-1][2:], parts[0][2:]]
    own_steps = [partners(orders, core, me) for orders in pieces]
    side_steps = [partners(orders, 1 - core, me) for orders in pieces]

    def piece(p, index):
        start = block_of(index) + BLOCK
        if p == 0:
            return flat.at[pl.ds(pl.multiple_of(start, BLOCK), cut)]
        if p == 1:
            return flat.at[pl.ds(pl.multiple_of(start + cut, BLOCK), inner - cut)]
        return held.at[pl.ds(pl.multiple_of(index * 2 * BLOCK, BLOCK), 2 * BLOCK)]

    def pass_on(p, r):
        steps = own_steps[p]
        at = piece(p, core * chips + shifted(me, steps, r))
        copies = []
        for k in range(bits - 1, r.bit_length() - 1, -1):
            to = (core, me + steps[k])
            copies.append(
                remote(at, at, send.at[p, (1 << k) - 1 + r], grecv.at[p, r | (1 << k)], to)
            )
        copies.append(remote(at, at, sibsend.at[p, r], gsibrecv.at[p, r], sibling))
        return copies

    def start_all(copies):
        for copy in copies:
            copy.start()

    def at_distance(c):
        return [(p, r) for r in range(chips) if bin(r).count("1") == c for p in range(3)]

    def arrive(p, r):
        at = piece(p, core * chips + shifted(me, own_steps[p], r))
        remote(at, at, send.at[p, 0], grecv.at[p, r], sibling).wait_recv()
        start_all(pass_on(p, r))

    def arrive_side(p, r):
        at = piece(p, (1 - core) * chips + shifted(me, side_steps[p], r))
        remote(at, at, sibsend.at[p, 0], gsibrecv.at[p, r], sibling).wait_recv()

    def pick(m):
        chosen = []
        for g in range(2):
            load(m, g).wait()
            kept_slots, _ = kept(counts, mask, m, g, core)
            chosen.append(
                [
                    jnp.concatenate(
                        [
                            (iota((a, b), 1) == 4 * iota((a, b), 0) + one).astype(BF16)
                            for one in kept_slots
                        ],
                        0,
                    )
                    for a, b in ((CHUNK, 4 * CHUNK), (ROWS - FULL, 4 * TAIL))
                ]
            )
        for c in range(FULL // CHUNK + 1):
            first = CHUNK * c
            size = CHUNK if first < FULL else ROWS - FULL
            count = CHUNK if first < FULL else TAIL
            got = [
                dot(
                    chosen[g][0 if first < FULL else 1],
                    stage[g, first : first + count].reshape(4 * count, PIN),
                ).astype(BF16)
                for g in range(2)
            ]
            for j in range(2):
                a, b = (got[g][size * j : size * j + size] for g in range(2))
                pix[2 * m + j, first : first + size] = jnp.where((core + owner[m]) % 2 == 0, a, b)
                pg[4 + 2 * m + j, first : first + size] = jnp.where((core + owner[m]) % 2 == 0, b, a)

    start = pl.multiple_of(block_of(mine), BLOCK)
    flat[pl.ds(pl.multiple_of(start + BLOCK, BLOCK), inner), :] = own[BLOCK : BLOCK + inner, :]
    at = pl.multiple_of(mine * 2 * BLOCK, BLOCK)
    held[pl.ds(at, BLOCK), :] = own[:BLOCK, :]
    held[pl.ds(pl.multiple_of(at + BLOCK, BLOCK), BLOCK), :] = own[rows - BLOCK :, :]
    for p in range(3):
        start_all(pass_on(p, 0))
    swap_in = remote(pg.at[pl.ds(4, 4)], far, pixsem.at[2], pixsem.at[3], sibling)
    pick(0)
    for g in range(2):
        load(1, g).start()
    for c in range(1, bits + 1):
        for p, r in at_distance(c):
            arrive(p, r)
        if c == 1:
            pick(1)
            swap_in.start()
        for p, r in at_distance(c - 1):
            arrive_side(p, r)
    for p, r in at_distance(bits):
        arrive_side(p, r)
    for r in range(chips):
        for p in range(3):
            for copy in pass_on(p, r):
                copy.wait_send()

    slot_of = []
    flag_of = []
    for b in range(2):
        pairs = [kept(counts, mask, b, (core + owner[b]) % 2, half) for half in range(2)]
        slot_of.append([pairs[t // 2][0][t % 2] for t in range(4)])
        flag_of.append([pairs[t // 2][1][t % 2] for t in range(4)])

    wo = wbig.at[0:D]
    wqkv = [wbig.at[D + D * j : 2 * D + D * j] for j in range(3)]
    win = [wbig.at[4 * D + D * j : 5 * D + D * j] for j in range(4)]
    wout = wbig.at[8 * D : 12 * D]

    count = 2 * chips

    def strip(index, b):
        return held[index * 2 * BLOCK + b : index * 2 * BLOCK + b + BLOCK, :]

    def join(i):
        a, b = block_of(i), block_of(i + 1)
        at = slice(b, b + BLOCK)
        before = strip(i, BLOCK) if b - a == rows - BLOCK else flat[at, :]
        flat[at, :] = before + strip(i + 1, 0)

    def gain(k, row):
        base = row // BLOCK * BLOCK
        gains[k : k + 1, :] = flat[base : base + BLOCK, :].astype(F32)[row - base : row - base + 1, :]

    flat[:BLOCK, :] = strip(0, 0)
    end = block_of(count - 1) + rows
    flat[end - BLOCK : end, :] = strip(count - 1, BLOCK)
    for i in range(count - 1):
        join(i)
    wp[...] = flat[ROW_PATCH : ROW_PATCH + PIN, :]
    wr[...] = flat[ROW_RHID : ROW_RHID + D, :]
    ww[...] = flat[ROW_WHID : ROW_WHID + D, :]
    for k, row in enumerate((ROW_BIAS, ROW_RGAIN, ROW_AGAIN, ROW_FGAIN, ROW_WGAIN)):
        gain(k, row)
    where, chosen, spread = score_masks(READ, 0)
    wide = dot(spread, flat[ROW_RSCORE : ROW_RSCORE + READ, :]).astype(BF16) * where
    wsr[...] = dot(chosen, wide, 1, 1).astype(BF16)
    scores = jnp.zeros((MEM, D), F32)
    for c in range(4):
        at = slice(c * 128, c * 128 + 128)
        planes[c, :MEM, :] = flat[ROW_WSCORE : ROW_WSCORE + MEM, at].astype(F32)
    for part in range(3):
        where, chosen, spread = score_masks(MEM, part)
        these = jnp.concatenate(
            [planes[c, pl.ds(part, 32, stride=3), :] for c in range(4)], -1
        ).astype(BF16)
        wide = dot(spread, these).astype(BF16) * where
        scores = scores + dot(chosen, wide, 1, 1)
    wsw[...] = scores.astype(BF16)

    wo[...] = flat[ROW_AOUT : ROW_AOUT + D, :]
    wout[...] = flat[ROW_FOUT : ROW_FOUT + FFN, :]
    for row, parts_j, dst in ((ROW_QKV, 3, wqkv), (ROW_FIN, 4, win)):
        for q in range(4):
            base = row + parts_j * 128 * q
            for c in range(4):
                at = slice(c * 128, c * 128 + 128)
                planes[c, : parts_j * 128, :] = flat[base : base + parts_j * 128, at].astype(F32)
                for j in range(parts_j):
                    these = planes[c, pl.ds(j, 128, stride=parts_j), :]
                    dst[j][128 * q : 128 * q + 128, at] = these.astype(BF16)

    bias = gains[0:1, :]
    g_read = gains[1:2, :]
    g_attn = gains[2:3, :]
    g_write = gains[4:5, :]

    lanes = iota((NCOL, ROWS), 1) < P_SIZE

    def write_rows(f):
        first = WRITES.index(f) * ROWS
        return slice(first, first + ROWS)

    def frame_forward(f):
        at = slice(f * ROWS, f * ROWS + ROWS)
        seen = jnp.where(f // 4 == core, pix[f % 4], far[f % 4])
        x = (dot(seen, wp[...]) + bias).astype(BF16)
        xs[f] = x
        xh, r = norm(x.astype(F32))
        a = (xh * g_read).astype(BF16)
        a_r[at, :] = a
        h, d = gelu(dot(a, wr[...]))
        h_r[at, :] = h
        d_r[at, :] = d
        scores = dot(wsr[...], h, 1, 1)
        cols = slice(MEM, NCOL)
        if f in WRITES:
            at = write_rows(f)
            a = (xh * g_write).astype(BF16)
            a_w[at, :] = a
            h, d = gelu(dot(a, ww[...]))
            h_w[at, :] = h
            d_w[at, :] = d
            scores = jnp.concatenate([dot(wsw[...], h, 1, 1), scores], 0)
            cols = slice(0, NCOL)
        scores = jnp.where(lanes[cols], scores, -HUGE)
        best = row_max(scores)
        p = jnp.exp(scores - best)
        pb = p.astype(BF16)
        ps[f, cols] = pb
        stat[f, cols, 0:1] = best
        stat[f, cols, 1:2] = row_sum(p)
        rs[f, cols] = dot(pb, x)

    swap_in.wait()
    for f in range(frames):
        frame_forward(f)
    g_ffn = gains[3:4, :]

    mem[...] = jnp.zeros(mem.shape, F32)
    head_of = [(iota((1, D), 1) // HEAD == h) for h in range(HEADS)]
    same_clip = ((iota((HEADS * 32, 32), 0) // READ) % 2) == (iota((HEADS * 32, 32), 1) // READ)
    zero = jnp.zeros((), F32)

    def by_head(x):
        return jnp.concatenate([jnp.where(m, x, jnp.zeros_like(x)) for m in head_of], 0)

    def from_heads(x):
        total = jnp.where(head_of[0], x[:32], zero)
        for h in range(1, HEADS):
            total = total + jnp.where(head_of[h], x[32 * h : 32 * h + 32], zero)
        return total

    base_r = frames * ROWS
    base_w = len(WRITES) * ROWS
    base_k = base_w + 2 * 192

    def step_forward(t):
        live = t > 0
        last = t == 3
        if live:
            ml = mem[...].astype(BF16)
            mls[t - 1] = ml
            xh, r = norm(ml.astype(F32))
            mxh[t - 1] = xh
            mr[t - 1] = r
            at = slice(base_r + (t - 1) * 192, base_r + t * 192)
            a = (xh * g_read).astype(BF16)
            a_r[at, :] = a
            h, d = gelu(dot(a, wr[...]))
            h_r[at, :] = h
            d_r[at, :] = d
            if not last:
                at = slice(base_w + (t - 1) * 192, base_w + t * 192)
                a = (xh * g_write).astype(BF16)
                a_w[at, :] = a
                hw, d = gelu(dot(a, ww[...]))
                h_w[at, :] = hw
                d_w[at, :] = d
        z_parts = []
        for b in range(2):
            f = frame_index(b, t)
            m_f = stat[f, MEM:, 0:1]
            if live:
                s = dot(wsr[...], h[96 * b : 96 * b + 96], 1, 1)
                best = jnp.maximum(row_max(s), m_f)
                e = jnp.exp(s - best)
                part = row_sum(e)
            else:
                best = jnp.maximum(m_f, 0.0)
                part = MEM * jnp.exp(-best)
            w = jnp.exp(m_f - best)
            inv = 1.0 / (part + w * stat[f, MEM:, 1:2])
            stat[f, MEM:, 2:3] = w * inv
            z = (w * inv) * rs[f, MEM:, :]
            if live:
                al = (e * inv).astype(BF16)
                al_r[t - 1, b] = al
                z = z + dot(al, ml[96 * b : 96 * b + 96])
            z_parts.append(z)
        z = jnp.concatenate(z_parts, 0)
        zs[t] = z
        at = slice(32 * t, 32 * t + 32)
        xh, r = norm(z)
        xh1[t] = xh
        r1[t] = r
        u = (xh * g_attn).astype(BF16)
        us[at, :] = u
        q = dot(u, wqkv[0][...]).astype(BF16)
        k = dot(u, wqkv[1][...]).astype(BF16)
        v = dot(u, wqkv[2][...]).astype(BF16)
        qs[0, t] = q
        qs[1, t] = k
        qs[2, t] = v
        s = jnp.where(same_clip, dot(by_head(q), k, 1, 1) * (1.0 / math.sqrt(HEAD)), -HUGE)
        e = jnp.exp(s - row_max(s))
        p = (e / row_sum(e)).astype(BF16)
        prob[t] = p
        joined = from_heads(dot(p, v)).astype(BF16)
        att[at, :] = joined
        y = z + dot(joined, wo[...])
        xh, r = norm(y)
        xh2[t] = xh
        r2[t] = r
        n = (xh * g_ffn).astype(BF16)
        u2[at, :] = n
        o = y
        for j in range(4):
            g, d = gelu(dot(n, win[j][...]))
            gs[at, D * j : D * j + D] = g
            dg[t, :, D * j : D * j + D] = d
            o = o + dot(g, wout[D * j : D * j + D, :])
        tok = o.astype(BF16)
        toks[t] = tok
        if last:
            return
        xh, r = norm(tok.astype(F32))
        xhk[t] = xh
        rk[t] = r
        a = (xh * g_write).astype(BF16)
        at = slice(base_k + 32 * t, base_k + 32 * t + 32)
        a_w[at, :] = a
        hk, d = gelu(dot(a, ww[...]))
        h_w[at, :] = hk
        d_w[at, :] = d
        for b in range(2):
            f = frame_index(b, t)
            m_f = stat[f, :MEM, 0:1]
            s_tok = dot(wsw[...], hk[16 * b : 16 * b + 16], 1, 1)
            best = jnp.maximum(row_max(s_tok), m_f)
            if live:
                s = dot(wsw[...], hw[96 * b : 96 * b + 96], 1, 1)
                best = jnp.maximum(best, row_max(s))
                e = jnp.exp(s - best)
                part = row_sum(e)
            else:
                best = jnp.maximum(best, 0.0)
                part = MEM * jnp.exp(-best)
            e_tok = jnp.exp(s_tok - best)
            w = jnp.exp(m_f - best)
            inv = 1.0 / (part + row_sum(e_tok) + w * stat[f, :MEM, 1:2])
            stat[f, :MEM, 2:3] = w * inv
            al = (e_tok * inv).astype(BF16)
            al_t[t, b] = al
            new = (w * inv) * rs[f, :MEM, :] + dot(al, tok[16 * b : 16 * b + 16])
            if live:
                al = (e * inv).astype(BF16)
                al_m[t - 1, b] = al
                new = new + dot(al, ml[96 * b : 96 * b + 96])
            mnew[t, b] = new
            old = mem[96 * b : 96 * b + 96, :]
            mem[96 * b : 96 * b + 96, :] = jnp.where(flag_of[b][t], new, old)

    for t in range(4):
        step_forward(t)

    vecs[...] = jnp.zeros(vecs.shape, F32)
    acc_r[...] = jnp.zeros(acc_r.shape, F32)
    acc_w[...] = jnp.zeros(acc_w.shape, F32)
    dmem[...] = jnp.zeros(dmem.shape, F32)

    def add_vec(k, x):
        vecs[k : k + 1, :] = vecs[k : k + 1, :] + x

    def step_backward(t):
        live = t > 0
        last = t == 3
        gates = [jnp.where(flag_of[b][t], 1.0, 0.0) for b in range(2)]
        d_out = []
        for b in range(2):
            base = 4 * (t // 2)
            given = cot[b, base + 3]
            for i in range(3):
                given = jnp.where(slot_of[b][t] == i, cot[b, base + i], given)
            d_out.append(given.astype(F32) * gates[b])
        d_ml = []
        dh_mem = []
        keeps = []
        if last:
            for b in range(2):
                keeps.append(jnp.zeros((96, D), F32))
                d_ml.append(keeps[b])
        else:
            dh_tok = []
            at_k = slice(base_k + 32 * t, base_k + 32 * t + 32)
            hk = h_w[at_k, :]
            tok = toks[t]
            for b in range(2):
                f = frame_index(b, t)
                down = dmem[96 * b : 96 * b + 96, :]
                ds = (down * gates[b]).astype(BF16)
                keeps.append(down * (1.0 - gates[b]))
                dsc[f, :MEM, :] = ds
                c = row_sum(ds.astype(F32) * mnew[t, b])
                stat[f, :MEM, 3:4] = c
                al = al_t[t, b]
                rows_b = slice(16 * b, 16 * b + 16)
                d_out[b] = d_out[b] + dot(al, ds, 0, 0)
                back = (al.astype(F32) * (dot(ds, tok[rows_b], 1, 1) - c)).astype(BF16)
                dh_tok.append(dot(back, wsw[...], 0, 0))
                acc = dot(back, hk[rows_b])
                if live:
                    rows_b = slice(96 * b, 96 * b + 96)
                    ml = mls[t - 1, rows_b, :]
                    al = al_m[t - 1, b]
                    d_ml.append(dot(al, ds, 0, 0))
                    back = (al.astype(F32) * (dot(ds, ml, 1, 1) - c)).astype(BF16)
                    dh_mem.append(dot(back, wsw[...], 0, 0))
                    at = slice(base_w + (t - 1) * 192 + 96 * b, base_w + (t - 1) * 192 + 96 * b + 96)
                    acc = acc + dot(back, h_w[at, :])
                acc_w[...] = acc_w[...] + acc
            dgk = (jnp.concatenate(dh_tok, 0) * d_w[at_k, :].astype(F32)).astype(BF16)
            d_w[at_k, :] = dgk
            da = dot(dgk, ww[...], 1, 1)
            xh = xhk[t]
            add_vec(4, col_sum(da * xh))
            dx = norm_back(da * g_write, xh, rk[t])
            for b in range(2):
                d_out[b] = d_out[b] + dx[16 * b : 16 * b + 16]
        at = slice(32 * t, 32 * t + 32)
        do = jnp.concatenate(d_out, 0)
        dob = do.astype(BF16)
        dos[at, :] = dob
        dn = jnp.zeros((32, D), F32)
        for j in range(4):
            sl = slice(D * j, D * j + D)
            dp = (dot(dob, wout[sl, :], 1, 1) * dg[t, :, sl].astype(F32)).astype(BF16)
            dpre[at, sl] = dp
            dn = dn + dot(dp, win[j][...], 1, 1)
        add_vec(3, col_sum(dn * xh2[t]))
        dy = do + norm_back(dn * g_ffn, xh2[t], r2[t])
        dyb = dy.astype(BF16)
        dys[at, :] = dyb
        dbig = by_head(dot(dyb, wo[...], 1, 1).astype(BF16))
        p = prob[t]
        q, k, v = qs[0, t], qs[1, t], qs[2, t]
        dp = dot(dbig, v, 1, 1)
        pf = p.astype(F32)
        ds = (pf * (dp - row_sum(dp * pf)) * (1.0 / math.sqrt(HEAD))).astype(BF16)
        dv = dot(p, dbig, 0, 0).astype(BF16)
        dq = from_heads(dot(ds, k)).astype(BF16)
        dk = dot(ds, by_head(q), 0, 0).astype(BF16)
        dqs[0, at, :] = dq
        dqs[1, at, :] = dk
        dqs[2, at, :] = dv
        du = dot(dq, wqkv[0][...], 1, 1) + dot(dk, wqkv[1][...], 1, 1) + dot(dv, wqkv[2][...], 1, 1)
        add_vec(2, col_sum(du * xh1[t]))
        dz = dy + norm_back(du * g_attn, xh1[t], r1[t])
        dzb = dz.astype(BF16)
        c_all = row_sum(dzb.astype(F32) * zs[t])
        dh_r = []
        for b in range(2):
            f = frame_index(b, t)
            ds = dzb[16 * b : 16 * b + 16]
            c = c_all[16 * b : 16 * b + 16]
            dsc[f, MEM:, :] = ds
            stat[f, MEM:, 3:4] = c
            if live:
                rows_b = slice(96 * b, 96 * b + 96)
                al = al_r[t - 1, b]
                d_ml[b] = d_ml[b] + dot(al, ds, 0, 0)
                back = (al.astype(F32) * (dot(ds, mls[t - 1, rows_b, :], 1, 1) - c)).astype(BF16)
                dh_r.append(dot(back, wsr[...], 0, 0))
                at_b = slice(base_r + (t - 1) * 192 + 96 * b, base_r + (t - 1) * 192 + 96 * b + 96)
                acc_r[...] = acc_r[...] + dot(back, h_r[at_b, :])
        if not live:
            return
        at_m = slice(base_r + (t - 1) * 192, base_r + t * 192)
        xh = mxh[t - 1]
        dgr = (jnp.concatenate(dh_r, 0) * d_r[at_m, :].astype(F32)).astype(BF16)
        d_r[at_m, :] = dgr
        da = dot(dgr, wr[...], 1, 1)
        add_vec(1, col_sum(da * xh))
        g = da * g_read
        if not last:
            at_m = slice(base_w + (t - 1) * 192, base_w + t * 192)
            dgw = (jnp.concatenate(dh_mem, 0) * d_w[at_m, :].astype(F32)).astype(BF16)
            d_w[at_m, :] = dgw
            da = dot(dgw, ww[...], 1, 1)
            add_vec(4, col_sum(da * xh))
            g = g + da * g_write
        dx = norm_back(g, xh, mr[t - 1])
        for b in range(2):
            rows_b = slice(96 * b, 96 * b + 96)
            dmem[rows_b, :] = keeps[b] + d_ml[b] + dx[rows_b]

    for t in range(3, -1, -1):
        step_backward(t)

    for other in [sibling] + [(core, me + step) for step in all_steps[0]]:
        pl.semaphore_signal(ready, inc=1, device_id=other, device_id_type=MESH)
    flat[ROW_AOUT : ROW_AOUT + D, :] = dot(att[...], dys[...], 0, 0).astype(BF16)
    for j in range(4):
        sl = slice(D * j, D * j + D)
        flat[ROW_FOUT + D * j : ROW_FOUT + D * j + D, :] = dot(gs[:, sl], dos[...], 0, 0).astype(BF16)
    for row, count, left, right in (
        (ROW_QKV, 3, us, lambda j: dqs[j]),
        (ROW_FIN, 4, u2, lambda j: dpre[:, D * j : D * j + D]),
    ):
        for q in range(4):
            for j in range(count):
                part = dot(left[:, 128 * q : 128 * q + 128], right(j), 0, 0)
                for c in range(4):
                    planes[c, pl.ds(j, 128, stride=count), :] = part[:, 128 * c : 128 * c + 128]
            base = row + count * 128 * q
            for c in range(4):
                at = slice(128 * c, 128 * c + 128)
                flat[base : base + count * 128, at] = planes[c, : count * 128, :].astype(BF16)
    flat[ROW_AGAIN : ROW_AGAIN + 1, :] = vecs[2:3, :].astype(BF16)
    flat[ROW_FGAIN : ROW_FGAIN + 1, :] = vecs[3:4, :].astype(BF16)

    def place_of(p, r):
        start, size = parts[p][:2]
        return chips * start + r * size

    def side(p, r):
        return wbig.at[pl.ds(place_of(p, r), parts[p][1])]

    def slot(p, k, r):
        start, size = parts[p][:2]
        return (chips - 1) * start + ((1 << k) - 1 + r) * size

    def turns(top, end):
        return [(p, r) for r in range(top - 1, end - 1, -1) for p in range(len(parts))]


    def swap(p, r):
        index = (1 - core) * chips + shifted(me, other_steps[p], r)
        start = pl.multiple_of(block_of(index) + parts[p][0], BLOCK)
        src = flat.at[pl.ds(start, parts[p][1])]
        return remote(src, side(p, r), sibsend.at[p, r], sibrecv.at[p, r], sibling), index

    def send_on(p, r):
        top = r.bit_length() - 1
        low = r - (1 << top)
        return remote(
            side(p, r),
            held.at[pl.ds(slot(p, top, low), parts[p][1])],
            send.at[p, r],
            recv.at[p, (1 << top) - 1 + low],
            (core, me + all_steps[p][top]),
        )

    def swap_all(late):
        for p, r in turns(chips, 0):
            copy, index = swap(p, r)

            @pl.when(is_outer(index) == late)
            def _(copy=copy):
                copy.start()

    def turn(p, r, late):
        index = core * chips + shifted(me, all_steps[p], r)
        start, size = parts[p][:2]

        @pl.when(is_outer(index) == late)
        def _():
            swap(p, r)[0].wait_recv()
            slots = []
            for k in range(bits - 1, r.bit_length() - 1, -1):
                at = held.at[pl.ds(slot(p, k, r), size)]
                remote(at, at, send.at[p, r], recv.at[p, (1 << k) - 1 + r], sibling).wait_recv()
                slots.append(slot(p, k, r))
            base = block_of(index) + start

            def add(i, carry):
                step = i * BLOCK
                at = pl.ds(pl.multiple_of(place_of(p, r) + step, BLOCK), BLOCK)
                mine = flat[pl.ds(pl.multiple_of(base + step, BLOCK), BLOCK), :]
                value = mine.astype(F32) + wbig[at, :].astype(F32)
                for one in slots:
                    value = value + held[pl.ds(pl.multiple_of(one + step, BLOCK), BLOCK), :].astype(F32)
                if r == 0:
                    for c in range(4):
                        spots = pl.ds(4 * (start + step) + c, BLOCK, stride=4)
                        total[spots, :] = value[:, 128 * c : 128 * c + 128]
                else:
                    wbig[at, :] = value.astype(BF16)
                return carry

            lax.fori_loop(0, size // BLOCK, add, 0)
            if r > 0:
                send_on(p, r).start()

    def frame_backward(f):
        at = slice(f * ROWS, f * ROWS + ROWS)
        x = xs[f]
        cols = slice(0 if f in WRITES else MEM, NCOL)
        ds = dsc[f, cols]
        al = ps[f, cols].astype(F32) * stat[f, cols, 2:3]
        alb = al.astype(BF16)
        back = (al * (dot(ds, x, 1, 1) - stat[f, cols, 3:4])).astype(BF16)
        back_r = back[-READ:]
        acc_r[...] = acc_r[...] + dot(back_r, h_r[at, :])
        xh, r = norm(x.astype(F32))
        dgr = (dot(back_r, wsr[...], 0, 0) * d_r[at, :].astype(F32)).astype(BF16)
        d_r[at, :] = dgr
        da = dot(dgr, wr[...], 1, 1)
        add_vec(1, col_sum(da * xh))
        g = da * g_read
        if f in WRITES:
            at = write_rows(f)
            acc_w[...] = acc_w[...] + dot(back[:MEM], h_w[at, :])
            dgw = (dot(back[:MEM], wsw[...], 0, 0) * d_w[at, :].astype(F32)).astype(BF16)
            d_w[at, :] = dgw
            da = dot(dgw, ww[...], 1, 1)
            add_vec(4, col_sum(da * xh))
            g = g + da * g_write
        dx = (dot(alb, ds, 0, 0) + norm_back(g, xh, r)).astype(BF16)
        xs[f] = dx
        add_vec(0, col_sum(dx.astype(F32)))
        to = jnp.where(core == f // 4, 0, 4) + f % 4
        pg[to] = dot(dx, wp[...], 1, 1).astype(BF16)

    pl.semaphore_wait(ready, bits + 1)
    swap_all(False)
    half = chips // 2
    todo = turns(chips, half)
    every = len(todo) // frames
    for i, (p, r) in enumerate(todo):
        if i % every == 0 and i // every < frames:
            frame_backward(i // every)
        turn(p, r, False)
    quarter = chips // 4
    for p, r in turns(half, quarter):
        turn(p, r, False)

    swap_pix = remote(pg.at[pl.ds(4, 4)], pgout, pixsem.at[0], pixsem.at[1], sibling)
    swap_pix.start()
    keep_pix = pltpu.make_async_copy(pg.at[pl.ds(0, 4)], near, pixsem.at[2])
    keep_pix.start()
    n = 4 * ROWS
    flat[ROW_PATCH : ROW_PATCH + PIN, :] = (
        dot(pix[...].reshape(n, PIN), xs[pl.ds(4 * core, 4)].reshape(n, D), 0, 0)
        + dot(far[...].reshape(n, PIN), xs[pl.ds(4 - 4 * core, 4)].reshape(n, D), 0, 0)
    ).astype(BF16)
    flat[ROW_RHID : ROW_RHID + D, :] = dot(a_r[...], d_r[...], 0, 0).astype(BF16)
    flat[ROW_WHID : ROW_WHID + D, :] = dot(a_w[...], d_w[...], 0, 0).astype(BF16)
    where, chosen, spread = score_masks(READ, 0)
    wide = dot(acc_r[...].astype(BF16), chosen, 0, 0).astype(BF16) * where
    flat[ROW_RSCORE : ROW_RSCORE + READ, :] = dot(spread, wide, 0, 0).astype(BF16)
    for part in range(3):
        where, chosen, spread = score_masks(MEM, part)
        wide = dot(acc_w[...].astype(BF16), chosen, 0, 0).astype(BF16) * where
        these = dot(spread, wide, 0, 0)
        for c in range(4):
            planes[c, pl.ds(part, 32, stride=3), :] = these[:, 128 * c : 128 * c + 128]
    for c in range(4):
        at = slice(128 * c, 128 * c + 128)
        flat[ROW_WSCORE : ROW_WSCORE + MEM, at] = planes[c, :MEM, :].astype(BF16)
    for k, row in ((0, ROW_BIAS), (1, ROW_RGAIN), (4, ROW_WGAIN)):
        flat[row : row + 1, :] = vecs[k : k + 1, :].astype(BF16)
    flat[ROW_END:, :] = jnp.zeros((flat.shape[0] - ROW_END, D), BF16)

    swap_all(True)
    for b in range(2):
        for s in range(STEPS):
            value = jnp.zeros((READ, D), BF16)
            for t in (s // 4 * 2, s // 4 * 2 + 1):
                hit = (slot_of[b][t] == s % 4) & flag_of[b][t]
                value = jnp.where(hit, toks[t, READ * b : READ * b + READ, :], value)
            done[b, s] = value
    for p, r in turns(chips, half):
        turn(p, r, True)
    for p, r in turns(half, quarter):
        turn(p, r, True)
    for p, r in turns(quarter, 0):
        turn(p, r, False)
        turn(p, r, True)
    for p, r in turns(chips, 0):
        swap(p, r)[0].wait_send()
        if r > 0:
            send_on(p, r).wait_send()
    swap_pix.wait()
    keep_pix.wait()


def main(own, pixels, cot, owner, counts, mask, chips, length):
    rows = own.shape[0]
    height = (2 * chips - 1) * length // (BLOCK * D) * BLOCK + rows
    n = 8 * ROWS
    vmem = pl.BlockSpec(memory_space=pltpu.VMEM)
    smem = pl.BlockSpec(memory_space=pltpu.SMEM)
    hbm = pl.BlockSpec(memory_space=pl.ANY)
    v = pltpu.VMEM
    dma = pltpu.SemaphoreType.DMA
    return pl.pallas_call(
        functools.partial(main_kernel, chips, length),
        out_shape=(
            jax.ShapeDtypeStruct((2, STEPS, READ, D), BF16),
            jax.ShapeDtypeStruct((4, ROWS, PIN), BF16),
            jax.ShapeDtypeStruct((4 * rows, 128), F32),
            jax.ShapeDtypeStruct((4, ROWS, PIN), BF16),
        ),
        in_specs=[smem, smem, smem, vmem, hbm, vmem],
        out_specs=[vmem, hbm, vmem, hbm],
        scratch_shapes=[
            v((height, D), BF16),
            v((4, D, 128), F32),
            v((PIN, D), BF16),
            v((D, D), BF16),
            v((D, D), BF16),
            v((max(12 * D, chips * rows), D), BF16),
            v((READ, D), BF16),
            v((MEM, D), BF16),
            v((8, D), F32),
            v((8, ROWS, D), BF16),
            v((n + 576, D), BF16),
            v((n - 2 * ROWS + 480, D), BF16),
            v((n + 576, D), BF16),
            v((n - 2 * ROWS + 480, D), BF16),
            v((n + 576, D), BF16),
            v((n - 2 * ROWS + 480, D), BF16),
            v((8, NCOL, ROWS), BF16),
            v((8, NCOL, D), F32),
            v((8, NCOL, 8), F32),
            v((8, NCOL, D), BF16),
            v((192, D), F32),
            v((192, D), F32),
            v((3, 192, D), BF16),
            v((3, 192, D), F32),
            v((3, 192, 1), F32),
            v((3, 2, MEM, D), F32),
            v((3, 2, READ, MEM), BF16),
            v((2, 2, MEM, MEM), BF16),
            v((3, 2, MEM, READ), BF16),
            v((4, 32, D), F32),
            v((4, 32, D), F32),
            v((4, 32, 1), F32),
            v((128, D), BF16),
            v((3, 4, 32, D), BF16),
            v((4, HEADS * 32, 32), BF16),
            v((128, D), BF16),
            v((4, 32, D), F32),
            v((4, 32, 1), F32),
            v((128, D), BF16),
            v((128, FFN), BF16),
            v((4, 32, FFN), BF16),
            v((4, 32, D), BF16),
            v((3, 32, D), F32),
            v((3, 32, 1), F32),
            v((3, 128, D), BF16),
            v((128, D), BF16),
            v((128, FFN), BF16),
            v((128, D), BF16),
            v((READ, D), F32),
            v((MEM, D), F32),
            v((8, D), F32),
            v((4, ROWS, PIN), BF16),
            v((4, ROWS, PIN), BF16),
            v((2, P_SIZE, 4, PIN), BF16),
            v((8, ROWS, PIN), BF16),
            v((max((chips - 1) * rows, 4 * chips * BLOCK), D), BF16),
            dma((2, 2)),
            dma((PARTS, chips)),
            dma((PARTS, chips)),
            dma((PARTS, chips)),
            dma((PARTS, chips)),
            dma((PARTS, chips)),
            dma((PARTS, chips)),
            dma((4,)),
            pltpu.SemaphoreType.REGULAR,
        ],
        compiler_params=pltpu.CompilerParams(
            collective_id=0, has_side_effects=True, vmem_limit_bytes=VMEM_LIMIT
        ),
        name="model",
    )(owner, counts, mask, own, pixels, cot)


def body(pixels, counts, step_mask, owner, params, cotangent):
    chips = lax.axis_size("dp")
    length = params.shape[0]
    core = lax.axis_index("grp").astype(jnp.int32)
    dp = lax.axis_index("dp").astype(jnp.int32)
    counts = counts[:, :, 0]
    mask = step_mask[:, :, 0]
    owner = owner[:, 0]

    rows = window_rows(length)
    offset = ((core * chips + dp) * length) % (BLOCK * D)
    wide = jnp.pad(params, (BLOCK * D, rows * D - length))
    win = lax.dynamic_slice(wide, (BLOCK * D - offset,), (rows * D,)).reshape(rows, D)

    cot = cotangent[:, 0, 0]
    done, near_grad, total, far_grad = main(
        win, jnp.swapaxes(pixels, 3, 4), cot, owner, counts, mask, chips, length
    )
    shard_grad = lax.dynamic_slice(total.reshape(rows * D), (offset,), (length,))
    pixel_grad = place(near_grad, far_grad, owner, counts, mask, pixels.shape)
    return (done[:, None, None], pixel_grad, shard_grad)


def solution(mesh):
    return jax.shard_map(
        body,
        mesh=mesh,
        in_specs=(
            P(None, None, "dp", "grp", None, None),
            P(None, None, "dp"),
            P(None, None, "dp", None),
            P(None, "dp"),
            P(("grp", "dp")),
            P(None, "grp", "dp", None, None, None),
        ),
        out_specs=(
            P(None, "grp", "dp", None, None, None),
            P(None, None, "dp", "grp", None, None),
            P(("grp", "dp")),
        ),
        check_vma=False,
    )
```
